128 devices in a mesh: vol: 16 (over z, x), col: 8 (over y, core).
Axes of the slice: x: 4, y: 4, z: 4, core: 2. Of those that a mesh axis runs over, the one named last changes fastest.
Arguments:
- face_area: float32 [16, 131072], P('vol', 'col'), may hold values from 0.25 to 2.5
- face_speed: float32 [16, 131072], P('vol', 'col'), may hold values from -6 to 6
- face_node: int32 [16, 131072], P('vol', 'col'), may hold values from 0 to 65535
- face_count: int32 [16, 8], P('vol', 'col'), may hold values from 4096 to 16384, as said below
- surface_metric: float32 [1024, 1024], P('vol'), may hold values from 1 to 10
- displacement: float32 [64, 1024, 1024], P('col', 'vol'), may hold values from -6 to 6
Outputs:
- surface_velocity: float32 [1024, 1024], P('vol')
- displaced: float32 [64, 1024, 1024], P('col', 'vol')
The draws below stay inside these ranges and needn't reach their ends.
Inputs may be any that keep to these rules, and one draw needn't show every extreme that they name: `face_count`: the live slots of a device are its first slots; some device has all 16384 slots live in every draw.
All inputs are finite; a program needn't handle non-finite values.
Results may differ from the reference program's by a relative error of at most 0.0003.
Values sent between devices are 32-bit elements; how exact they have to be, the bound alone decides.
No kernel may reach another device: no remote copies, remote signals or barrier semaphores. Data moves between devices by JAX's collectives and lax.ppermute only.
A program may use at most 64 MiB of HBM per device.

```python
import math
import jax
import jax.numpy as jnp
from jax import lax

CY = 64
NX = 1024
FACE_DEV = 16384
ITERS = 10
SWEEPS = 4
TOP_DEVICES = 16
COL_DEVICES = 8
NZ = 64
NY = 1024


def draw_face_count(key, part):
    key = jax.random.fold_in(key, 7)
    level_key, pick_key = jax.random.split(key)
    counts = jax.random.randint(level_key, (TOP_DEVICES, COL_DEVICES), FACE_DEV // 4, FACE_DEV + 1)
    pick = jax.random.randint(pick_key, (), 0, TOP_DEVICES * COL_DEVICES)
    flat_index = jnp.arange(TOP_DEVICES * COL_DEVICES, dtype=jnp.int32).reshape(TOP_DEVICES, COL_DEVICES)
    return jnp.where(flat_index == pick, FACE_DEV, counts).astype(jnp.int32)


def plant(entries, stream_key, low, top_value):
    extent = entries.shape
    index_at = [jax.random.randint(jax.random.fold_in(stream_key, axis), (), 0, extent[axis]) for axis in range(len(extent))]
    entries = entries.at[tuple(index_at)].set(low)
    longest = extent.index(max(extent))
    index_at[longest] = (index_at[longest] + 1) % extent[longest]
    return entries.at[tuple(index_at)].set(top_value)


def block_scale(rng, dims, cuts, least, top_value):
    def one(position, parts):
        steps = jax.random.uniform(jax.random.fold_in(jax.random.fold_in(rng, 6), position), (parts,), jnp.float32, least / len(cuts), top_value / len(cuts))
        return jnp.repeat(jnp.exp(steps), dims[position] // parts).reshape((-1,) + (1,) * (len(dims) - position - 1))

    loudness = one(*cuts[0])
    for cut in cuts[1:]:
        loudness = loudness * one(*cut)
    return loudness


def bell_draw(key, shape, width, reach, cuts=(), held_as=jnp.bfloat16):
    array = width * jax.random.normal(key, shape, jnp.float32)
    if cuts:
        array = array * block_scale(key, shape, cuts, -0.22, 0.18)
    return jnp.clip(array, -reach, reach).astype(held_as)


def setup_inputs(seed: int = 0) -> dict:
    streams_of = jax.random.split(jax.random.key(seed), 7)
    return {
        "face_area": jnp.clip(jnp.exp(math.log(2.5) - 2.3025851 * jax.random.uniform(streams_of[0], (TOP_DEVICES, FACE_DEV * COL_DEVICES), jnp.float32) ** block_scale(streams_of[0], (TOP_DEVICES, FACE_DEV * COL_DEVICES), ((0, 16), (1, 8)), -0.2, 0.2)), 0.25, 2.5),
        "face_speed": bell_draw(streams_of[1], (TOP_DEVICES, FACE_DEV * COL_DEVICES), 1.0, 6.0, ((0, 16), (1, 8)), jnp.float32),
        "face_node": plant(jax.random.randint(streams_of[2], (TOP_DEVICES, FACE_DEV * COL_DEVICES), 0, CY * NX), jax.random.fold_in(streams_of[2], 1), 0, (CY * NX) - 1).astype(jnp.int32),
        "face_count": draw_face_count(jax.random.fold_in(streams_of[6], 71), 0),
        "surface_metric": jnp.clip(jnp.exp(math.log(10.0) - 2.3025851 * jax.random.uniform(streams_of[4], (NY, NX), jnp.float32) ** block_scale(streams_of[4], (NY, NX), ((0, 16),), -0.2, 0.2)), 1.0, 10.0),
        "displacement": bell_draw(streams_of[5], (NZ, NY, NX), 1.0, 6.0, ((0, 8), (1, 16)), jnp.float32),
    }


mass_even = (-1.0 / 15.0, 2.0 / 15.0, 8.0 / 15.0, 2.0 / 15.0, -1.0 / 15.0)
mass_odd = (0.0, 2.0 / 15.0, 16.0 / 15.0, 2.0 / 15.0, 0.0)
stiff_even = (1.0 / 6.0, -8.0 / 6.0, 14.0 / 6.0, -8.0 / 6.0, 1.0 / 6.0)
stiff_odd = (0.0, -8.0 / 6.0, 16.0 / 6.0, -8.0 / 6.0, 0.0)
relaxation = 0.5
step_length = 0.5

def padded_line(padded, along_axis, even_taps, odd_taps, first_index):
    line_count = padded.shape[along_axis] - 4
    total_even = None
    total_odd = None
    for tap_index in range(5):
        slab_piece = lax.slice_in_dim(padded, tap_index, tap_index + line_count, axis=along_axis)
        if even_taps[tap_index] != 0.0:
            term = even_taps[tap_index] * slab_piece
            total_even = term if total_even is None else total_even + term
        if odd_taps[tap_index] != 0.0:
            term = odd_taps[tap_index] * slab_piece
            total_odd = term if total_odd is None else total_odd + term
    even_mask = (lax.broadcasted_iota(jnp.int32, total_even.shape, along_axis) + first_index) % 2 == 0
    return jnp.where(even_mask, total_even, total_odd)

def surface_lines(padded_rows):
    padded = jnp.pad(padded_rows, ((0, 0), (2, 2)))
    across = padded_line(padded, 1, mass_even, mass_odd, 0)
    return padded_line(across, 0, mass_even, mass_odd, 0)

def diagonal(shape, first_index):
    depth_even = (lax.broadcasted_iota(jnp.int32, shape, 0) + first_index) % 2 == 0
    rows_even = lax.broadcasted_iota(jnp.int32, shape, 1) % 2 == 0
    cols_even = lax.broadcasted_iota(jnp.int32, shape, 2) % 2 == 0
    stiff_depth = jnp.where(depth_even, stiff_even[2], stiff_odd[2])
    mass_depth = jnp.where(depth_even, mass_even[2], mass_odd[2])
    stiff_rows = jnp.where(rows_even, stiff_even[2], stiff_odd[2])
    mass_rows = jnp.where(rows_even, mass_even[2], mass_odd[2])
    stiff_cols = jnp.where(cols_even, stiff_even[2], stiff_odd[2])
    mass_cols = jnp.where(cols_even, mass_even[2], mass_odd[2])
    lateral_mass = mass_rows * mass_cols
    lateral_stiff = stiff_rows * mass_cols + mass_rows * stiff_cols
    return stiff_depth * lateral_mass + mass_depth * lateral_stiff

def lateral_plane(plane):
    padded = jnp.pad(plane, 2)
    mass_x = padded_line(padded, 1, mass_even, mass_odd, 0)
    stiff_x = padded_line(padded, 1, stiff_even, stiff_odd, 0)
    along = padded_line(mass_x, 0, mass_even, mass_odd, 0)
    cross = padded_line(mass_x, 0, stiff_even, stiff_odd, 0) + padded_line(stiff_x, 0, mass_even, mass_odd, 0)
    return (along, cross)

def sweep(field):
    along, cross = lax.map(lateral_plane, field)
    padded_along = jnp.pad(along, ((2, 2), (0, 0), (0, 0)))
    padded_cross = jnp.pad(cross, ((2, 2), (0, 0), (0, 0)))

    def one_plane(plane_index):
        slab_along = lax.dynamic_slice_in_dim(padded_along, plane_index, 5, 0)
        slab_cross = lax.dynamic_slice_in_dim(padded_cross, plane_index, 5, 0)
        operator_image = padded_line(slab_along, 0, stiff_even, stiff_odd, plane_index) + padded_line(slab_cross, 0, mass_even, mass_odd, plane_index)
        current = lax.dynamic_slice_in_dim(field, plane_index, 1, 0)
        scale = diagonal((1, NY, NX), plane_index)
        return (current - relaxation * operator_image / scale)[0]
    return lax.map(one_plane, jnp.arange(NZ, dtype=jnp.int32))

def conjugate(flux, apply_mass):
    solution = jnp.zeros_like(flux)
    residual = flux
    direction = flux
    norm_now = jnp.sum(residual * residual)
    for iteration in range(ITERS):
        mass_image = apply_mass(direction)
        step_alpha = norm_now / jnp.sum(direction * mass_image)
        solution = solution + step_alpha * direction
        residual = residual - step_alpha * mass_image
        norm_next = jnp.sum(residual * residual)
        direction = residual + norm_next / norm_now * direction
        norm_now = norm_next
    return solution

def reference(face_area, face_speed, face_node, face_count, surface_metric, displacement):
    slot_index = jnp.arange(FACE_DEV * COL_DEVICES, dtype=jnp.int32)
    block_counts = face_count[:, slot_index // FACE_DEV]
    live_slots = (slot_index % FACE_DEV)[None, :] < block_counts
    band_start = jnp.arange(TOP_DEVICES, dtype=jnp.int32) * (CY * NX)
    global_nodes = face_node + band_start[:, None]
    contributions = jnp.where(live_slots, face_area * face_speed, 0.0)
    flux = jax.ops.segment_sum(contributions.reshape(-1), global_nodes.reshape(-1), num_segments=NY * NX).reshape(NY, NX)
    metric_root = jnp.sqrt(surface_metric)

    def apply_mass(values_in):
        weighted = metric_root * values_in
        return metric_root * surface_lines(jnp.pad(weighted, ((2, 2), (0, 0))))
    surface_velocity = conjugate(flux, apply_mass)
    top_plane = displacement[0] + step_length * surface_velocity
    field = displacement.at[0].set(top_plane)
    for sweep_index in range(SWEEPS):
        field = sweep(field)
        field = field.at[0].set(top_plane)
    return (surface_velocity, field)
```

```python
import jax
import jax.numpy as jnp
import numpy as np
from jax import lax
from jax.experimental import pallas as pl
from jax.experimental.pallas import tpu as pltpu
from jax.sharding import PartitionSpec as P

ITERS = 10
SWEEPS = 4
LANES = 128
SUB = 8
MIB = 1024 * 1024

BASIS_LOW = 0.1
BASIS_HIGH = 12.0
CONDITION_MAX = 2000.0


def wrapped_roll(x, shift, axis):
    return pltpu.roll(x, shift % x.shape[axis], axis)


def lane_shift(tiles, offset):
    lane = lax.broadcasted_iota(jnp.int32, tiles[0].shape, 1)
    rolled = [wrapped_roll(tile, -offset, 1) for tile in tiles]
    zero = jnp.zeros_like(tiles[0])
    if offset < 0:
        edge = lane < -offset
        return [
            jnp.where(edge, rolled[t - 1] if t > 0 else zero, rolled[t])
            for t in range(len(tiles))
        ]
    edge = lane >= LANES - offset
    return [
        jnp.where(edge, rolled[t + 1] if t + 1 < len(tiles) else zero, rolled[t])
        for t in range(len(tiles))
    ]


def lane_sums(tiles):
    left, right = lane_shift(tiles, -1), lane_shift(tiles, 1)
    far_left, far_right = lane_shift(tiles, -2), lane_shift(tiles, 2)
    near = [a + b for a, b in zip(left, right)]
    far = [a + b for a, b in zip(far_left, far_right)]
    return near, far


def lane_choice(even, odd):
    lane = lax.broadcasted_iota(jnp.int32, (SUB, LANES), 1)
    return jnp.where(lane % 2 == 0, jnp.float32(even), jnp.float32(odd))


def ring(rows):
    n = len(rows)
    return (
        [wrapped_roll(rows[n - 2], 1, 0), wrapped_roll(rows[n - 1], 1, 0)]
        + list(rows)
        + [wrapped_roll(rows[0], -1, 0), wrapped_roll(rows[1], -1, 0)]
    )


def mass_line(padded, index):
    i = index + 2
    near = padded[i - 1] + padded[i + 1]
    if index % 2:
        return near + 8.0 * padded[i]
    return (near + 4.0 * padded[i]) - 0.5 * (padded[i - 2] + padded[i + 2])


def both_line(padded, index):
    i = index + 2
    near = padded[i - 1] + padded[i + 1]
    return (16.0 / 3.0 if index % 2 else 11.0 / 3.0) * padded[i] - near


def face_kernel(where_ref, count_ref, area_ref, speed_ref, node_ref, keep_ref, send_ref, acc_ref):
    slots = area_ref.shape[1]
    chunk = min(2048, slots)
    core = where_ref[0, 0]
    ids = lax.broadcasted_iota(jnp.int32, (256, chunk), 0)
    ids = ids.astype(jnp.float32).astype(jnp.bfloat16)
    zero = jnp.zeros((), jnp.bfloat16)
    one = jnp.ones((), jnp.bfloat16)
    contract = (((1,), (1,)), ((), ()))
    acc_ref[...] = jnp.zeros_like(acc_ref)

    def wide(x):
        return jnp.broadcast_to(x.astype(jnp.bfloat16), (256, chunk))

    def body(step, carry):
        at = pl.ds(pl.multiple_of(step * chunk, chunk), chunk)
        slot = lax.broadcasted_iota(jnp.int32, (1, chunk), 1) + step * chunk
        value = jnp.where(slot < count_ref[0, 0], area_ref[:, at] * speed_ref[:, at], 0.0)
        node = node_ref[:, at]
        low = (node & 255).astype(jnp.float32)
        high = (((node >> 8) & 3) * 64 + (node >> 10)).astype(jnp.float32)
        first = value.astype(jnp.bfloat16)
        second = value - first.astype(jnp.float32)
        here = wide(high) == ids
        upper = jnp.where(here, wide(first), zero)
        lower = jnp.where(here, wide(second), zero)
        columns = jnp.where(wide(low) == ids, one, zero)
        acc_ref[...] += lax.dot_general(
            upper, columns, contract, preferred_element_type=jnp.float32
        ) + lax.dot_general(lower, columns, contract, preferred_element_type=jnp.float32)
        return carry

    lax.fori_loop(0, slots // chunk, body, 0)
    for j in range(4):
        keep_ref[:, 256 * j : 256 * (j + 1)] = acc_ref[pl.ds(64 * j + 32 * core, 32), :]
        send_ref[:, 256 * j : 256 * (j + 1)] = acc_ref[pl.ds(64 * j + 32 - 32 * core, 32), :]


def face_sums(where, count, area, speed, node):
    half = jax.ShapeDtypeStruct((32, 1024), jnp.float32)
    smem = pl.BlockSpec(memory_space=pltpu.SMEM)
    vmem = pl.BlockSpec(memory_space=pltpu.VMEM)
    return pl.pallas_call(
        face_kernel,
        out_shape=(half, half),
        in_specs=[smem, smem, vmem, vmem, vmem],
        out_specs=(vmem, vmem),
        scratch_shapes=[pltpu.VMEM((256, 256), jnp.float32)],
        compiler_params=pltpu.CompilerParams(vmem_limit_bytes=32 * MIB),
        cost_estimate=pl.CostEstimate(flops=4_000_000_000, bytes_accessed=500_000, transcendentals=0),
        name="face_sums",
    )(where, count, area, speed, node)


HALO = 32
ROWS = 128
GROUPS = 16


def basis_kernel(
    where_ref, own_ref, other_ref, same_ref, cross_ref,
    metric_ref, before_ref, after_ref, basis_ref, sums_ref, root_ref, line_ref,
):
    core = where_ref[0, 0]
    tiles = own_ref.shape[1] // LANES
    for t in range(tiles):
        cols = slice(LANES * t, LANES * (t + 1))
        basis_ref[0, t, pl.ds(32 + 32 * core, 32), :] = own_ref[:, cols]
        basis_ref[0, t, pl.ds(64 - 32 * core, 32), :] = other_ref[:, cols]
        basis_ref[0, t, pl.ds(96 * core, 32), :] = cross_ref[:, cols]
        basis_ref[0, t, pl.ds(96 - 96 * core, 32), :] = same_ref[:, cols]
        root_ref[t, 0:32, :] = jnp.sqrt(before_ref[:, cols])
        root_ref[t, 32:96, :] = jnp.sqrt(metric_ref[:, cols])
        root_ref[t, 96:128, :] = jnp.sqrt(after_ref[:, cols])

    centre = (BASIS_LOW + BASIS_HIGH) / 2
    scale = 2 / (BASIS_HIGH - BASIS_LOW)
    at_centre = lane_choice(4.0, 8.0)
    at_far = lane_choice(-0.5, 0.0)
    group = lax.broadcasted_iota(jnp.int32, (SUB, LANES), 0)
    own_rows = jnp.where((group >= 2) & (group < 6), 1.0, 0.0).astype(jnp.float32)

    def rows_of(ys):
        return pl.ds(ys, SUB, stride=GROUPS)

    def step(k, carry):
        before = jnp.maximum(k - 1, 0)
        first = jnp.where(k == 0, 1.0, 2.0).astype(jnp.float32)
        second = jnp.where(k == 0, 0.0, 1.0).astype(jnp.float32)

        def along_x(ys, carry):
            weighted = []
            for t in range(tiles):
                weighted.append(basis_ref[k, t, rows_of(ys), :] * root_ref[t, rows_of(ys), :])
            near, far = lane_sums(weighted)
            for t in range(tiles):
                line_ref[ys, t] = near[t] + at_centre * weighted[t] + at_far * far[t]
            return carry

        lax.fori_loop(0, GROUPS, along_x, 0)

        square = jnp.zeros((SUB, LANES), jnp.float32)
        shifted = jnp.zeros((SUB, LANES), jnp.float32)
        for t in range(tiles):
            padded = ring([line_ref[ys, t] for ys in range(GROUPS)])
            for ys in range(GROUPS):
                image = (root_ref[t, rows_of(ys), :] * (4.0 / 225.0 * scale)) * mass_line(padded, ys)
                now = basis_ref[k, t, rows_of(ys), :]
                last = basis_ref[before, t, rows_of(ys), :]
                later = first * (image - (centre * scale) * now) - second * last
                basis_ref[k + 1, t, rows_of(ys), :] = later
                square = square + now * now
                shifted = shifted + later * now
        sums_ref[pl.ds(2 * k, 1), :] = jnp.sum(square * own_rows, axis=0, keepdims=True)
        sums_ref[pl.ds(2 * k + 1, 1), :] = jnp.sum(shifted * own_rows, axis=0, keepdims=True)
        return carry

    sums_ref[...] = jnp.zeros_like(sums_ref)
    lax.fori_loop(0, ITERS, step, 0)


def surface_basis(where, own, other, same, cross, metric, before, after):
    cols = own.shape[1]
    smem = pl.BlockSpec(memory_space=pltpu.SMEM)
    vmem = pl.BlockSpec(memory_space=pltpu.VMEM)
    return pl.pallas_call(
        basis_kernel,
        out_shape=(
            jax.ShapeDtypeStruct((ITERS + 1, cols // LANES, ROWS, LANES), jnp.float32),
            jax.ShapeDtypeStruct((24, LANES), jnp.float32),
        ),
        in_specs=[smem] + [vmem] * 7,
        out_specs=(vmem, vmem),
        scratch_shapes=[
            pltpu.VMEM((cols // LANES, ROWS, LANES), jnp.float32),
            pltpu.VMEM((GROUPS, cols // LANES, SUB, LANES), jnp.float32),
        ],
        compiler_params=pltpu.CompilerParams(vmem_limit_bytes=40 * MIB),
        cost_estimate=pl.CostEstimate(flops=40_000_000, bytes_accessed=8_000_000, transcendentals=0),
        name="surface_basis",
    )(where, own, other, same, cross, metric, before, after)


def solve_weights():
    n = ITERS
    moment = np.zeros((2 * n, 2 * n))
    for m in range(2 * n):
        if m < 2:
            moment[m, m] = 1.0
        else:
            moment[m, m] = 2.0
            moment[m, m % 2] = -1.0
    centre, half = (BASIS_LOW + BASIS_HIGH) / 2, (BASIS_HIGH - BASIS_LOW) / 2
    weights = np.zeros((2 * n, 16, LANES))
    for i in range(n):
        for j in range(n):
            lower = abs(j - 1)
            for factor, index in (
                (centre / 2, i + j),
                (centre / 2, abs(i - j)),
                (half / 4, i + j + 1),
                (half / 4, abs(i - j - 1)),
                (half / 4, i + lower),
                (half / 4, abs(i - lower)),
            ):
                weights[:, i, j] += factor * moment[index]
        weights[:, i, n] += moment[i]
    return weights.astype(np.float32)


def solve_kernel(basis_ref, sums_ref, weights_ref, out_ref, flag_ref, part_ref, sem):
    n = ITERS
    first = HALO - 8
    count = out_ref.shape[0]
    copy = pltpu.make_async_copy(basis_ref.at[pl.ds(0, n), :, pl.ds(first, count), :], part_ref, sem)
    copy.start()
    total = sums_ref[0]
    for i in range(1, sums_ref.shape[0]):
        total = total + sums_ref[i]
    total = jnp.broadcast_to(jnp.sum(total, axis=1, keepdims=True), total.shape)
    row = lax.broadcasted_iota(jnp.int32, (16, LANES), 0)
    lane = lax.broadcasted_iota(jnp.int32, (16, LANES), 1)
    system = jnp.where((lane == row + 16) & (row < n), 1.0, 0.0).astype(jnp.float32)
    for m in range(2 * n):
        system = system + weights_ref[m] * total[m : m + 1, :]
    centre = jnp.sum(jnp.where(lane == row, system, 0.0), axis=1, keepdims=True)
    for k in range(n):
        pivot_row = system[k : k + 1, :] / system[k : k + 1, k : k + 1]
        column = system[:, k : k + 1]
        system = jnp.where(row == k, pivot_row, system - column * pivot_row)
    inverse = jnp.sum(jnp.where(lane == row + 16, system, 0.0), axis=1, keepdims=True)
    figure = jnp.broadcast_to(centre * inverse, (16, LANES))
    inside = (row < n) & (lane == 0)
    least = jnp.min(jnp.where(inside, figure, 1.0))
    whole = jnp.sum(jnp.where(inside, figure, 0.0))
    flag_ref[0, 0] = jnp.where((least > 0.5) & (whole < CONDITION_MAX), 1, 0).astype(jnp.int32)
    copy.wait()
    for t in range(out_ref.shape[1] // LANES):
        cols = slice(LANES * t, LANES * (t + 1))
        value = None
        for k in range(n):
            term = system[k : k + 1, n : n + 1] * part_ref[k, t]
            value = term if value is None else value + term
        out_ref[:, cols] = value


def surface_solve(basis, sums):
    tiles = basis.shape[1]
    cols = tiles * LANES
    smem = pl.BlockSpec(memory_space=pltpu.SMEM)
    vmem = pl.BlockSpec(memory_space=pltpu.VMEM)
    return pl.pallas_call(
        solve_kernel,
        out_shape=(
            jax.ShapeDtypeStruct((80, cols), jnp.float32),
            jax.ShapeDtypeStruct((1, 1), jnp.int32),
        ),
        in_specs=[pl.BlockSpec(memory_space=pl.ANY), vmem, vmem],
        out_specs=(vmem, smem),
        scratch_shapes=[pltpu.VMEM((ITERS, tiles, 80, LANES), jnp.float32), pltpu.SemaphoreType.DMA],
        compiler_params=pltpu.CompilerParams(vmem_limit_bytes=32 * MIB),
        cost_estimate=pl.CostEstimate(flops=2_000_000, bytes_accessed=4_000_000, transcendentals=0),
        name="surface_solve",
    )(basis, sums, jnp.asarray(solve_weights()))


DEEP = 2 * SWEEPS
Y_GROUPS = 10
Y_ROWS = 80


def sweep_kernel(
    where_ref, block_ref, ylow_ref, yhigh_ref, zlow_ref, zhigh_ref, speed_ref, out_ref,
    field, along, cross, line_a, line_b, factor, top, sems,
):
    col, cols = where_ref[0, 1], where_ref[0, 2]
    vol, vols = where_ref[0, 3], where_ref[0, 4]
    layers, rows = block_ref.shape[0], block_ref.shape[1]
    tiles = block_ref.shape[2] // LANES
    total = layers + 2 * DEEP
    copies = []
    for t in range(tiles):
        lanes = pl.ds(LANES * t, LANES)
        for source, at_z, nz, at_y, ny in (
            (block_ref, DEEP, layers, DEEP, rows),
            (ylow_ref, DEEP, layers, 0, DEEP),
            (yhigh_ref, DEEP, layers, DEEP + rows, DEEP),
            (zlow_ref, 0, DEEP, 0, Y_ROWS),
            (zhigh_ref, DEEP + layers, DEEP, 0, Y_ROWS),
        ):
            copies.append(
                pltpu.make_async_copy(
                    source.at[:, :, lanes],
                    field.at[pl.ds(at_z, nz), t, pl.ds(at_y, ny), :],
                    sems.at[len(copies)],
                )
            )
    for copy in copies:
        copy.start()

    group = lax.broadcasted_iota(jnp.int32, (SUB, LANES), 0)
    lane = lax.broadcasted_iota(jnp.int32, (SUB, LANES), 1)
    mass, stiff = (8.0, 16.0), (14.0, 16.0)
    for pz in range(2):
        for ys in range(Y_GROUPS):
            py = ys % 2
            values = [
                -12.0
                / (stiff[pz] * mass[py] * mass[px] + mass[pz] * (stiff[py] * mass[px] + mass[py] * stiff[px]))
                for px in range(2)
            ]
            row = group * Y_GROUPS + ys
            outside = ((vol == 0) & (row < DEEP)) | ((vol == vols - 1) & (row >= DEEP + rows))
            factor[pz, ys] = jnp.where(
                outside, 0.0, jnp.where(lane % 2 == 0, jnp.float32(values[0]), jnp.float32(values[1]))
            )
    at_centre = lane_choice(4.0, 8.0)
    at_far = lane_choice(-0.5, 0.0)
    at_both = lane_choice(11.0 / 3.0, 16.0 / 3.0)

    for copy in copies:
        copy.wait()

    @pl.when(col <= 1)
    def _():
        at = DEEP - DEEP * col
        for t in range(tiles):
            lanes = slice(LANES * t, LANES * (t + 1))
            plane = field[at, t] + 0.5 * speed_ref[:, lanes]
            field[at, t] = plane
            top[t] = plane

    def lateral(z, carry):
        def across(ys, carry):
            rows_at = pl.ds(ys, SUB, stride=Y_GROUPS)
            u = [field[z, t, rows_at, :] for t in range(tiles)]
            near, far = lane_sums(u)
            for t in range(tiles):
                m = near[t] + at_centre * u[t] + at_far * far[t]
                line_a[t, ys] = m
                line_b[t, ys] = at_both * u[t] - near[t] - m
            return carry

        lax.fori_loop(0, Y_GROUPS, across, 0)

        def down(t, carry):
            a = ring([line_a[t, ys] for ys in range(Y_GROUPS)])
            b = ring([line_b[t, ys] for ys in range(Y_GROUPS)])
            for ys in range(Y_GROUPS):
                along[z, t, ys] = mass_line(a, ys)
                cross[z, t, ys] = both_line(a, ys) + mass_line(b, ys)
            return carry

        lax.fori_loop(0, tiles, down, 0)
        return carry

    def update(pair, carry):
        for pz in range(2):
            z = 2 * pair + pz

            def one(t, carry):
                for ys in range(Y_GROUPS):
                    w = along[z, t, ys]
                    c = cross[z, t, ys]
                    step = (16.0 / 3.0 if pz else 11.0 / 3.0) * w - (along[z - 1, t, ys] + along[z + 1, t, ys])
                    near = cross[z - 1, t, ys] + cross[z + 1, t, ys]
                    if pz:
                        step = step + (near + 8.0 * c)
                    else:
                        far = cross[z - 2, t, ys] + cross[z + 2, t, ys]
                        step = step + (near + 4.0 * c) - 0.5 * far
                    rows_at = pl.ds(ys, SUB, stride=Y_GROUPS)
                    field[z, t, rows_at, :] += factor[pz, ys] * step
                return carry

            lax.fori_loop(0, tiles, one, 0)
        return carry

    for sweep in range(SWEEPS):
        edge = 2 * sweep
        lax.fori_loop(edge, total - edge, lateral, 0)
        low = jnp.where(col == 0, DEEP // 2, sweep + 1)
        high = jnp.where(col == cols - 1, (DEEP + layers) // 2, total // 2 - sweep - 1)
        lax.fori_loop(low, high, update, 0)

        @pl.when(col == 0)
        def _():
            for t in range(tiles):
                field[DEEP, t] = top[t]

    results = []
    for t in range(tiles):
        results.append(
            pltpu.make_async_copy(
                field.at[pl.ds(DEEP, layers), t, pl.ds(DEEP, rows), :],
                out_ref.at[:, :, pl.ds(LANES * t, LANES)],
                sems.at[t],
            )
        )
    for copy in results:
        copy.start()
    for copy in results:
        copy.wait()


def extend_mesh(where, block, ylow, yhigh, zlow, zhigh, speed):
    layers, rows, cols = block.shape
    tiles = cols // LANES
    total = layers + 2 * DEEP
    smem = pl.BlockSpec(memory_space=pltpu.SMEM)
    vmem = pl.BlockSpec(memory_space=pltpu.VMEM)
    hbm = pl.BlockSpec(memory_space=pl.ANY)
    work = pltpu.VMEM((total, tiles, Y_GROUPS, SUB, LANES), jnp.float32)
    line = pltpu.VMEM((tiles, Y_GROUPS, SUB, LANES), jnp.float32)
    return pl.pallas_call(
        sweep_kernel,
        out_shape=jax.ShapeDtypeStruct(block.shape, jnp.float32),
        in_specs=[smem, hbm, hbm, hbm, hbm, hbm, vmem],
        out_specs=hbm,
        scratch_shapes=[
            pltpu.VMEM((total, tiles, Y_ROWS, LANES), jnp.float32),
            work, work, line, line,
            pltpu.VMEM((2, Y_GROUPS, SUB, LANES), jnp.float32),
            pltpu.VMEM((tiles, Y_ROWS, LANES), jnp.float32),
            pltpu.SemaphoreType.DMA((5 * tiles,)),
        ],
        compiler_params=pltpu.CompilerParams(vmem_limit_bytes=50 * MIB),
        cost_estimate=pl.CostEstimate(flops=200_000_000, bytes_accessed=12_000_000, transcendentals=0),
        name="extend_mesh",
    )(where, block, ylow, yhigh, zlow, zhigh, speed)


mass_even = (-1.0 / 15.0, 2.0 / 15.0, 8.0 / 15.0, 2.0 / 15.0, -1.0 / 15.0)
mass_odd = (0.0, 2.0 / 15.0, 16.0 / 15.0, 2.0 / 15.0, 0.0)


def mass_along(padded, axis):
    count = padded.shape[axis] - 4
    pieces = [lax.slice_in_dim(padded, i, i + count, axis=axis) for i in range(5)]
    even = sum(mass_even[i] * pieces[i] for i in range(5))
    odd = sum(mass_odd[i] * pieces[i] for i in range(1, 4))
    at_even = lax.broadcasted_iota(jnp.int32, even.shape, axis) % 2 == 0
    return jnp.where(at_even, even, odd)


def with_rows(x, width):
    size = lax.axis_size("vol")
    up = [(i, i + 1) for i in range(size - 1)]
    down = [(j, i) for i, j in up]
    before = lax.ppermute(x[-width:], "vol", up)
    after = lax.ppermute(x[:width], "vol", down)
    return jnp.concatenate([before, x, after], axis=0)


def stepwise(flux, metric):
    root = jnp.sqrt(metric)

    def dot(a, b):
        return lax.psum(jnp.sum(a * b), "vol")

    def step(_, state):
        solved, residual, direction, norm = state
        padded = jnp.pad(with_rows(root * direction, 2), ((0, 0), (2, 2)))
        image = root * mass_along(mass_along(padded, 1), 0)
        alpha = norm / dot(direction, image)
        solved = solved + alpha * direction
        residual = residual - alpha * image
        after = dot(residual, residual)
        direction = residual + after / norm * direction
        return solved, residual, direction, after

    state = (jnp.zeros_like(flux), flux, flux, dot(flux, flux))
    return with_rows(lax.fori_loop(0, ITERS, step, state)[0], DEEP)


def on_device(face_area, face_speed, face_node, face_count, surface_metric, displacement):
    vols, cols = lax.axis_size("vol"), lax.axis_size("col")
    vol, col = lax.axis_index("vol"), lax.axis_index("col")
    core = col % 2
    where = jnp.stack([core, col, jnp.int32(cols), vol, jnp.int32(vols)]).astype(jnp.int32).reshape(1, 5)
    up = [(i, i + 1) for i in range(vols - 1)]
    down = [(j, i) for i, j in up]
    col_up = [(i, i + 1) for i in range(cols - 1)]
    col_down = [(j, i) for i, j in col_up]

    with jax.named_scope("volume_halo"):
        ylow = lax.ppermute(displacement[:, -DEEP:], "vol", up)
        yhigh = lax.ppermute(displacement[:, :DEEP], "vol", down)
        wide = jnp.concatenate([ylow, displacement, yhigh], axis=1)
        zlow = lax.ppermute(wide, "col", col_up)
        zhigh = lax.ppermute(wide, "col", col_down)
    with jax.named_scope("metric_halo"):
        metric_before = lax.ppermute(surface_metric[-HALO:], "vol", up)
        metric_after = lax.ppermute(surface_metric[:HALO], "vol", down)

    keep, send = face_sums(where, face_count, face_area, face_speed, face_node)
    with jax.named_scope("flux_sum"):
        keep = keep + lax.ppermute(send, "col", [(j, j ^ 1) for j in range(cols)])
        turned = [
            lax.ppermute(keep, "col", [(j, (j + 2 * k) % cols) for j in range(cols)]) for k in (1, 2, 3)
        ]
        own = (keep + turned[1]) + (turned[0] + turned[2])
    with jax.named_scope("flux_halo"):
        other = lax.ppermute(own, "col", [(j, j ^ 1) for j in range(cols)])
        same_pairs, cross_pairs = [], []
        for i in range(vols):
            for j in range(cols):
                to = i - 1 if j % 2 == 0 else i + 1
                if 0 <= to < vols:
                    same_pairs.append((i * cols + j, to * cols + j))
                    cross_pairs.append((i * cols + j, to * cols + (j ^ 1)))
        same = lax.ppermute(own, ("vol", "col"), same_pairs)
        cross = lax.ppermute(own, ("vol", "col"), cross_pairs)

    basis, sums = surface_basis(
        where, own, other, same, cross, surface_metric, metric_before, metric_after
    )
    with jax.named_scope("gather_sums"):
        spread = jnp.broadcast_to(sums[None], (vols,) + sums.shape)
        gathered = lax.all_to_all(spread, "vol", 0, 0)
    speed, flag = surface_solve(basis, gathered)

    def step_by_step():
        low = jnp.where(core == 0, own, other)
        high = jnp.where(core == 0, other, own)
        return stepwise(jnp.concatenate([low, high], axis=0), surface_metric)

    speed = lax.cond(flag[0, 0] > 0, lambda: speed, step_by_step)
    displaced = extend_mesh(where, displacement, ylow, yhigh, zlow, zhigh, speed)
    return speed[DEEP:-DEEP], displaced


def solution(mesh):
    in_specs = (
        P("vol", "col"),
        P("vol", "col"),
        P("vol", "col"),
        P("vol", "col"),
        P("vol", None),
        P("col", "vol", None),
    )
    out_specs = (P("vol", None), P("col", "vol", None))
    return jax.shard_map(
        on_device, mesh=mesh, in_specs=in_specs, out_specs=out_specs, check_vma=False
    )
```

```python
import jax
import jax.numpy as jnp
import numpy as np
from jax import lax
from jax.experimental import pallas as pl
from jax.experimental.pallas import tpu as pltpu
from jax.sharding import PartitionSpec as P

ITERS = 10
SWEEPS = 4
LANES = 128
SUB = 8
MIB = 1024 * 1024
DEEP = 2 * SWEEPS
HALO = 32
ROWS = 128
GROUPS = 16
Y_GROUPS = 10
Y_ROWS = 80

BASIS_LOW = 0.1
BASIS_HIGH = 12.0
CONDITION_MAX = 2000.0


def rolled(x, shift, axis):
    return pltpu.roll(x, shift % x.shape[axis], axis)


def column_ring(tiles):
    n = len(tiles)
    lane = lax.broadcasted_iota(jnp.int32, tiles[0].shape, 1)
    first, last = lane == 0, lane == LANES - 1
    return (
        [jnp.where(first, 0.0, rolled(tiles[j], 1, 1)) for j in (n - 2, n - 1)]
        + list(tiles)
        + [jnp.where(last, 0.0, rolled(tiles[j], -1, 1)) for j in (0, 1)]
    )


def row_ring(rows):
    n = len(rows)
    return (
        [rolled(rows[j], 1, 0) for j in (n - 2, n - 1)]
        + list(rows)
        + [rolled(rows[j], -1, 0) for j in (0, 1)]
    )


def mass_line(padded, index):
    i = index + 2
    near = padded[i - 1] + padded[i + 1]
    if index % 2:
        return near + 8.0 * padded[i]
    return (near + 4.0 * padded[i]) - 0.5 * (padded[i - 2] + padded[i + 2])


def both_line(padded, index):
    i = index + 2
    near = padded[i - 1] + padded[i + 1]
    return (16.0 / 3.0 if index % 2 else 11.0 / 3.0) * padded[i] - near


SMEM = pl.BlockSpec(memory_space=pltpu.SMEM)
VMEM = pl.BlockSpec(memory_space=pltpu.VMEM)
HBM = pl.BlockSpec(memory_space=pl.ANY)


def f32(*shape):
    return jax.ShapeDtypeStruct(shape, jnp.float32)


def params(mib):
    return pltpu.CompilerParams(vmem_limit_bytes=mib * MIB)


def cost(us):
    return pl.CostEstimate(flops=0, bytes_accessed=int(us * 3_000_000), transcendentals=0)


def split(x):
    first = x.astype(jnp.bfloat16)
    return first, (x - first.astype(jnp.float32)).astype(jnp.bfloat16)


def to_blocked(j):
    x = lax.broadcasted_iota(jnp.int32, (1024, 256), 0)
    n = lax.broadcasted_iota(jnp.int32, (1024, 256), 1)
    hit = x == 8 * (n & 127) + j + (n >> 7)
    return jnp.where(hit, 1.0, 0.0).astype(jnp.bfloat16)


def to_plain(q):
    k = lax.broadcasted_iota(jnp.int32, (1024, 256), 0)
    x = lax.broadcasted_iota(jnp.int32, (1024, 256), 1) + 256 * q
    hit = x == 8 * (k & 127) + (k >> 7)
    return jnp.where(hit, 1.0, 0.0).astype(jnp.bfloat16)


def regroup_kernel(block_ref, metric_ref, out_ref, root_ref, up_ref, down_ref, parts_ref):
    layers, rows, _ = block_ref.shape
    total = layers * rows + rows
    for z in range(layers):
        first, second = split(block_ref[z])
        parts_ref[rows * z : rows * (z + 1), :] = first
        parts_ref[total + rows * z : total + rows * (z + 1), :] = second
    first, second = split(jnp.sqrt(metric_ref[...]))
    parts_ref[rows * layers : total, :] = first
    parts_ref[total + rows * layers : 2 * total, :] = second
    for j in range(0, 8, 2):
        pair = jnp.dot(parts_ref[...], to_blocked(j), preferred_element_type=jnp.float32)
        pair = pair[:total] + pair[total:]
        for i in range(2):
            tile = pair[:, LANES * i : LANES * (i + 1)]
            for z in range(layers):
                plane = tile[rows * z : rows * (z + 1)]
                out_ref[z, j + i] = plane
                up_ref[j + i, DEEP * z : DEEP * (z + 1), :] = plane[rows - DEEP :]
                down_ref[j + i, DEEP * z : DEEP * (z + 1), :] = plane[:DEEP]
            plane = tile[rows * layers :]
            root_ref[j + i] = plane
            up_ref[j + i, DEEP * layers :, :] = plane[rows - HALO :]
            down_ref[j + i, DEEP * layers :, :] = plane[:HALO]


def regroup(block, metric):
    layers, rows, cols = block.shape
    packed = f32(8, layers * DEEP + HALO, LANES)
    return pl.pallas_call(
        regroup_kernel,
        out_shape=(f32(layers, 8, rows, LANES), f32(8, rows, LANES), packed, packed),
        in_specs=[VMEM, VMEM],
        out_specs=(VMEM, VMEM, VMEM, VMEM),
        scratch_shapes=[pltpu.VMEM((2 * rows * (layers + 1), cols), jnp.bfloat16)],
        compiler_params=params(40),
        cost_estimate=cost(4),
        name="regroup",
    )(block, metric)


def plain_columns(parts_ref, rows, write):
    for q in range(4):
        value = jnp.dot(parts_ref[...], to_plain(q), preferred_element_type=jnp.float32)
        write(q, value[:rows] + value[rows:])


def face_kernel(where_ref, count_ref, area_ref, speed_ref, node_ref, keep_ref, send_ref, acc_ref):
    slots = area_ref.shape[1]
    chunk = min(2048, slots)
    core = where_ref[0, 0]
    ids = lax.broadcasted_iota(jnp.int32, (256, chunk), 0)
    ids = ids.astype(jnp.float32).astype(jnp.bfloat16)
    zero = jnp.zeros((), jnp.bfloat16)
    one = jnp.ones((), jnp.bfloat16)
    contract = (((1,), (1,)), ((), ()))
    acc_ref[...] = jnp.zeros_like(acc_ref)

    def wide(x):
        return jnp.broadcast_to(x.astype(jnp.bfloat16), (256, chunk))

    def body(step, carry):
        at = pl.ds(pl.multiple_of(step * chunk, chunk), chunk)
        slot = lax.broadcasted_iota(jnp.int32, (1, chunk), 1) + step * chunk
        value = jnp.where(slot < count_ref[0, 0], area_ref[:, at] * speed_ref[:, at], 0.0)
        node = node_ref[:, at]
        low = (((node & 1) << 7) + ((node >> 3) & 127)).astype(jnp.float32)
        high = (((node >> 1) & 3) * 64 + (node >> 10)).astype(jnp.float32)
        first = value.astype(jnp.bfloat16)
        second = value - first.astype(jnp.float32)
        here = wide(high) == ids
        upper = jnp.where(here, wide(first), zero)
        lower = jnp.where(here, wide(second), zero)
        columns = jnp.where(wide(low) == ids, one, zero)
        acc_ref[...] += lax.dot_general(
            upper, columns, contract, preferred_element_type=jnp.float32
        ) + lax.dot_general(lower, columns, contract, preferred_element_type=jnp.float32)
        return carry

    lax.fori_loop(0, slots // chunk, body, 0)
    for j in range(8):
        at, lanes = 64 * (j // 2), slice(LANES * (j % 2), LANES * (j % 2 + 1))
        keep_ref[j] = acc_ref[pl.ds(at + 32 * core, 32), lanes]
        send_ref[j] = acc_ref[pl.ds(at + 32 - 32 * core, 32), lanes]


def face_sums(where, count, area, speed, node):
    half = f32(8, 32, LANES)
    return pl.pallas_call(
        face_kernel,
        out_shape=(half, half),
        in_specs=[SMEM, SMEM, VMEM, VMEM, VMEM],
        out_specs=(VMEM, VMEM),
        scratch_shapes=[pltpu.VMEM((256, 256), jnp.float32)],
        compiler_params=params(32),
        cost_estimate=cost(7),
        name="face_sums",
    )(where, count, area, speed, node)


def basis_kernel(
    where_ref, own_ref, other_ref, same_ref, cross_ref, root_own_ref, before_ref, after_ref,
    basis_ref, sums_ref, field, root, line, sems,
):
    core = where_ref[0, 0]
    packed = before_ref.shape[1]
    for t in range(8):
        field[0, t, pl.ds(32 + 32 * core, 32), :] = own_ref[t]
        field[0, t, pl.ds(64 - 32 * core, 32), :] = other_ref[t]
        field[0, t, pl.ds(96 * core, 32), :] = cross_ref[t]
        field[0, t, pl.ds(96 - 96 * core, 32), :] = same_ref[t]
        root[t, 0:32, :] = before_ref[t, packed - HALO :, :]
        root[t, 32:96, :] = root_own_ref[t]
        root[t, 96:128, :] = after_ref[t, packed - HALO :, :]

    centre = (BASIS_LOW + BASIS_HIGH) / 2
    scale = 2 / (BASIS_HIGH - BASIS_LOW)
    group = lax.broadcasted_iota(jnp.int32, (SUB, LANES), 0)
    own_rows = jnp.where((group >= 2) & (group < 6), 1.0, 0.0).astype(jnp.float32)

    def rows_of(ys):
        return pl.ds(ys, SUB, stride=GROUPS)

    def out_copy(k):
        return pltpu.make_async_copy(
            field.at[k, :, pl.ds(HALO - DEEP, Y_ROWS), :], basis_ref.at[k], sems.at[k]
        )

    def step(k, carry):
        out_copy(k).start()
        before = jnp.maximum(k - 1, 0)
        first = jnp.where(k == 0, 1.0, 2.0).astype(jnp.float32)
        second = jnp.where(k == 0, 0.0, 1.0).astype(jnp.float32)
        for ys in range(GROUPS):
            weighted = [field[k, t, rows_of(ys), :] * root[t, rows_of(ys), :] for t in range(8)]
            padded = column_ring(weighted)
            for t in range(8):
                line[ys, t] = mass_line(padded, t)
        square = jnp.zeros((SUB, LANES), jnp.float32)
        shifted = jnp.zeros((SUB, LANES), jnp.float32)
        for t in range(8):
            padded = row_ring([line[ys, t] for ys in range(GROUPS)])
            for ys in range(GROUPS):
                image = (root[t, rows_of(ys), :] * (4.0 / 225.0 * scale)) * mass_line(padded, ys)
                now = field[k, t, rows_of(ys), :]
                last = field[before, t, rows_of(ys), :]
                later = first * (image - (centre * scale) * now) - second * last
                field[k + 1, t, rows_of(ys), :] = later
                square = square + now * now
                shifted = shifted + later * now
        sums_ref[pl.ds(2 * k, 1), :] = jnp.sum(square * own_rows, axis=0, keepdims=True)
        sums_ref[pl.ds(2 * k + 1, 1), :] = jnp.sum(shifted * own_rows, axis=0, keepdims=True)
        return carry

    sums_ref[...] = jnp.zeros_like(sums_ref)
    lax.fori_loop(0, ITERS, step, 0)
    for k in range(ITERS):
        out_copy(k).wait()


def surface_basis(where, own, other, same, cross, root, before, after):
    return pl.pallas_call(
        basis_kernel,
        out_shape=(f32(ITERS, 8, Y_ROWS, LANES), f32(24, LANES)),
        in_specs=[SMEM] + [VMEM] * 7,
        out_specs=(HBM, VMEM),
        scratch_shapes=[
            pltpu.VMEM((ITERS + 1, 8, ROWS, LANES), jnp.float32),
            pltpu.VMEM((8, ROWS, LANES), jnp.float32),
            pltpu.VMEM((GROUPS, 8, SUB, LANES), jnp.float32),
            pltpu.SemaphoreType.DMA((ITERS,)),
        ],
        compiler_params=params(40),
        cost_estimate=cost(7),
        name="surface_basis",
    )(where, own, other, same, cross, root, before, after)


def solve_weights():
    n = ITERS
    moment = np.zeros((2 * n, 2 * n))
    for m in range(2 * n):
        if m < 2:
            moment[m, m] = 1.0
        else:
            moment[m, m] = 2.0
            moment[m, m % 2] = -1.0
    centre, half = (BASIS_LOW + BASIS_HIGH) / 2, (BASIS_HIGH - BASIS_LOW) / 2
    weights = np.zeros((2 * n, 16, LANES))
    for i in range(n):
        for j in range(n):
            lower = abs(j - 1)
            for factor, index in (
                (centre / 2, i + j),
                (centre / 2, abs(i - j)),
                (half / 4, i + j + 1),
                (half / 4, abs(i - j - 1)),
                (half / 4, i + lower),
                (half / 4, abs(i - lower)),
            ):
                weights[:, i, j] += factor * moment[index]
        weights[:, i, n] += moment[i]
    return weights.astype(np.float32)


def solve_kernel(basis_ref, sums_ref, weights_ref, out_ref, flag_ref, part_ref, sem):
    n = ITERS
    copy = pltpu.make_async_copy(basis_ref, part_ref, sem)
    copy.start()
    total = sums_ref[0]
    for i in range(1, sums_ref.shape[0]):
        total = total + sums_ref[i]
    total = jnp.broadcast_to(jnp.sum(total, axis=1, keepdims=True), total.shape)
    row = lax.broadcasted_iota(jnp.int32, (16, LANES), 0)
    lane = lax.broadcasted_iota(jnp.int32, (16, LANES), 1)
    system = jnp.where((lane == row + 16) & (row < n), 1.0, 0.0).astype(jnp.float32)
    for m in range(2 * n):
        system = system + weights_ref[m] * total[m : m + 1, :]
    centre = jnp.sum(jnp.where(lane == row, system, 0.0), axis=1, keepdims=True)
    for k in range(n):
        pivot_row = system[k : k + 1, :] / system[k : k + 1, k : k + 1]
        column = system[:, k : k + 1]
        system = jnp.where(row == k, pivot_row, system - column * pivot_row)
    inverse = jnp.sum(jnp.where(lane == row + 16, system, 0.0), axis=1, keepdims=True)
    figure = jnp.broadcast_to(centre * inverse, (16, LANES))
    inside = (row < n) & (lane == 0)
    least = jnp.min(jnp.where(inside, figure, 1.0))
    whole = jnp.sum(jnp.where(inside, figure, 0.0))
    flag_ref[0, 0] = jnp.where((least > 0.5) & (whole < CONDITION_MAX), 1, 0).astype(jnp.int32)
    copy.wait()
    for t in range(8):
        value = None
        for k in range(n):
            term = system[k : k + 1, n : n + 1] * part_ref[k, t]
            value = term if value is None else value + term
        out_ref[t] = value


def surface_solve(basis, sums):
    return pl.pallas_call(
        solve_kernel,
        out_shape=(f32(8, Y_ROWS, LANES), jax.ShapeDtypeStruct((1, 1), jnp.int32)),
        in_specs=[HBM, VMEM, VMEM],
        out_specs=(VMEM, SMEM),
        scratch_shapes=[pltpu.VMEM(basis.shape, jnp.float32), pltpu.SemaphoreType.DMA],
        compiler_params=params(32),
        cost_estimate=cost(3),
        name="surface_solve",
    )(basis, sums, jnp.asarray(solve_weights()))


def fill_factors(factor, where_ref, rows):
    vol, vols = where_ref[0, 3], where_ref[0, 4]
    group = lax.broadcasted_iota(jnp.int32, (SUB, LANES), 0)
    mass, stiff = (8.0, 16.0), (14.0, 16.0)
    for ys in range(Y_GROUPS):
        row = group * Y_GROUPS + ys
        outside = ((vol == 0) & (row < DEEP)) | ((vol == vols - 1) & (row >= DEEP + rows))
        py = ys % 2
        for pz in range(2):
            for px in range(2):
                value = -12.0 / (
                    stiff[pz] * mass[py] * mass[px]
                    + mass[pz] * (stiff[py] * mass[px] + mass[py] * stiff[px])
                )
                factor[pz, px, ys] = jnp.where(outside, 0.0, jnp.float32(value))


def lateral_lines(get, line_a, line_b, put):
    for ys in range(Y_GROUPS):
        padded = column_ring([get(t, ys) for t in range(8)])
        for t in range(8):
            m = mass_line(padded, t)
            line_a[t, ys] = m
            line_b[t, ys] = both_line(padded, t) - m
    for t in range(8):
        a = row_ring([line_a[t, ys] for ys in range(Y_GROUPS)])
        b = row_ring([line_b[t, ys] for ys in range(Y_GROUPS)])
        for ys in range(Y_GROUPS):
            put(t, ys, mass_line(a, ys), both_line(a, ys) + mass_line(b, ys))


def pair_steps(w, c):
    near = c[1] + c[3]
    even = (11.0 / 3.0 * w[1] - (w[0] + w[2])) + ((near + 4.0 * c[2]) - 0.5 * (c[0] + c[4]))
    near = c[2] + c[4]
    odd = (16.0 / 3.0 * w[2] - (w[1] + w[3])) + (near + 8.0 * c[3])
    return even, odd


def strided(ys):
    return pl.ds(ys, SUB, stride=Y_GROUPS)


def base_kernel(
    where_ref, block_ref, before_ref, after_ref, zlow_ref, zhigh_ref, corner_low_ref, corner_high_ref,
    out_ref, field, along, cross, line_a, line_b, factor, top, parts, sems,
):
    col, cols = where_ref[0, 1], where_ref[0, 2]
    layers, _, rows, _ = block_ref.shape
    total = layers + 2 * DEEP
    copies = []

    def bring(source, at_z, nz, at_y, ny):
        copies.append(
            pltpu.make_async_copy(
                source, field.at[pl.ds(at_z, nz), :, pl.ds(at_y, ny), :], sems.at[len(copies)]
            )
        )

    bring(block_ref, DEEP, layers, DEEP, rows)
    bring(zlow_ref, 0, DEEP, DEEP, rows)
    bring(zhigh_ref, DEEP + layers, DEEP, DEEP, rows)
    for z in range(layers):
        for source, corner, at_y in ((before_ref, 0, 0), (after_ref, 1, DEEP + rows)):
            at = pl.ds(DEEP * z, DEEP)
            for part, at_z in ((source.at[:, at, :], DEEP + z),
                               (corner_low_ref.at[corner, :, at, :], z),
                               (corner_high_ref.at[corner, :, at, :], DEEP + layers + z)):
                copies.append(
                    pltpu.make_async_copy(
                        part, field.at[at_z, :, pl.ds(at_y, DEEP), :], sems.at[len(copies)]
                    )
                )
    for copy in copies:
        copy.start()
    fill_factors(factor, where_ref, rows)
    for copy in copies:
        copy.wait()

    @pl.when(col == 0)
    def _():
        for t in range(8):
            top[t] = field[DEEP, t]

    def lateral(z, carry):
        def put(t, ys, w, c):
            along[z, t, ys] = w
            cross[z, t, ys] = c

        lateral_lines(lambda t, ys: field[z, t, strided(ys), :], line_a, line_b, put)
        return carry

    def update(pair, carry):
        z = 2 * pair
        for t in range(8):
            for ys in range(Y_GROUPS):
                even, odd = pair_steps(
                    [along[z + i, t, ys] for i in range(-1, 3)], [cross[z + i, t, ys] for i in range(-2, 4)]
                )
                even = field[z, t, strided(ys), :] + factor[0, t % 2, ys] * even
                odd = field[z + 1, t, strided(ys), :] + factor[1, t % 2, ys] * odd
                field[z, t, strided(ys), :] = even
                field[z + 1, t, strided(ys), :] = odd
        return carry

    def one_sweep(sweep, carry):
        edge = 2 * sweep
        lax.fori_loop(edge, total - edge, lateral, 0)
        low = jnp.where(col == 0, DEEP // 2, sweep + 1)
        high = jnp.where(col == cols - 1, (DEEP + layers) // 2, total // 2 - sweep - 1)
        lax.fori_loop(low, high, update, 0)

        @pl.when(col == 0)
        def _():
            for t in range(8):
                field[DEEP, t] = top[t]

        return carry

    lax.fori_loop(0, SWEEPS, one_sweep, 0)
    count = layers * rows
    for z in range(layers):
        for t in range(8):
            first, second = split(field[DEEP + z, t, DEEP : DEEP + rows, :])
            lanes = slice(LANES * t, LANES * (t + 1))
            parts[rows * z : rows * (z + 1), lanes] = first
            parts[count + rows * z : count + rows * (z + 1), lanes] = second

    def write(q, value):
        out_ref[:, :, 256 * q : 256 * (q + 1)] = value.reshape(layers, rows, 256)

    plain_columns(parts, count, write)


def base_sweeps(where, block, before, after, zlow, zhigh, corner_low, corner_high):
    layers, _, rows, _ = block.shape
    total = layers + 2 * DEEP
    work = pltpu.VMEM((total, 8, Y_GROUPS, SUB, LANES), jnp.float32)
    line = pltpu.VMEM((8, Y_GROUPS, SUB, LANES), jnp.float32)
    return pl.pallas_call(
        base_kernel,
        out_shape=f32(layers, rows, 8 * LANES),
        in_specs=[SMEM] + [HBM] * 7,
        out_specs=VMEM,
        scratch_shapes=[
            pltpu.VMEM((total, 8, Y_ROWS, LANES), jnp.float32),
            work, work, line, line,
            pltpu.VMEM((2, 2, Y_GROUPS, SUB, LANES), jnp.float32),
            pltpu.VMEM((8, Y_ROWS, LANES), jnp.float32),
            pltpu.VMEM((2 * layers * rows, 8 * LANES), jnp.bfloat16),
            pltpu.SemaphoreType.DMA((3 + 6 * layers,)),
        ],
        compiler_params=params(50),
        cost_estimate=cost(25),
        name="base_sweeps",
    )(where, block, before, after, zlow, zhigh, corner_low, corner_high)


def top_kernel(
    where_ref, base_ref, speed_ref, velocity_ref, out_ref,
    cells, along, cross, line_a, line_b, factor, plain, parts, parts_speed, shown, sem,
):
    col = where_ref[0, 1]
    layers, rows, _ = out_ref.shape
    for t in range(8):
        lanes = slice(LANES * t, LANES * (t + 1))
        first, second = split(speed_ref[t, DEEP : DEEP + rows, :])
        parts_speed[:rows, lanes] = first
        parts_speed[rows:, lanes] = second

    def write_speed(q, value):
        velocity_ref[:, 256 * q : 256 * (q + 1)] = value

    plain_columns(parts_speed, rows, write_speed)

    def lateral(z, carry):
        def put(t, ys, w, c):
            along[z, t, ys] = w
            cross[z, t, ys] = c

        lateral_lines(lambda t, ys: cells[z, t, ys], line_a, line_b, put)
        return carry

    def start():
        fill_factors(factor, where_ref, rows)
        for t in range(8):
            for ys in range(Y_GROUPS):
                cells[2, t, ys] = 0.5 * speed_ref[t, strided(ys), :]

    @pl.when(col == 0)
    def _():
        copy = pltpu.make_async_copy(base_ref, shown, sem)
        copy.start()
        start()
        clear = jnp.zeros((8, Y_GROUPS, SUB, LANES), jnp.float32)
        for z in range(layers + 4):
            if z != 2:
                cross[z] = clear
                along[z] = clear
                if z < layers + 2:
                    cells[z] = clear

        def update(pair, carry):
            z = 2 * pair + 2
            for t in range(8):
                for ys in range(Y_GROUPS):
                    even, odd = pair_steps(
                        [along[z + i, t, ys] for i in range(-1, 3)],
                        [cross[z + i, t, ys] for i in range(-2, 4)],
                    )
                    cells[z, t, ys] += factor[0, t % 2, ys] * even
                    cells[z + 1, t, ys] += factor[1, t % 2, ys] * odd
            return carry

        def one_sweep(sweep, carry):
            lax.fori_loop(2, 2 * sweep + 3, lateral, 0)
            lax.fori_loop(0, jnp.minimum(sweep + 2, layers // 2), update, 0)
            for t in range(8):
                for ys in range(Y_GROUPS):
                    cells[2, t, ys] = 0.5 * speed_ref[t, strided(ys), :]
            return carry

        lax.fori_loop(0, SWEEPS, one_sweep, 0)
        count = layers * rows
        for z in range(layers):
            for t in range(8):
                for ys in range(Y_GROUPS):
                    plain[strided(ys), :] = cells[z + 2, t, ys]
                first, second = split(plain[DEEP : DEEP + rows, :])
                lanes = slice(LANES * t, LANES * (t + 1))
                parts[rows * z : rows * (z + 1), lanes] = first
                parts[count + rows * z : count + rows * (z + 1), lanes] = second
        copy.wait()

        def write(q, value):
            at = slice(256 * q, 256 * (q + 1))
            shown[:, :, at] = shown[:, :, at] + value.reshape(layers, rows, 256)

        plain_columns(parts, count, write)
        back = pltpu.make_async_copy(shown, out_ref, sem)
        back.start()
        back.wait()

    @pl.when(col == 1)
    def _():
        copy = pltpu.make_async_copy(base_ref.at[pl.ds(0, 1)], shown.at[pl.ds(0, 1)], sem)
        copy.start()
        start()

        def one_sweep(sweep, carry):
            lateral(2, 0)
            for t in range(8):
                for ys in range(Y_GROUPS):
                    cells[2, t, ys] = factor[0, t % 2, ys] * (-0.5 * cross[2, t, ys])
            return carry

        lax.fori_loop(0, SWEEPS, one_sweep, 0)
        for t in range(8):
            for ys in range(Y_GROUPS):
                plain[strided(ys), :] = cells[2, t, ys]
            first, second = split(plain[DEEP : DEEP + rows, :])
            lanes = slice(LANES * t, LANES * (t + 1))
            parts_speed[:rows, lanes] = first
            parts_speed[rows:, lanes] = second
        copy.wait()

        def write(q, value):
            at = slice(256 * q, 256 * (q + 1))
            shown[0, :, at] = shown[0, :, at] + value

        plain_columns(parts_speed, rows, write)
        back = pltpu.make_async_copy(shown.at[pl.ds(0, 1)], out_ref.at[pl.ds(0, 1)], sem)
        back.start()
        back.wait()


def add_top(where, base, speed):
    layers, rows, cols = base.shape
    work = pltpu.VMEM((layers + 4, 8, Y_GROUPS, SUB, LANES), jnp.float32)
    line = pltpu.VMEM((8, Y_GROUPS, SUB, LANES), jnp.float32)
    return pl.pallas_call(
        top_kernel,
        out_shape=(f32(rows, cols), f32(layers, rows, cols)),
        in_specs=[SMEM, HBM, VMEM],
        out_specs=(VMEM, HBM),
        input_output_aliases={1: 1},
        scratch_shapes=[
            pltpu.VMEM((layers + 2, 8, Y_GROUPS, SUB, LANES), jnp.float32),
            work, work, line, line,
            pltpu.VMEM((2, 2, Y_GROUPS, SUB, LANES), jnp.float32),
            pltpu.VMEM((Y_ROWS, LANES), jnp.float32),
            pltpu.VMEM((2 * layers * rows, cols), jnp.bfloat16),
            pltpu.VMEM((2 * rows, cols), jnp.bfloat16),
            pltpu.VMEM((layers, rows, cols), jnp.float32),
            pltpu.SemaphoreType.DMA,
        ],
        compiler_params=params(48),
        cost_estimate=cost(10),
        name="add_top",
    )(where, base, speed)


mass_even = (-1.0 / 15.0, 2.0 / 15.0, 8.0 / 15.0, 2.0 / 15.0, -1.0 / 15.0)
mass_odd = (0.0, 2.0 / 15.0, 16.0 / 15.0, 2.0 / 15.0, 0.0)


def mass_along(padded, axis):
    count = padded.shape[axis] - 4
    pieces = [lax.slice_in_dim(padded, i, i + count, axis=axis) for i in range(5)]
    even = sum(mass_even[i] * pieces[i] for i in range(5))
    odd = sum(mass_odd[i] * pieces[i] for i in range(1, 4))
    at_even = lax.broadcasted_iota(jnp.int32, even.shape, axis) % 2 == 0
    return jnp.where(at_even, even, odd)


def with_rows(x, width):
    size = lax.axis_size("vol")
    up = [(i, i + 1) for i in range(size - 1)]
    down = [(j, i) for i, j in up]
    before = lax.ppermute(x[-width:], "vol", up)
    after = lax.ppermute(x[:width], "vol", down)
    return jnp.concatenate([before, x, after], axis=0)


def stepwise(flux, metric):
    root = jnp.sqrt(metric)

    def dot(a, b):
        return lax.psum(jnp.sum(a * b), "vol")

    def step(_, state):
        solved, residual, direction, norm = state
        padded = jnp.pad(with_rows(root * direction, 2), ((0, 0), (2, 2)))
        image = root * mass_along(mass_along(padded, 1), 0)
        alpha = norm / dot(direction, image)
        solved = solved + alpha * direction
        residual = residual - alpha * image
        after = dot(residual, residual)
        direction = residual + after / norm * direction
        return solved, residual, direction, after

    state = (jnp.zeros_like(flux), flux, flux, dot(flux, flux))
    return with_rows(lax.fori_loop(0, ITERS, step, state)[0], DEEP)


def after(x, *others):
    return lax.optimization_barrier((x,) + others)[0]


def on_device(face_area, face_speed, face_node, face_count, surface_metric, displacement):
    vols, cols = lax.axis_size("vol"), lax.axis_size("col")
    vol, col = lax.axis_index("vol"), lax.axis_index("col")
    core = col % 2
    where = jnp.stack([core, col, jnp.int32(cols), vol, jnp.int32(vols)]).astype(jnp.int32).reshape(1, 5)
    up = [(i, i + 1) for i in range(vols - 1)]
    down = [(j, i) for i, j in up]
    col_up = [(i, i + 1) for i in range(cols - 1)]
    col_down = [(j, i) for i, j in col_up]
    packed = displacement.shape[0] * DEEP

    block, root, rows_up, rows_down = regroup(displacement, surface_metric)
    with jax.named_scope("row_halo"):
        rows_before = lax.ppermute(rows_up, "vol", up)
        rows_after = lax.ppermute(rows_down, "vol", down)
    with jax.named_scope("depth_halo"):
        zlow = lax.ppermute(block, "col", col_up)
        zhigh = lax.ppermute(block, "col", col_down)

    keep, send = face_sums(where, face_count, face_area, face_speed, face_node)
    with jax.named_scope("flux_sum"):
        keep = keep + lax.ppermute(send, "col", [(j, j ^ 1) for j in range(cols)])
        turned = [
            lax.ppermute(keep, "col", [(j, (j + 2 * k) % cols) for j in range(cols)]) for k in (1, 2, 3)
        ]
        own = (keep + turned[1]) + (turned[0] + turned[2])
    with jax.named_scope("flux_halo"):
        other = lax.ppermute(own, "col", [(j, j ^ 1) for j in range(cols)])
        same_pairs, cross_pairs = [], []
        for i in range(vols):
            for j in range(cols):
                to = i - 1 if j % 2 == 0 else i + 1
                if 0 <= to < vols:
                    same_pairs.append((i * cols + j, to * cols + j))
                    cross_pairs.append((i * cols + j, to * cols + (j ^ 1)))
        same = lax.ppermute(own, ("vol", "col"), same_pairs)
        cross = lax.ppermute(own, ("vol", "col"), cross_pairs)

    with jax.named_scope("corner_halo"):
        corners = jnp.stack([rows_before[:, :packed], rows_after[:, :packed]])
        corner_low = lax.ppermute(corners, "col", col_up)
        corner_high = lax.ppermute(corners, "col", col_down)

    basis, sums = surface_basis(where, own, other, same, cross, root, rows_before, rows_after)
    with jax.named_scope("gather_sums"):
        spread = jnp.broadcast_to(sums[None], (vols,) + sums.shape)
        gathered = lax.all_to_all(spread, "vol", 0, 0)
    base = base_sweeps(where, block, rows_before, rows_after, zlow, zhigh, corner_low, corner_high)
    speed, flag = surface_solve(basis, gathered)

    def step_by_step():
        low = jnp.where(core == 0, own, other)
        high = jnp.where(core == 0, other, own)
        flux = jnp.concatenate([low, high], axis=1)
        flux = flux.transpose(1, 2, 0).reshape(surface_metric.shape)
        wide = stepwise(flux, surface_metric)
        return wide.reshape(Y_ROWS, LANES, 8).transpose(2, 0, 1)

    speed = lax.cond(flag[0, 0] > 0, lambda: speed, step_by_step)
    return add_top(where, base, speed)


def solution(mesh):
    in_specs = (
        P("vol", "col"),
        P("vol", "col"),
        P("vol", "col"),
        P("vol", "col"),
        P("vol", None),
        P("col", "vol", None),
    )
    out_specs = (P("vol", None), P("col", "vol", None))
    return jax.shard_map(
        on_device, mesh=mesh, in_specs=in_specs, out_specs=out_specs, check_vma=False
    )
```

```python
import jax
import jax.numpy as jnp
import numpy as np
from jax import lax
from jax.experimental import pallas as pl
from jax.experimental.pallas import tpu as pltpu
from jax.sharding import PartitionSpec as P

ITERS = 10
SWEEPS = 4
LANES = 128
SUB = 8
MIB = 1024 * 1024
DEEP = 2 * SWEEPS
HALO = 32
ROWS = 128
GROUPS = 16
Y_GROUPS = 10
Y_ROWS = 80

BASIS_LOW = 0.1
BASIS_HIGH = 12.0
CONDITION_MAX = 2000.0


def rolled(x, shift, axis):
    return pltpu.roll(x, shift % x.shape[axis], axis)


def column_ring(tiles):
    n = len(tiles)
    lane = lax.broadcasted_iota(jnp.int32, tiles[0].shape, 1)
    first, last = lane == 0, lane == LANES - 1
    return (
        [jnp.where(first, 0.0, rolled(tiles[j], 1, 1)) for j in (n - 2, n - 1)]
        + list(tiles)
        + [jnp.where(last, 0.0, rolled(tiles[j], -1, 1)) for j in (0, 1)]
    )


def row_ring(rows):
    n = len(rows)
    return (
        [rolled(rows[j], 1, 0) for j in (n - 2, n - 1)]
        + list(rows)
        + [rolled(rows[j], -1, 0) for j in (0, 1)]
    )


def mass_line(padded, index):
    i = index + 2
    near = padded[i - 1] + padded[i + 1]
    if index % 2:
        return near + 8.0 * padded[i]
    return (near + 4.0 * padded[i]) - 0.5 * (padded[i - 2] + padded[i + 2])


def both_line(padded, index):
    i = index + 2
    near = padded[i - 1] + padded[i + 1]
    return (16.0 / 3.0 if index % 2 else 11.0 / 3.0) * padded[i] - near


SMEM = pl.BlockSpec(memory_space=pltpu.SMEM)
VMEM = pl.BlockSpec(memory_space=pltpu.VMEM)
HBM = pl.BlockSpec(memory_space=pl.ANY)


def f32(*shape):
    return jax.ShapeDtypeStruct(shape, jnp.float32)


def params(mib):
    return pltpu.CompilerParams(vmem_limit_bytes=mib * MIB)


def cost(us):
    return pl.CostEstimate(flops=0, bytes_accessed=int(us * 3_000_000), transcendentals=0)


def split(x):
    first = x.astype(jnp.bfloat16)
    return first, (x - first.astype(jnp.float32)).astype(jnp.bfloat16)


def to_blocked(j):
    x = lax.broadcasted_iota(jnp.int32, (1024, 256), 0)
    n = lax.broadcasted_iota(jnp.int32, (1024, 256), 1)
    hit = x == 8 * (n & 127) + j + (n >> 7)
    return jnp.where(hit, 1.0, 0.0).astype(jnp.bfloat16)


def plain_selection():
    k = np.arange(1024)
    out = np.zeros((1024, 1024), np.float32)
    out[k, 8 * (k % LANES) + k // LANES] = 1.0
    return jnp.asarray(out, jnp.bfloat16)


def regroup_kernel(block_ref, metric_ref, before_ref, after_ref, wide_ref, root_ref, parts_ref):
    layers, rows, _ = block_ref.shape
    packed = DEEP * layers
    total = layers * Y_ROWS + ROWS

    def put(at, value):
        first, second = split(value)
        parts_ref[at : at + value.shape[0], :] = first
        parts_ref[total + at : total + at + value.shape[0], :] = second

    for z in range(layers):
        put(Y_ROWS * z, before_ref[DEEP * z : DEEP * (z + 1), :])
        put(Y_ROWS * z + DEEP, block_ref[z])
        put(Y_ROWS * z + DEEP + rows, after_ref[DEEP * z : DEEP * (z + 1), :])
    at = layers * Y_ROWS
    put(at, jnp.sqrt(before_ref[packed:, :]))
    put(at + HALO, jnp.sqrt(metric_ref[...]))
    put(at + HALO + rows, jnp.sqrt(after_ref[packed:, :]))
    for j in range(0, 8, 2):
        pair = jnp.dot(parts_ref[...], to_blocked(j), preferred_element_type=jnp.float32)
        pair = pair[:total] + pair[total:]
        for i in range(2):
            tile = pair[:, LANES * i : LANES * (i + 1)]
            for z in range(layers):
                wide_ref[z, j + i] = tile[Y_ROWS * z : Y_ROWS * (z + 1)]
            root_ref[j + i] = tile[layers * Y_ROWS :]


def regroup(block, metric, before, after):
    layers, rows, cols = block.shape
    return pl.pallas_call(
        regroup_kernel,
        out_shape=(f32(layers, 8, Y_ROWS, LANES), f32(8, ROWS, LANES)),
        in_specs=[VMEM] * 4,
        out_specs=(VMEM, VMEM),
        scratch_shapes=[pltpu.VMEM((2 * (Y_ROWS * layers + ROWS), cols), jnp.bfloat16)],
        compiler_params=params(40),
        cost_estimate=cost(6),
        name="regroup",
    )(block, metric, before, after)


def plain_columns(select_ref, parts, rows, write):
    for q in range(4):
        at = slice(256 * q, 256 * (q + 1))
        value = jnp.dot(parts, select_ref[:, at], preferred_element_type=jnp.float32)
        write(at, value[:rows] + value[rows:])


def face_kernel(
    where_ref, count_ref, area_ref, speed_ref, node_ref, block_ref, metric_ref,
    keep_ref, send_ref, up_ref, down_ref, acc_ref, sems,
):
    slots = area_ref.shape[1]
    layers, rows, _ = block_ref.shape
    copies = []
    for out_ref, row, root_row in ((up_ref, rows - DEEP, rows - HALO), (down_ref, 0, 0)):
        for z in range(layers):
            part = block_ref.at[z, pl.ds(row, DEEP), :]
            copies.append((part, out_ref.at[pl.ds(DEEP * z, DEEP), :]))
        part = metric_ref.at[pl.ds(root_row, HALO), :]
        copies.append((part, out_ref.at[pl.ds(DEEP * layers, HALO), :]))
    copies = [pltpu.make_async_copy(*pair, sems.at[i]) for i, pair in enumerate(copies)]
    for copy in copies:
        copy.start()
    chunk = min(2048, slots)
    core = where_ref[0, 0]
    ids = lax.broadcasted_iota(jnp.int32, (256, chunk), 0)
    ids = ids.astype(jnp.float32).astype(jnp.bfloat16)
    zero = jnp.zeros((), jnp.bfloat16)
    one = jnp.ones((), jnp.bfloat16)
    contract = (((1,), (1,)), ((), ()))
    acc_ref[...] = jnp.zeros_like(acc_ref)

    def wide(x):
        return jnp.broadcast_to(x.astype(jnp.bfloat16), (256, chunk))

    def body(step, carry):
        at = pl.ds(pl.multiple_of(step * chunk, chunk), chunk)
        slot = lax.broadcasted_iota(jnp.int32, (1, chunk), 1) + step * chunk
        value = jnp.where(slot < count_ref[0, 0], area_ref[:, at] * speed_ref[:, at], 0.0)
        node = node_ref[:, at]
        low = (((node & 1) << 7) + ((node >> 3) & 127)).astype(jnp.float32)
        high = (((node >> 1) & 3) * 64 + (node >> 10)).astype(jnp.float32)
        first = value.astype(jnp.bfloat16)
        second = value - first.astype(jnp.float32)
        here = wide(high) == ids
        upper = jnp.where(here, wide(first), zero)
        lower = jnp.where(here, wide(second), zero)
        columns = jnp.where(wide(low) == ids, one, zero)
        acc_ref[...] += lax.dot_general(
            upper, columns, contract, preferred_element_type=jnp.float32
        ) + lax.dot_general(lower, columns, contract, preferred_element_type=jnp.float32)
        return carry

    lax.fori_loop(0, slots // chunk, body, 0)
    for j in range(8):
        at, lanes = 64 * (j // 2), slice(LANES * (j % 2), LANES * (j % 2 + 1))
        keep_ref[j] = acc_ref[pl.ds(at + 32 * core, 32), lanes]
        send_ref[j] = acc_ref[pl.ds(at + 32 - 32 * core, 32), lanes]
    for copy in copies:
        copy.wait()


def face_sums(where, count, area, speed, node, block, metric):
    half = f32(8, 32, LANES)
    layers, _, cols = block.shape
    rows = f32(DEEP * layers + HALO, cols)
    return pl.pallas_call(
        face_kernel,
        out_shape=(half, half, rows, rows),
        in_specs=[SMEM, SMEM, VMEM, VMEM, VMEM, HBM, HBM],
        out_specs=(VMEM, VMEM, HBM, HBM),
        scratch_shapes=[
            pltpu.VMEM((256, 256), jnp.float32),
            pltpu.SemaphoreType.DMA((2 * layers + 2,)),
        ],
        compiler_params=params(32),
        cost_estimate=cost(7),
        name="face_sums",
    )(where, count, area, speed, node, block, metric)


def basis_kernel(
    where_ref, own_ref, other_ref, same_ref, cross_ref, root_ref,
    basis_ref, sums_ref, rows, field, root, outer, line, partial, sems,
):
    core = where_ref[0, 0]
    centre = (BASIS_LOW + BASIS_HIGH) / 2
    scale = 2 / (BASIS_HIGH - BASIS_LOW)
    for t in range(8):
        rows[t, pl.ds(32 + 32 * core, 32), :] = own_ref[t]
        rows[t, pl.ds(64 - 32 * core, 32), :] = other_ref[t]
        rows[t, pl.ds(96 * core, 32), :] = cross_ref[t]
        rows[t, pl.ds(96 - 96 * core, 32), :] = same_ref[t]
    for t in range(8):
        for ys in range(GROUPS):
            field[0, t, ys] = rows[t, pl.ds(ys, SUB, stride=GROUPS), :]
            value = root_ref[t, pl.ds(ys, SUB, stride=GROUPS), :]
            root[t, ys] = value
            outer[t, ys] = value * (2 * scale * 4.0 / 225.0)

    group = lax.broadcasted_iota(jnp.int32, (SUB, LANES), 0)
    own_rows = jnp.where((group >= 2) & (group < 6), 1.0, 0.0).astype(jnp.float32)

    def out_copy(k):
        return pltpu.make_async_copy(field.at[k], basis_ref.at[k], sems.at[k])

    def step(k, begin):
        out_copy(k).start()
        for ys in range(GROUPS):
            padded = column_ring([field[k, t, ys] * root[t, ys] for t in range(8)])
            for t in range(8):
                line[ys, t] = mass_line(padded, t)
        squares, shifts = [], []
        for t in range(8):
            square = jnp.zeros((SUB, LANES), jnp.float32)
            shifted = jnp.zeros((SUB, LANES), jnp.float32)
            padded = row_ring([line[ys, t] for ys in range(GROUPS)])
            for ys in range(GROUPS):
                now = field[k, t, ys]
                later = outer[t, ys] * mass_line(padded, ys) - (2 * centre * scale) * now
                later = 0.5 * later if begin else later - field[k - 1, t, ys]
                field[k + 1, t, ys] = later
                square = square + now * now
                shifted = shifted + later * now
            squares.append(square)
            shifts.append(shifted)

        def add(parts):
            while len(parts) > 1:
                parts = [parts[i] + parts[i + 1] for i in range(0, len(parts), 2)]
            return jnp.sum(parts[0] * own_rows, axis=0, keepdims=True)

        partial[pl.ds(2 * k, 1), :] = add(squares)
        partial[pl.ds(2 * k + 1, 1), :] = add(shifts)

    def later_step(k, carry):
        step(k, False)
        return carry

    partial[...] = jnp.zeros_like(partial)
    step(0, True)
    lax.fori_loop(1, ITERS, later_step, 0)
    whole = jnp.sum(partial[...], axis=1, keepdims=True)
    row = lax.broadcasted_iota(jnp.int32, partial.shape, 0)
    lane = lax.broadcasted_iota(jnp.int32, partial.shape, 1)
    line_of = jnp.sum(jnp.where(row == lane, whole, 0.0), axis=0, keepdims=True)
    sums_ref[...] = jnp.broadcast_to(line_of, sums_ref.shape)
    for k in range(ITERS):
        out_copy(k).wait()


def surface_basis(where, own, other, same, cross, root):
    return pl.pallas_call(
        basis_kernel,
        out_shape=(f32(ITERS, 8, GROUPS, SUB, LANES), f32(SUB, LANES)),
        in_specs=[SMEM] + [VMEM] * 5,
        out_specs=(HBM, VMEM),
        scratch_shapes=[
            pltpu.VMEM((8, ROWS, LANES), jnp.float32),
            pltpu.VMEM((ITERS + 1, 8, GROUPS, SUB, LANES), jnp.float32),
            pltpu.VMEM((8, GROUPS, SUB, LANES), jnp.float32),
            pltpu.VMEM((8, GROUPS, SUB, LANES), jnp.float32),
            pltpu.VMEM((GROUPS, 8, SUB, LANES), jnp.float32),
            pltpu.VMEM((24, LANES), jnp.float32),
            pltpu.SemaphoreType.DMA((ITERS,)),
        ],
        compiler_params=params(40),
        cost_estimate=cost(7),
        name="surface_basis",
    )(where, own, other, same, cross, root)


def solve_weights():
    n = ITERS
    moment = np.zeros((2 * n, 2 * n))
    for m in range(2 * n):
        if m < 2:
            moment[m, m] = 1.0
        else:
            moment[m, m] = 2.0
            moment[m, m % 2] = -1.0
    centre, half = (BASIS_LOW + BASIS_HIGH) / 2, (BASIS_HIGH - BASIS_LOW) / 2
    weights = np.zeros((2 * n, 16, LANES))
    for i in range(n):
        for j in range(n):
            lower = abs(j - 1)
            for factor, index in (
                (centre / 2, i + j),
                (centre / 2, abs(i - j)),
                (half / 4, i + j + 1),
                (half / 4, abs(i - j - 1)),
                (half / 4, i + lower),
                (half / 4, abs(i - lower)),
            ):
                weights[:, i, j] += factor * moment[index]
        weights[:, i, n] += moment[i]
    return weights.astype(np.float32)


def solve_kernel(basis_ref, sums_ref, weights_ref, out_ref, flag_ref, part_ref, rows, sem):
    n = ITERS
    copy = pltpu.make_async_copy(basis_ref, part_ref, sem)
    copy.start()
    total = sums_ref[0]
    for i in range(1, sums_ref.shape[0]):
        total = total + sums_ref[i]
    row = lax.broadcasted_iota(jnp.int32, (16, LANES), 0)
    lane = lax.broadcasted_iota(jnp.int32, (16, LANES), 1)
    system = jnp.where((lane == row + 16) & (row < n), 1.0, 0.0).astype(jnp.float32)
    for m in range(2 * n):
        system = system + weights_ref[m] * total[0:1, m : m + 1]
    centre = jnp.sum(jnp.where(lane == row, system, 0.0), axis=1, keepdims=True)
    for k in range(n):
        pivot_row = system[k : k + 1, :] / system[k : k + 1, k : k + 1]
        column = system[:, k : k + 1]
        system = jnp.where(row == k, pivot_row, system - column * pivot_row)
    inverse = jnp.sum(jnp.where(lane == row + 16, system, 0.0), axis=1, keepdims=True)
    figure = jnp.broadcast_to(centre * inverse, (16, LANES))
    inside = (row < n) & (lane == 0)
    least = jnp.min(jnp.where(inside, figure, 1.0))
    whole = jnp.sum(jnp.where(inside, figure, 0.0))
    flag_ref[0, 0] = jnp.where((least > 0.5) & (whole < CONDITION_MAX), 1, 0).astype(jnp.int32)
    copy.wait()
    weights = [jnp.broadcast_to(system[k : k + 1, n : n + 1], (SUB, LANES)) for k in range(n)]
    for t in range(8):
        for ys in range(GROUPS):
            value = weights[0] * part_ref[0, t, ys]
            for k in range(1, n):
                value = value + weights[k] * part_ref[k, t, ys]
            rows[t, pl.ds(ys, SUB, stride=GROUPS), :] = value
        out_ref[t] = rows[t, HALO - DEEP : HALO - DEEP + Y_ROWS, :]


def surface_solve(basis, sums):
    return pl.pallas_call(
        solve_kernel,
        out_shape=(f32(8, Y_ROWS, LANES), jax.ShapeDtypeStruct((1, 1), jnp.int32)),
        in_specs=[HBM, VMEM, VMEM],
        out_specs=(VMEM, SMEM),
        scratch_shapes=[
            pltpu.VMEM(basis.shape, jnp.float32),
            pltpu.VMEM((8, ROWS, LANES), jnp.float32),
            pltpu.SemaphoreType.DMA,
        ],
        compiler_params=params(32),
        cost_estimate=cost(3),
        name="surface_solve",
    )(basis, sums, jnp.asarray(solve_weights()))


def fill_factors(factor, where_ref, rows):
    vol, vols = where_ref[0, 3], where_ref[0, 4]
    group = lax.broadcasted_iota(jnp.int32, (SUB, LANES), 0)
    mass, stiff = (8.0, 16.0), (14.0, 16.0)
    for ys in range(Y_GROUPS):
        row = group * Y_GROUPS + ys
        outside = ((vol == 0) & (row < DEEP)) | ((vol == vols - 1) & (row >= DEEP + rows))
        py = ys % 2
        for pz in range(2):
            for px in range(2):
                value = -12.0 / (
                    stiff[pz] * mass[py] * mass[px]
                    + mass[pz] * (stiff[py] * mass[px] + mass[py] * stiff[px])
                )
                factor[pz, px, ys] = jnp.where(outside, 0.0, jnp.float32(value))


def lateral_lines(get, line_a, line_b, put):
    for ys in range(Y_GROUPS):
        padded = column_ring([get(t, ys) for t in range(8)])
        for t in range(8):
            m = mass_line(padded, t)
            line_a[t, ys] = m
            line_b[t, ys] = both_line(padded, t) - m
    for t in range(8):
        a = row_ring([line_a[t, ys] for ys in range(Y_GROUPS)])
        b = row_ring([line_b[t, ys] for ys in range(Y_GROUPS)])
        for ys in range(Y_GROUPS):
            put(t, ys, mass_line(a, ys), both_line(a, ys) + mass_line(b, ys))


def pair_steps(w, c):
    near = c[1] + c[3]
    even = (11.0 / 3.0 * w[1] - (w[0] + w[2])) + ((near + 4.0 * c[2]) - 0.5 * (c[0] + c[4]))
    near = c[2] + c[4]
    odd = (16.0 / 3.0 * w[2] - (w[1] + w[3])) + (near + 8.0 * c[3])
    return even, odd


def strided(ys):
    return pl.ds(ys, SUB, stride=Y_GROUPS)


def change_kernel(
    where_ref, speed_ref, out_ref, cells, along, cross, line_a, line_b, factor, plain, sem,
):
    col = where_ref[0, 1]
    layers, _, rows, _ = out_ref.shape

    def lateral(z, carry):
        def put(t, ys, w, c):
            along[z, t, ys] = w
            cross[z, t, ys] = c

        lateral_lines(lambda t, ys: cells[z, t, ys], line_a, line_b, put)
        return carry

    def set_top():
        for t in range(8):
            for ys in range(Y_GROUPS):
                cells[2, t, ys] = 0.5 * speed_ref[t, strided(ys), :]

    def send(count):
        for z in range(count):
            for t in range(8):
                for ys in range(Y_GROUPS):
                    plain[z, t, strided(ys), :] = cells[z + 2, t, ys]
        copy = pltpu.make_async_copy(
            plain.at[pl.ds(0, count), :, pl.ds(DEEP, rows), :], out_ref.at[pl.ds(0, count)], sem
        )
        copy.start()
        copy.wait()

    @pl.when(col == 0)
    def _():
        fill_factors(factor, where_ref, rows)
        set_top()
        clear = jnp.zeros((8, Y_GROUPS, SUB, LANES), jnp.float32)
        for z in range(layers + 3):
            if z != 2:
                cross[z] = clear
                if z:
                    along[z] = clear
        for z in range(3, layers + 2):
            cells[z] = clear

        def update(pair, carry):
            z = 2 * pair + 2
            for ys in range(Y_GROUPS):
                factors = [[factor[pz, px, ys] for px in range(2)] for pz in range(2)]
                for t in range(8):
                    even, odd = pair_steps(
                        [along[z + i, t, ys] for i in range(-1, 3)],
                        [cross[z + i, t, ys] for i in range(-2, 3)],
                    )
                    cells[z, t, ys] += factors[0][t % 2] * even
                    cells[z + 1, t, ys] += factors[1][t % 2] * odd
            return carry

        def one_sweep(sweep, carry):
            lax.fori_loop(2, 2 * sweep + 3, lateral, 0)
            lax.fori_loop(0, jnp.minimum(sweep + 2, layers // 2), update, 0)
            set_top()
            return carry

        lax.fori_loop(0, SWEEPS, one_sweep, 0)
        send(layers)

    @pl.when(col == 1)
    def _():
        fill_factors(factor, where_ref, rows)
        set_top()

        def one_sweep(sweep, carry):
            lateral(2, 0)
            for t in range(8):
                for ys in range(Y_GROUPS):
                    cells[2, t, ys] = factor[0, t % 2, ys] * (-0.5 * cross[2, t, ys])
            return carry

        lax.fori_loop(0, SWEEPS, one_sweep, 0)
        send(1)


def surface_change(where, speed, layers, rows):
    work = pltpu.VMEM((layers + 4, 8, Y_GROUPS, SUB, LANES), jnp.float32)
    line = pltpu.VMEM((8, Y_GROUPS, SUB, LANES), jnp.float32)
    return pl.pallas_call(
        change_kernel,
        out_shape=f32(layers, 8, rows, LANES),
        in_specs=[SMEM, VMEM],
        out_specs=HBM,
        scratch_shapes=[
            pltpu.VMEM((layers + 2, 8, Y_GROUPS, SUB, LANES), jnp.float32),
            work, work, line, line,
            pltpu.VMEM((2, 2, Y_GROUPS, SUB, LANES), jnp.float32),
            pltpu.VMEM((layers, 8, Y_ROWS, LANES), jnp.float32),
            pltpu.SemaphoreType.DMA,
        ],
        compiler_params=params(40),
        cost_estimate=cost(8),
        name="surface_change",
    )(where, speed)


def base_kernel(
    where_ref, wide_ref, zlow_ref, zhigh_ref, change_ref, speed_ref, select_ref,
    velocity_ref, out_ref, field, along, cross, line_a, line_b, factor, change, parts, sems,
):
    col, cols = where_ref[0, 1], where_ref[0, 2]
    layers, _, rows, _ = change_ref.shape
    total = layers + 2 * DEEP
    own = pltpu.make_async_copy(wide_ref, field.at[pl.ds(DEEP, layers)], sems.at[0])
    low = pltpu.make_async_copy(zlow_ref, field.at[pl.ds(0, DEEP)], sems.at[1])
    high = pltpu.make_async_copy(zhigh_ref, field.at[pl.ds(DEEP + layers, DEEP)], sems.at[2])
    all_change = pltpu.make_async_copy(change_ref, change, sems.at[3])
    one_change = pltpu.make_async_copy(
        change_ref.at[pl.ds(0, 1)], change.at[pl.ds(0, 1)], sems.at[4]
    )
    own.start()
    low.start()
    high.start()
    pl.when(col == 0)(all_change.start)
    pl.when(col == 1)(one_change.start)
    fill_factors(factor, where_ref, rows)
    count = (layers + 1) * rows

    def cut(value, at, t):
        first, second = split(value)
        lanes = slice(LANES * t, LANES * (t + 1))
        parts[at : at + rows, lanes] = first
        parts[count + at : count + at + rows, lanes] = second

    for t in range(8):
        cut(speed_ref[t, DEEP : DEEP + rows, :], 0, t)

    def lateral(z, carry):
        def put(t, ys, w, c):
            along[z, t, ys] = w
            cross[z, t, ys] = c

        lateral_lines(lambda t, ys: field[z, t, strided(ys), :], line_a, line_b, put)
        return carry

    def update(pair, carry):
        z = 2 * pair
        for ys in range(Y_GROUPS):
            factors = [[factor[pz, px, ys] for px in range(2)] for pz in range(2)]
            for t in range(8):
                even, odd = pair_steps(
                    [along[z + i, t, ys] for i in range(-1, 3)], [cross[z + i, t, ys] for i in range(-2, 3)]
                )
                scale = jnp.where((col == 0) & (z == DEEP), 0.0, factors[0][t % 2])
                even = field[z, t, strided(ys), :] + scale * even
                odd = field[z + 1, t, strided(ys), :] + factors[1][t % 2] * odd
                field[z, t, strided(ys), :] = even
                field[z + 1, t, strided(ys), :] = odd
        return carry

    begin = jnp.where(col == 0, DEEP, 0)
    end = jnp.where(col == cols - 1, DEEP + layers + 1, total - 1)

    def one_sweep(sweep, carry):
        first = jnp.maximum(begin, 2 * sweep)
        last = jnp.minimum(end, total - 2 * sweep - 1)

        @pl.when(sweep == 0)
        def _():
            own.wait()

        lax.fori_loop(jnp.where(sweep == 0, DEEP, first), jnp.where(sweep == 0, DEEP + layers, last), lateral, 0)

        @pl.when(sweep == 0)
        def _():
            low.wait()
            high.wait()

        lax.fori_loop(jnp.where(sweep == 0, first, DEEP), DEEP, lateral, 0)
        lax.fori_loop(jnp.where(sweep == 0, DEEP + layers, last), last, lateral, 0)
        low_pair = jnp.where(col == 0, DEEP // 2, sweep + 1)
        high_pair = jnp.where(col == cols - 1, (DEEP + layers) // 2, total // 2 - sweep - 1)
        lax.fori_loop(low_pair, high_pair, update, 0)
        return carry

    @pl.when(col == 0)
    def _():
        clear = jnp.zeros((8, Y_GROUPS, SUB, LANES), jnp.float32)
        for z in (DEEP - 2, DEEP - 1):
            along[z] = clear
            cross[z] = clear

    lax.fori_loop(0, SWEEPS, one_sweep, 0)

    @pl.when(col == 0)
    def _():
        all_change.wait()
        for z in range(layers):
            for t in range(8):
                field[DEEP + z, t, DEEP : DEEP + rows, :] += change[z, t]

    @pl.when(col == 1)
    def _():
        one_change.wait()
        for t in range(8):
            field[DEEP, t, DEEP : DEEP + rows, :] += change[0, t]

    for z in range(layers):
        for t in range(8):
            cut(field[DEEP + z, t, DEEP : DEEP + rows, :], rows * (z + 1), t)

    def write(at, value):
        velocity_ref[:, at] = value[:rows]
        out_ref[:, :, at] = value[rows:].reshape(layers, rows, 256)

    plain_columns(select_ref, parts[...], count, write)


def base_sweeps(where, wide, zlow, zhigh, change, speed, select):
    layers, _, rows, _ = change.shape
    total = layers + 2 * DEEP
    work = pltpu.VMEM((total, 8, Y_GROUPS, SUB, LANES), jnp.float32)
    line = pltpu.VMEM((8, Y_GROUPS, SUB, LANES), jnp.float32)
    return pl.pallas_call(
        base_kernel,
        out_shape=(f32(rows, 8 * LANES), f32(layers, rows, 8 * LANES)),
        in_specs=[SMEM] + [HBM] * 4 + [VMEM] * 2,
        out_specs=(VMEM, VMEM),
        scratch_shapes=[
            pltpu.VMEM((total, 8, Y_ROWS, LANES), jnp.float32),
            work, work, line, line,
            pltpu.VMEM((2, 2, Y_GROUPS, SUB, LANES), jnp.float32),
            pltpu.VMEM((layers, 8, rows, LANES), jnp.float32),
            pltpu.VMEM((2 * (layers + 1) * rows, 8 * LANES), jnp.bfloat16),
            pltpu.SemaphoreType.DMA((5,)),
        ],
        compiler_params=params(50),
        cost_estimate=cost(25),
        name="base_sweeps",
    )(where, wide, zlow, zhigh, change, speed, select)


mass_even = (-1.0 / 15.0, 2.0 / 15.0, 8.0 / 15.0, 2.0 / 15.0, -1.0 / 15.0)
mass_odd = (0.0, 2.0 / 15.0, 16.0 / 15.0, 2.0 / 15.0, 0.0)


def mass_along(padded, axis):
    count = padded.shape[axis] - 4
    pieces = [lax.slice_in_dim(padded, i, i + count, axis=axis) for i in range(5)]
    even = sum(mass_even[i] * pieces[i] for i in range(5))
    odd = sum(mass_odd[i] * pieces[i] for i in range(1, 4))
    at_even = lax.broadcasted_iota(jnp.int32, even.shape, axis) % 2 == 0
    return jnp.where(at_even, even, odd)


def with_rows(x, width):
    size = lax.axis_size("vol")
    up = [(i, i + 1) for i in range(size - 1)]
    down = [(j, i) for i, j in up]
    before = lax.ppermute(x[-width:], "vol", up)
    after = lax.ppermute(x[:width], "vol", down)
    return jnp.concatenate([before, x, after], axis=0)


def stepwise(flux, metric):
    root = jnp.sqrt(metric)

    def dot(a, b):
        return lax.psum(jnp.sum(a * b), "vol")

    def step(_, state):
        solved, residual, direction, norm = state
        padded = jnp.pad(with_rows(root * direction, 2), ((0, 0), (2, 2)))
        image = root * mass_along(mass_along(padded, 1), 0)
        alpha = norm / dot(direction, image)
        solved = solved + alpha * direction
        residual = residual - alpha * image
        after = dot(residual, residual)
        direction = residual + after / norm * direction
        return solved, residual, direction, after

    state = (jnp.zeros_like(flux), flux, flux, dot(flux, flux))
    return with_rows(lax.fori_loop(0, ITERS, step, state)[0], DEEP)


def after(x, *others):
    return lax.optimization_barrier((x,) + others)[0]


def on_device(face_area, face_speed, face_node, face_count, surface_metric, displacement):
    vols, cols = lax.axis_size("vol"), lax.axis_size("col")
    vol, col = lax.axis_index("vol"), lax.axis_index("col")
    core = col % 2
    where = jnp.stack([core, col, jnp.int32(cols), vol, jnp.int32(vols)]).astype(jnp.int32).reshape(1, 5)
    up = [(i, i + 1) for i in range(vols - 1)]
    down = [(j, i) for i, j in up]
    col_up = [(i, i + 1) for i in range(cols - 1)]
    col_down = [(j, i) for i, j in col_up]
    packed = displacement.shape[0] * DEEP

    select = plain_selection()

    def moved(x, steps):
        dv, dc = steps
        pairs = [
            (i * cols + j, (i + dv) * cols + j + dc)
            for i in range(vols)
            for j in range(cols)
            if 0 <= i + dv < vols and 0 <= j + dc < cols
        ]
        return lax.ppermute(x, ("vol", "col"), pairs)

    keep, send, rows_up, rows_down = face_sums(
        where, face_count, face_area, face_speed, face_node, displacement, surface_metric
    )
    with jax.named_scope("flux_sum"):
        keep = keep + lax.ppermute(send, "col", [(j, j ^ 1) for j in range(cols)])
        turned = [
            lax.ppermute(keep, "col", [(j, (j + 2 * k) % cols) for j in range(cols)]) for k in (1, 2, 3)
        ]
        own = (keep + turned[1]) + (turned[0] + turned[2])
    with jax.named_scope("row_halo"):
        rows_before, rows_after = moved(rows_up, (1, 0)), moved(rows_down, (-1, 0))
    wide, root = regroup(displacement, surface_metric, rows_before, rows_after)
    own = after(own, wide)
    with jax.named_scope("flux_halo"):
        other = lax.ppermute(own, "col", [(j, j ^ 1) for j in range(cols)])
        same_pairs, cross_pairs = [], []
        for i in range(vols):
            for j in range(cols):
                to = i - 1 if j % 2 == 0 else i + 1
                if 0 <= to < vols:
                    same_pairs.append((i * cols + j, to * cols + j))
                    cross_pairs.append((i * cols + j, to * cols + (j ^ 1)))
        same = lax.ppermute(own, ("vol", "col"), same_pairs)
        cross = lax.ppermute(own, ("vol", "col"), cross_pairs)

    with jax.named_scope("depth_halo"):
        sent = after(wide, other)
        zlow, zhigh = moved(sent, (0, 1)), moved(sent, (0, -1))
    basis, sums = surface_basis(where, own, other, same, cross, root)
    with jax.named_scope("gather_sums"):
        spread = jnp.broadcast_to(sums[None], (vols,) + sums.shape)
        gathered = lax.all_to_all(spread, "vol", 0, 0)
    speed, flag = surface_solve(basis, gathered)

    def step_by_step(state):
        low = jnp.where(core == 0, own, other)
        high = jnp.where(core == 0, other, own)
        flux = jnp.concatenate([low, high], axis=1)
        flux = flux.transpose(1, 2, 0).reshape(surface_metric.shape)
        wide = stepwise(flux, surface_metric)
        return jnp.int32(1), wide.reshape(Y_ROWS, LANES, 8).transpose(2, 0, 1)

    _, speed = lax.while_loop(lambda state: state[0] == 0, step_by_step, (flag[0, 0], speed))
    change = surface_change(where, speed, displacement.shape[0], displacement.shape[1])
    return base_sweeps(where, wide, zlow, zhigh, change, speed, select)


def solution(mesh):
    in_specs = (
        P("vol", "col"),
        P("vol", "col"),
        P("vol", "col"),
        P("vol", "col"),
        P("vol", None),
        P("col", "vol", None),
    )
    out_specs = (P("vol", None), P("col", "vol", None))
    return jax.shard_map(
        on_device, mesh=mesh, in_specs=in_specs, out_specs=out_specs, check_vma=False
    )
```

```python
import jax
import jax.numpy as jnp
import numpy as np
from jax import lax
from jax.experimental import pallas as pl
from jax.experimental.pallas import tpu as pltpu
from jax.sharding import PartitionSpec as P

ITERS = 10
SWEEPS = 4
LANES = 128
SUB = 8
MIB = 1024 * 1024
DEEP = 2 * SWEEPS
HALO = 32
ROWS = 128
GROUPS = 16
Y_GROUPS = 10
Y_ROWS = 80

BASIS_LOW = 0.1
BASIS_HIGH = 12.0
CONDITION_MAX = 2000.0


def rolled(x, shift, axis):
    return pltpu.roll(x, shift % x.shape[axis], axis)


def column_ring(tiles):
    n = len(tiles)
    lane = lax.broadcasted_iota(jnp.int32, tiles[0].shape, 1)
    first, last = lane == 0, lane == LANES - 1
    return (
        [jnp.where(first, 0.0, rolled(tiles[j], 1, 1)) for j in (n - 2, n - 1)]
        + list(tiles)
        + [jnp.where(last, 0.0, rolled(tiles[j], -1, 1)) for j in (0, 1)]
    )


def row_ring(rows):
    n = len(rows)
    return (
        [rolled(rows[j], 1, 0) for j in (n - 2, n - 1)]
        + list(rows)
        + [rolled(rows[j], -1, 0) for j in (0, 1)]
    )


def mass_line(padded, index):
    i = index + 2
    near = padded[i - 1] + padded[i + 1]
    if index % 2:
        return near + 8.0 * padded[i]
    return (near + 4.0 * padded[i]) - 0.5 * (padded[i - 2] + padded[i + 2])


def both_line(padded, index):
    i = index + 2
    near = padded[i - 1] + padded[i + 1]
    return (16.0 / 3.0 if index % 2 else 11.0 / 3.0) * padded[i] - near


SMEM = pl.BlockSpec(memory_space=pltpu.SMEM)
VMEM = pl.BlockSpec(memory_space=pltpu.VMEM)
HBM = pl.BlockSpec(memory_space=pl.ANY)


def f32(*shape):
    return jax.ShapeDtypeStruct(shape, jnp.float32)


def params(mib):
    return pltpu.CompilerParams(vmem_limit_bytes=mib * MIB)


def cost(us):
    return pl.CostEstimate(flops=0, bytes_accessed=int(us * 100_000), transcendentals=0)


def split(x):
    first = x.astype(jnp.bfloat16)
    return first, (x - first.astype(jnp.float32)).astype(jnp.bfloat16)


def to_blocked(j):
    x = lax.broadcasted_iota(jnp.int32, (1024, 256), 0)
    n = lax.broadcasted_iota(jnp.int32, (1024, 256), 1)
    hit = x == 8 * (n & 127) + j + (n >> 7)
    return jnp.where(hit, 1.0, 0.0).astype(jnp.bfloat16)


def plain_selection():
    k = np.arange(1024)
    out = np.zeros((1024, 1024), np.float32)
    out[k, 8 * (k % LANES) + k // LANES] = 1.0
    return jnp.asarray(out, jnp.bfloat16)


def regroup_kernel(block_ref, metric_ref, before_ref, after_ref, wide_ref, root_ref, parts_ref):
    layers, rows, _ = block_ref.shape
    packed = DEEP * layers
    total = layers * Y_ROWS + ROWS

    def put(at, value):
        first, second = split(value)
        parts_ref[at : at + value.shape[0], :] = first
        parts_ref[total + at : total + at + value.shape[0], :] = second

    for z in range(layers):
        put(Y_ROWS * z, before_ref[DEEP * z : DEEP * (z + 1), :])
        put(Y_ROWS * z + DEEP, block_ref[z])
        put(Y_ROWS * z + DEEP + rows, after_ref[DEEP * z : DEEP * (z + 1), :])
    at = layers * Y_ROWS
    put(at, jnp.sqrt(before_ref[packed:, :]))
    put(at + HALO, jnp.sqrt(metric_ref[...]))
    put(at + HALO + rows, jnp.sqrt(after_ref[packed:, :]))
    for j in range(0, 8, 2):
        pair = jnp.dot(parts_ref[...], to_blocked(j), preferred_element_type=jnp.float32)
        pair = pair[:total] + pair[total:]
        for i in range(2):
            tile = pair[:, LANES * i : LANES * (i + 1)]
            for z in range(layers):
                wide_ref[z, j + i] = tile[Y_ROWS * z : Y_ROWS * (z + 1)]
            root_ref[j + i] = tile[layers * Y_ROWS :]


def regroup(block, metric, before, after):
    layers, rows, cols = block.shape
    return pl.pallas_call(
        regroup_kernel,
        out_shape=(f32(layers, 8, Y_ROWS, LANES), f32(8, ROWS, LANES)),
        in_specs=[VMEM] * 4,
        out_specs=(VMEM, VMEM),
        scratch_shapes=[pltpu.VMEM((2 * (Y_ROWS * layers + ROWS), cols), jnp.bfloat16)],
        compiler_params=params(40),
        cost_estimate=cost(6),
        name="regroup",
    )(block, metric, before, after)


def plain_columns(select_ref, parts, rows, write):
    for q in range(4):
        at = slice(256 * q, 256 * (q + 1))
        value = jnp.dot(parts, select_ref[:, at], preferred_element_type=jnp.float32)
        write(at, value[:rows] + value[rows:])


def face_kernel(
    where_ref, count_ref, area_ref, speed_ref, node_ref, block_ref, metric_ref,
    keep_ref, send_ref, up_ref, down_ref, acc_ref, sems,
):
    slots = area_ref.shape[1]
    layers, rows, _ = block_ref.shape
    copies = []
    for out_ref, row, root_row in ((up_ref, rows - DEEP, rows - HALO), (down_ref, 0, 0)):
        for z in range(layers):
            part = block_ref.at[z, pl.ds(row, DEEP), :]
            copies.append((part, out_ref.at[pl.ds(DEEP * z, DEEP), :]))
        part = metric_ref.at[pl.ds(root_row, HALO), :]
        copies.append((part, out_ref.at[pl.ds(DEEP * layers, HALO), :]))
    copies = [pltpu.make_async_copy(*pair, sems.at[i]) for i, pair in enumerate(copies)]
    for copy in copies:
        copy.start()
    chunk = min(4096, slots)
    core = where_ref[0, 0]
    ids = lax.broadcasted_iota(jnp.int32, (256, chunk), 0)
    ids = ids.astype(jnp.float32).astype(jnp.bfloat16)
    zero = jnp.zeros((), jnp.bfloat16)
    one = jnp.ones((), jnp.bfloat16)
    contract = (((1,), (1,)), ((), ()))
    acc_ref[...] = jnp.zeros_like(acc_ref)

    def wide(x):
        return jnp.broadcast_to(x.astype(jnp.bfloat16), (256, chunk))

    def body(step, carry):
        at = pl.ds(pl.multiple_of(step * chunk, chunk), chunk)
        slot = lax.broadcasted_iota(jnp.int32, (1, chunk), 1) + step * chunk
        value = jnp.where(slot < count_ref[0, 0], area_ref[:, at] * speed_ref[:, at], 0.0)
        node = node_ref[:, at]
        low = (((node & 1) << 7) + ((node >> 3) & 127)).astype(jnp.float32)
        high = (((node >> 1) & 3) * 64 + (node >> 10)).astype(jnp.float32)
        first = value.astype(jnp.bfloat16)
        second = value - first.astype(jnp.float32)
        here = wide(high) == ids
        upper = jnp.where(here, wide(first), zero)
        lower = jnp.where(here, wide(second), zero)
        columns = jnp.where(wide(low) == ids, one, zero)
        both = jnp.concatenate([upper, lower], axis=0)
        acc_ref[...] += lax.dot_general(both, columns, contract, preferred_element_type=jnp.float32)
        return carry

    lax.fori_loop(0, slots // chunk, body, 0)
    for j in range(8):
        at, lanes = 64 * (j // 2), slice(LANES * (j % 2), LANES * (j % 2 + 1))
        near, far = at + 32 * core, at + 32 - 32 * core
        keep_ref[j] = acc_ref[pl.ds(near, 32), lanes] + acc_ref[pl.ds(256 + near, 32), lanes]
        send_ref[j] = acc_ref[pl.ds(far, 32), lanes] + acc_ref[pl.ds(256 + far, 32), lanes]
    for copy in copies:
        copy.wait()


def face_sums(where, count, area, speed, node, block, metric):
    half = f32(8, 32, LANES)
    layers, _, cols = block.shape
    rows = f32(DEEP * layers + HALO, cols)
    return pl.pallas_call(
        face_kernel,
        out_shape=(half, half, rows, rows),
        in_specs=[SMEM, SMEM, VMEM, VMEM, VMEM, HBM, HBM],
        out_specs=(VMEM, VMEM, VMEM, VMEM),
        scratch_shapes=[
            pltpu.VMEM((512, 256), jnp.float32),
            pltpu.SemaphoreType.DMA((2 * layers + 2,)),
        ],
        compiler_params=params(58),
        cost_estimate=cost(7),
        name="face_sums",
    )(where, count, area, speed, node, block, metric)


def basis_kernel(
    where_ref, own_ref, other_ref, same_ref, cross_ref, root_ref,
    basis_ref, sums_ref, rows, field, root, outer, line, partial, sems,
):
    core = where_ref[0, 0]
    centre = (BASIS_LOW + BASIS_HIGH) / 2
    scale = 2 / (BASIS_HIGH - BASIS_LOW)
    for t in range(8):
        rows[t, pl.ds(32 + 32 * core, 32), :] = own_ref[t]
        rows[t, pl.ds(64 - 32 * core, 32), :] = other_ref[t]
        rows[t, pl.ds(96 * core, 32), :] = cross_ref[t]
        rows[t, pl.ds(96 - 96 * core, 32), :] = same_ref[t]
    for t in range(8):
        for ys in range(GROUPS):
            field[0, t, ys] = rows[t, pl.ds(ys, SUB, stride=GROUPS), :]
            value = root_ref[t, pl.ds(ys, SUB, stride=GROUPS), :]
            root[t, ys] = value
            outer[t, ys] = value * (2 * scale * 4.0 / 225.0)

    group = lax.broadcasted_iota(jnp.int32, (SUB, LANES), 0)
    own_rows = jnp.where((group >= 2) & (group < 6), 1.0, 0.0).astype(jnp.float32)

    def out_copy(k):
        return pltpu.make_async_copy(field.at[k], basis_ref.at[k], sems.at[k])

    def step(k, begin):
        out_copy(k).start()
        for ys in range(GROUPS):
            padded = column_ring([field[k, t, ys] * root[t, ys] for t in range(8)])
            for t in range(8):
                line[ys, t] = mass_line(padded, t)
        squares, shifts = [], []
        for t in range(8):
            square = jnp.zeros((SUB, LANES), jnp.float32)
            shifted = jnp.zeros((SUB, LANES), jnp.float32)
            padded = row_ring([line[ys, t] for ys in range(GROUPS)])
            for ys in range(GROUPS):
                now = field[k, t, ys]
                later = outer[t, ys] * mass_line(padded, ys) - (2 * centre * scale) * now
                later = 0.5 * later if begin else later - field[k - 1, t, ys]
                field[k + 1, t, ys] = later
                square = square + now * now
                shifted = shifted + later * now
            squares.append(square)
            shifts.append(shifted)

        def add(parts):
            while len(parts) > 1:
                parts = [parts[i] + parts[i + 1] for i in range(0, len(parts), 2)]
            return jnp.sum(parts[0] * own_rows, axis=0, keepdims=True)

        partial[pl.ds(2 * k, 1), :] = add(squares)
        partial[pl.ds(2 * k + 1, 1), :] = add(shifts)

    def later_step(k, carry):
        step(k, False)
        return carry

    partial[...] = jnp.zeros_like(partial)
    step(0, True)
    lax.fori_loop(1, ITERS, later_step, 0)
    whole = jnp.sum(partial[...], axis=1, keepdims=True)
    row = lax.broadcasted_iota(jnp.int32, partial.shape, 0)
    lane = lax.broadcasted_iota(jnp.int32, partial.shape, 1)
    line_of = jnp.sum(jnp.where(row == lane, whole, 0.0), axis=0, keepdims=True)
    sums_ref[...] = jnp.broadcast_to(line_of, sums_ref.shape)
    for k in range(ITERS):
        out_copy(k).wait()


def surface_basis(where, own, other, same, cross, root):
    return pl.pallas_call(
        basis_kernel,
        out_shape=(f32(ITERS, 8, GROUPS, SUB, LANES), f32(SUB, LANES)),
        in_specs=[SMEM] + [VMEM] * 5,
        out_specs=(HBM, VMEM),
        scratch_shapes=[
            pltpu.VMEM((8, ROWS, LANES), jnp.float32),
            pltpu.VMEM((ITERS + 1, 8, GROUPS, SUB, LANES), jnp.float32),
            pltpu.VMEM((8, GROUPS, SUB, LANES), jnp.float32),
            pltpu.VMEM((8, GROUPS, SUB, LANES), jnp.float32),
            pltpu.VMEM((GROUPS, 8, SUB, LANES), jnp.float32),
            pltpu.VMEM((24, LANES), jnp.float32),
            pltpu.SemaphoreType.DMA((ITERS,)),
        ],
        compiler_params=params(58),
        cost_estimate=cost(7),
        name="surface_basis",
    )(where, own, other, same, cross, root)


def solve_weights():
    n = ITERS
    moment = np.zeros((2 * n, 2 * n))
    for m in range(2 * n):
        if m < 2:
            moment[m, m] = 1.0
        else:
            moment[m, m] = 2.0
            moment[m, m % 2] = -1.0
    centre, half = (BASIS_LOW + BASIS_HIGH) / 2, (BASIS_HIGH - BASIS_LOW) / 2
    weights = np.zeros((2 * n, 16, LANES))
    for i in range(n):
        for j in range(n):
            lower = abs(j - 1)
            for factor, index in (
                (centre / 2, i + j),
                (centre / 2, abs(i - j)),
                (half / 4, i + j + 1),
                (half / 4, abs(i - j - 1)),
                (half / 4, i + lower),
                (half / 4, abs(i - lower)),
            ):
                weights[:, i, j] += factor * moment[index]
        weights[:, i, n] += moment[i]
    return weights.astype(np.float32)


def solve_kernel(basis_ref, sums_ref, weights_ref, out_ref, flag_ref, part_ref, rows, sem):
    n = ITERS
    copy = pltpu.make_async_copy(basis_ref, part_ref, sem)
    copy.start()
    total = sums_ref[0]
    for i in range(1, sums_ref.shape[0]):
        total = total + sums_ref[i]
    row = lax.broadcasted_iota(jnp.int32, (16, LANES), 0)
    lane = lax.broadcasted_iota(jnp.int32, (16, LANES), 1)
    system = jnp.where((lane == row + 16) & (row < n), 1.0, 0.0).astype(jnp.float32)
    for m in range(2 * n):
        system = system + weights_ref[m] * total[0:1, m : m + 1]
    centre = jnp.sum(jnp.where(lane == row, system, 0.0), axis=1, keepdims=True)
    for k in range(n):
        pivot_row = system[k : k + 1, :] / system[k : k + 1, k : k + 1]
        column = system[:, k : k + 1]
        system = jnp.where(row == k, pivot_row, system - column * pivot_row)
    inverse = jnp.sum(jnp.where(lane == row + 16, system, 0.0), axis=1, keepdims=True)
    figure = jnp.broadcast_to(centre * inverse, (16, LANES))
    inside = (row < n) & (lane == 0)
    least = jnp.min(jnp.where(inside, figure, 1.0))
    whole = jnp.sum(jnp.where(inside, figure, 0.0))
    flag_ref[0, 0] = jnp.where((least > 0.5) & (whole < CONDITION_MAX), 1, 0).astype(jnp.int32)
    copy.wait()
    weights = [jnp.broadcast_to(system[k : k + 1, n : n + 1], (SUB, LANES)) for k in range(n)]
    for t in range(8):
        for ys in range(GROUPS):
            value = weights[0] * part_ref[0, t, ys]
            for k in range(1, n):
                value = value + weights[k] * part_ref[k, t, ys]
            rows[t, pl.ds(ys, SUB, stride=GROUPS), :] = value
        out_ref[t] = rows[t, HALO - DEEP : HALO - DEEP + Y_ROWS, :]


def surface_solve(basis, sums):
    return pl.pallas_call(
        solve_kernel,
        out_shape=(f32(8, Y_ROWS, LANES), jax.ShapeDtypeStruct((1, 1), jnp.int32)),
        in_specs=[HBM, VMEM, VMEM],
        out_specs=(VMEM, SMEM),
        scratch_shapes=[
            pltpu.VMEM(basis.shape, jnp.float32),
            pltpu.VMEM((8, ROWS, LANES), jnp.float32),
            pltpu.SemaphoreType.DMA,
        ],
        compiler_params=params(58),
        cost_estimate=cost(3),
        name="surface_solve",
    )(basis, sums, jnp.asarray(solve_weights()))


def fill_factors(factor, where_ref, rows):
    vol, vols = where_ref[0, 3], where_ref[0, 4]
    group = lax.broadcasted_iota(jnp.int32, (SUB, LANES), 0)
    mass, stiff = (8.0, 16.0), (14.0, 16.0)
    for ys in range(Y_GROUPS):
        row = group * Y_GROUPS + ys
        outside = ((vol == 0) & (row < DEEP)) | ((vol == vols - 1) & (row >= DEEP + rows))
        py = ys % 2
        for pz in range(2):
            for px in range(2):
                value = -12.0 / (
                    stiff[pz] * mass[py] * mass[px]
                    + mass[pz] * (stiff[py] * mass[px] + mass[py] * stiff[px])
                )
                factor[pz, px, ys] = jnp.where(outside, 0.0, jnp.float32(value))


def lateral_lines(get, line_a, line_b, put):
    for ys in range(Y_GROUPS):
        padded = column_ring([get(t, ys) for t in range(8)])
        for t in range(8):
            m = mass_line(padded, t)
            line_a[t, ys] = m
            line_b[t, ys] = both_line(padded, t) - m
    for t in range(8):
        a = row_ring([line_a[t, ys] for ys in range(Y_GROUPS)])
        b = row_ring([line_b[t, ys] for ys in range(Y_GROUPS)])
        for ys in range(Y_GROUPS):
            put(t, ys, mass_line(a, ys), both_line(a, ys) + mass_line(b, ys))


def pair_steps(w, c):
    near = c[1] + c[3]
    even = (11.0 / 3.0 * w[1] - (w[0] + w[2])) + ((near + 4.0 * c[2]) - 0.5 * (c[0] + c[4]))
    near = c[2] + c[4]
    odd = (16.0 / 3.0 * w[2] - (w[1] + w[3])) + (near + 8.0 * c[3])
    return even, odd


def strided(ys):
    return pl.ds(ys, SUB, stride=Y_GROUPS)


def change_kernel(
    where_ref, speed_ref, out_ref, cells, along, cross, line_a, line_b, factor, plain, sem,
):
    col = where_ref[0, 1]
    layers, _, rows, _ = out_ref.shape

    def lateral(z, carry):
        def put(t, ys, w, c):
            along[z, t, ys] = w
            cross[z, t, ys] = c

        lateral_lines(lambda t, ys: cells[z, t, ys], line_a, line_b, put)
        return carry

    def set_top():
        for t in range(8):
            for ys in range(Y_GROUPS):
                cells[2, t, ys] = 0.5 * speed_ref[t, strided(ys), :]

    def send(count):
        for z in range(count):
            for t in range(8):
                for ys in range(Y_GROUPS):
                    plain[z, t, strided(ys), :] = cells[z + 2, t, ys]
        copy = pltpu.make_async_copy(
            plain.at[pl.ds(0, count), :, pl.ds(DEEP, rows), :], out_ref.at[pl.ds(0, count)], sem
        )
        copy.start()
        copy.wait()

    @pl.when(col == 0)
    def _():
        fill_factors(factor, where_ref, rows)
        set_top()
        clear = jnp.zeros((8, Y_GROUPS, SUB, LANES), jnp.float32)
        for z in range(layers + 3):
            if z != 2:
                cross[z] = clear
                if z:
                    along[z] = clear
        for z in range(3, layers + 2):
            cells[z] = clear

        def update(pair, carry):
            z = 2 * pair + 2
            for ys in range(Y_GROUPS):
                factors = [[factor[pz, px, ys] for px in range(2)] for pz in range(2)]
                for t in range(8):
                    even, odd = pair_steps(
                        [along[z + i, t, ys] for i in range(-1, 3)],
                        [cross[z + i, t, ys] for i in range(-2, 3)],
                    )
                    cells[z, t, ys] += factors[0][t % 2] * even
                    cells[z + 1, t, ys] += factors[1][t % 2] * odd
            return carry

        def one_sweep(sweep, carry):
            lax.fori_loop(2, 2 * sweep + 3, lateral, 0)
            lax.fori_loop(0, jnp.minimum(sweep + 2, layers // 2), update, 0)
            set_top()
            return carry

        lax.fori_loop(0, SWEEPS, one_sweep, 0)
        send(layers)

    @pl.when(col == 1)
    def _():
        fill_factors(factor, where_ref, rows)
        set_top()

        def one_sweep(sweep, carry):
            lateral(2, 0)
            for t in range(8):
                for ys in range(Y_GROUPS):
                    cells[2, t, ys] = factor[0, t % 2, ys] * (-0.5 * cross[2, t, ys])
            return carry

        lax.fori_loop(0, SWEEPS, one_sweep, 0)
        send(1)


def surface_change(where, speed, layers, rows):
    work = pltpu.VMEM((layers + 4, 8, Y_GROUPS, SUB, LANES), jnp.float32)
    line = pltpu.VMEM((8, Y_GROUPS, SUB, LANES), jnp.float32)
    return pl.pallas_call(
        change_kernel,
        out_shape=f32(layers, 8, rows, LANES),
        in_specs=[SMEM, VMEM],
        out_specs=HBM,
        scratch_shapes=[
            pltpu.VMEM((layers + 2, 8, Y_GROUPS, SUB, LANES), jnp.float32),
            work, work, line, line,
            pltpu.VMEM((2, 2, Y_GROUPS, SUB, LANES), jnp.float32),
            pltpu.VMEM((layers, 8, Y_ROWS, LANES), jnp.float32),
            pltpu.SemaphoreType.DMA,
        ],
        compiler_params=params(58),
        cost_estimate=cost(8),
        name="surface_change",
    )(where, speed)


def base_kernel(
    where_ref, wide_ref, zlow_ref, zhigh_ref, change_ref, speed_ref, select_ref,
    velocity_ref, out_ref, field, along, cross, line_a, line_b, factor, change, parts, sems,
):
    col, cols = where_ref[0, 1], where_ref[0, 2]
    layers, _, rows, _ = change_ref.shape
    total = layers + 2 * DEEP
    own = pltpu.make_async_copy(wide_ref, field.at[pl.ds(DEEP, layers)], sems.at[0])
    low = pltpu.make_async_copy(zlow_ref, field.at[pl.ds(0, DEEP)], sems.at[1])
    high = pltpu.make_async_copy(zhigh_ref, field.at[pl.ds(DEEP + layers, DEEP)], sems.at[2])
    all_change = pltpu.make_async_copy(change_ref, change, sems.at[3])
    one_change = pltpu.make_async_copy(
        change_ref.at[pl.ds(0, 1)], change.at[pl.ds(0, 1)], sems.at[4]
    )
    own.start()
    low.start()
    high.start()
    pl.when(col == 0)(all_change.start)
    pl.when(col == 1)(one_change.start)
    fill_factors(factor, where_ref, rows)
    count = (layers + 1) * rows

    def cut(value, at, t):
        first, second = split(value)
        lanes = slice(LANES * t, LANES * (t + 1))
        parts[at : at + rows, lanes] = first
        parts[count + at : count + at + rows, lanes] = second

    for t in range(8):
        cut(speed_ref[t, DEEP : DEEP + rows, :], 0, t)

    def lateral(z, carry):
        def put(t, ys, w, c):
            along[z, t, ys] = w
            cross[z, t, ys] = c

        lateral_lines(lambda t, ys: field[z, t, strided(ys), :], line_a, line_b, put)
        return carry

    def update(pair, carry):
        z = 2 * pair
        for ys in range(Y_GROUPS):
            factors = [[factor[pz, px, ys] for px in range(2)] for pz in range(2)]
            for t in range(8):
                even, odd = pair_steps(
                    [along[z + i, t, ys] for i in range(-1, 3)], [cross[z + i, t, ys] for i in range(-2, 3)]
                )
                scale = jnp.where((col == 0) & (z == DEEP), 0.0, factors[0][t % 2])
                even = field[z, t, strided(ys), :] + scale * even
                odd = field[z + 1, t, strided(ys), :] + factors[1][t % 2] * odd
                field[z, t, strided(ys), :] = even
                field[z + 1, t, strided(ys), :] = odd
        return carry

    begin = jnp.where(col == 0, DEEP, 0)
    end = jnp.where(col == cols - 1, DEEP + layers + 1, total - 1)

    def one_sweep(sweep, carry):
        first = jnp.maximum(begin, 2 * sweep)
        last = jnp.minimum(end, total - 2 * sweep - 1)

        @pl.when(sweep == 0)
        def _():
            own.wait()

        lax.fori_loop(jnp.where(sweep == 0, DEEP, first), jnp.where(sweep == 0, DEEP + layers, last), lateral, 0)

        @pl.when(sweep == 0)
        def _():
            low.wait()
            high.wait()

        lax.fori_loop(jnp.where(sweep == 0, first, DEEP), DEEP, lateral, 0)
        lax.fori_loop(jnp.where(sweep == 0, DEEP + layers, last), last, lateral, 0)
        low_pair = jnp.where(col == 0, DEEP // 2, sweep + 1)
        high_pair = jnp.where(col == cols - 1, (DEEP + layers) // 2, total // 2 - sweep - 1)
        lax.fori_loop(low_pair, high_pair, update, 0)
        return carry

    @pl.when(col == 0)
    def _():
        clear = jnp.zeros((8, Y_GROUPS, SUB, LANES), jnp.float32)
        for z in (DEEP - 2, DEEP - 1):
            along[z] = clear
            cross[z] = clear

    lax.fori_loop(0, SWEEPS, one_sweep, 0)

    @pl.when(col == 0)
    def _():
        all_change.wait()
        for z in range(layers):
            for t in range(8):
                field[DEEP + z, t, DEEP : DEEP + rows, :] += change[z, t]

    @pl.when(col == 1)
    def _():
        one_change.wait()
        for t in range(8):
            field[DEEP, t, DEEP : DEEP + rows, :] += change[0, t]

    for z in range(layers):
        for t in range(8):
            cut(field[DEEP + z, t, DEEP : DEEP + rows, :], rows * (z + 1), t)

    def write(at, value):
        velocity_ref[:, at] = value[:rows]
        out_ref[:, :, at] = value[rows:].reshape(layers, rows, 256)

    plain_columns(select_ref, parts[...], count, write)


def base_sweeps(where, wide, zlow, zhigh, change, speed, select):
    layers, _, rows, _ = change.shape
    total = layers + 2 * DEEP
    work = pltpu.VMEM((total, 8, Y_GROUPS, SUB, LANES), jnp.float32)
    line = pltpu.VMEM((8, Y_GROUPS, SUB, LANES), jnp.float32)
    return pl.pallas_call(
        base_kernel,
        out_shape=(f32(rows, 8 * LANES), f32(layers, rows, 8 * LANES)),
        in_specs=[SMEM] + [HBM] * 4 + [VMEM] * 2,
        out_specs=(VMEM, VMEM),
        scratch_shapes=[
            pltpu.VMEM((total, 8, Y_ROWS, LANES), jnp.float32),
            work, work, line, line,
            pltpu.VMEM((2, 2, Y_GROUPS, SUB, LANES), jnp.float32),
            pltpu.VMEM((layers, 8, rows, LANES), jnp.float32),
            pltpu.VMEM((2 * (layers + 1) * rows, 8 * LANES), jnp.bfloat16),
            pltpu.SemaphoreType.DMA((5,)),
        ],
        compiler_params=params(58),
        cost_estimate=cost(25),
        name="base_sweeps",
    )(where, wide, zlow, zhigh, change, speed, select)


mass_even = (-1.0 / 15.0, 2.0 / 15.0, 8.0 / 15.0, 2.0 / 15.0, -1.0 / 15.0)
mass_odd = (0.0, 2.0 / 15.0, 16.0 / 15.0, 2.0 / 15.0, 0.0)


def mass_along(padded, axis):
    count = padded.shape[axis] - 4
    pieces = [lax.slice_in_dim(padded, i, i + count, axis=axis) for i in range(5)]
    even = sum(mass_even[i] * pieces[i] for i in range(5))
    odd = sum(mass_odd[i] * pieces[i] for i in range(1, 4))
    at_even = lax.broadcasted_iota(jnp.int32, even.shape, axis) % 2 == 0
    return jnp.where(at_even, even, odd)


def with_rows(x, width):
    size = lax.axis_size("vol")
    up = [(i, i + 1) for i in range(size - 1)]
    down = [(j, i) for i, j in up]
    before = lax.ppermute(x[-width:], "vol", up)
    after = lax.ppermute(x[:width], "vol", down)
    return jnp.concatenate([before, x, after], axis=0)


def stepwise(flux, metric):
    root = jnp.sqrt(metric)

    def dot(a, b):
        return lax.psum(jnp.sum(a * b), "vol")

    def step(_, state):
        solved, residual, direction, norm = state
        padded = jnp.pad(with_rows(root * direction, 2), ((0, 0), (2, 2)))
        image = root * mass_along(mass_along(padded, 1), 0)
        alpha = norm / dot(direction, image)
        solved = solved + alpha * direction
        residual = residual - alpha * image
        after = dot(residual, residual)
        direction = residual + after / norm * direction
        return solved, residual, direction, after

    state = (jnp.zeros_like(flux), flux, flux, dot(flux, flux))
    return with_rows(lax.fori_loop(0, ITERS, step, state)[0], DEEP)


def after(x, *others):
    return lax.optimization_barrier((x,) + others)[0]


def on_device(face_area, face_speed, face_node, face_count, surface_metric, displacement):
    vols, cols = lax.axis_size("vol"), lax.axis_size("col")
    vol, col = lax.axis_index("vol"), lax.axis_index("col")
    core = col % 2
    where = jnp.stack([core, col, jnp.int32(cols), vol, jnp.int32(vols)]).astype(jnp.int32).reshape(1, 5)
    up = [(i, i + 1) for i in range(vols - 1)]
    down = [(j, i) for i, j in up]
    col_up = [(i, i + 1) for i in range(cols - 1)]
    col_down = [(j, i) for i, j in col_up]
    packed = displacement.shape[0] * DEEP

    select = plain_selection()

    def moved(x, steps):
        dv, dc = steps
        pairs = [
            (i * cols + j, (i + dv) * cols + j + dc)
            for i in range(vols)
            for j in range(cols)
            if 0 <= i + dv < vols and 0 <= j + dc < cols
        ]
        return lax.ppermute(x, ("vol", "col"), pairs)

    keep, send, rows_up, rows_down = face_sums(
        where, face_count, face_area, face_speed, face_node, displacement, surface_metric
    )
    with jax.named_scope("flux_sum"):
        keep = keep + lax.ppermute(send, "col", [(j, j ^ 1) for j in range(cols)])
        turned = [
            lax.ppermute(keep, "col", [(j, (j + 2 * k) % cols) for j in range(cols)]) for k in (1, 2, 3)
        ]
        own = (keep + turned[1]) + (turned[0] + turned[2])
    with jax.named_scope("row_halo"):
        rows_before, rows_after = moved(rows_up, (1, 0)), moved(rows_down, (-1, 0))
    wide, root = regroup(displacement, surface_metric, rows_before, rows_after)
    own = after(own, wide)
    with jax.named_scope("flux_halo"):
        other = lax.ppermute(own, "col", [(j, j ^ 1) for j in range(cols)])
        same_pairs, cross_pairs = [], []
        for i in range(vols):
            for j in range(cols):
                to = i - 1 if j % 2 == 0 else i + 1
                if 0 <= to < vols:
                    same_pairs.append((i * cols + j, to * cols + j))
                    cross_pairs.append((i * cols + j, to * cols + (j ^ 1)))
        same = lax.ppermute(own, ("vol", "col"), same_pairs)
        cross = lax.ppermute(own, ("vol", "col"), cross_pairs)

    with jax.named_scope("depth_halo"):
        sent = after(wide, own)
        zlow, zhigh = moved(sent, (0, 1)), moved(sent, (0, -1))
    basis, sums = surface_basis(where, own, other, same, cross, root)
    with jax.named_scope("gather_sums"):
        spread = jnp.broadcast_to(sums[None], (vols,) + sums.shape)
        gathered = lax.all_to_all(spread, "vol", 0, 0)
    speed, flag = surface_solve(basis, gathered)

    def finish(speed):
        change = surface_change(where, speed, displacement.shape[0], displacement.shape[1])
        return base_sweeps(where, wide, zlow, zhigh, change, speed, select)

    def step_by_step():
        low = jnp.where(core == 0, own, other)
        high = jnp.where(core == 0, other, own)
        flux = jnp.concatenate([low, high], axis=1)
        flux = flux.transpose(1, 2, 0).reshape(surface_metric.shape)
        solved = stepwise(flux, surface_metric)
        return finish(solved.reshape(Y_ROWS, LANES, 8).transpose(2, 0, 1))

    return lax.cond(flag[0, 0] > 0, lambda: finish(speed), step_by_step)


def solution(mesh):
    in_specs = (
        P("vol", "col"),
        P("vol", "col"),
        P("vol", "col"),
        P("vol", "col"),
        P("vol", None),
        P("col", "vol", None),
    )
    out_specs = (P("vol", None), P("col", "vol", None))
    return jax.shard_map(
        on_device, mesh=mesh, in_specs=in_specs, out_specs=out_specs, check_vma=False
    )
```

```python
import jax
import jax.numpy as jnp
import numpy as np
from jax import lax
from jax.experimental import pallas as pl
from jax.experimental.pallas import tpu as pltpu
from jax.sharding import PartitionSpec as P

ITERS = 10
SWEEPS = 4
LANES = 128
SUB = 8
MIB = 1024 * 1024
DEEP = 2 * SWEEPS
HALO = 32
ROWS = 128
GROUPS = 16
Y_GROUPS = 10
Y_ROWS = 80

BASIS_LOW = 0.1
BASIS_HIGH = 12.0
CONDITION_MAX = 2000.0


def rolled(x, shift, axis):
    return pltpu.roll(x, shift % x.shape[axis], axis)


def column_ring(tiles):
    n = len(tiles)
    lane = lax.broadcasted_iota(jnp.int32, tiles[0].shape, 1)
    first, last = lane == 0, lane == LANES - 1
    return (
        [jnp.where(first, 0.0, rolled(tiles[j], 1, 1)) for j in (n - 2, n - 1)]
        + list(tiles)
        + [jnp.where(last, 0.0, rolled(tiles[j], -1, 1)) for j in (0, 1)]
    )


def row_ring(rows):
    n = len(rows)
    return (
        [rolled(rows[j], 1, 0) for j in (n - 2, n - 1)]
        + list(rows)
        + [rolled(rows[j], -1, 0) for j in (0, 1)]
    )


def mass_line(padded, index):
    i = index + 2
    near = padded[i - 1] + padded[i + 1]
    if index % 2:
        return near + 8.0 * padded[i]
    return (near + 4.0 * padded[i]) - 0.5 * (padded[i - 2] + padded[i + 2])


def both_line(padded, index):
    i = index + 2
    near = padded[i - 1] + padded[i + 1]
    return (16.0 / 3.0 if index % 2 else 11.0 / 3.0) * padded[i] - near


SMEM = pl.BlockSpec(memory_space=pltpu.SMEM)
VMEM = pl.BlockSpec(memory_space=pltpu.VMEM)
HBM = pl.BlockSpec(memory_space=pltpu.HBM)


def f32(*shape):
    return jax.ShapeDtypeStruct(shape, jnp.float32)


def params(mib):
    return pltpu.CompilerParams(vmem_limit_bytes=mib * MIB)


def cost(us):
    return pl.CostEstimate(flops=0, bytes_accessed=int(us * 100_000), transcendentals=0)


def split(x):
    first = x.astype(jnp.bfloat16)
    return first, (x - first.astype(jnp.float32)).astype(jnp.bfloat16)


def to_blocked(j):
    x = lax.broadcasted_iota(jnp.int32, (1024, 256), 0)
    n = lax.broadcasted_iota(jnp.int32, (1024, 256), 1)
    hit = x == 8 * (n & 127) + j + (n >> 7)
    return jnp.where(hit, 1.0, 0.0).astype(jnp.bfloat16)


def plain_selection():
    k = np.arange(1024)
    out = np.zeros((1024, 1024), np.float32)
    out[k, 8 * (k % LANES) + k // LANES] = 1.0
    return jnp.asarray(out, jnp.bfloat16)


def regroup_kernel(block_ref, metric_ref, before_ref, after_ref, wide_ref, root_ref, parts_ref):
    layers, rows, _ = block_ref.shape
    packed = DEEP * layers
    total = layers * Y_ROWS + ROWS

    def put(at, value):
        first, second = split(value)
        parts_ref[at : at + value.shape[0], :] = first
        parts_ref[total + at : total + at + value.shape[0], :] = second

    for z in range(layers):
        put(Y_ROWS * z, before_ref[DEEP * z : DEEP * (z + 1), :])
        put(Y_ROWS * z + DEEP, block_ref[z])
        put(Y_ROWS * z + DEEP + rows, after_ref[DEEP * z : DEEP * (z + 1), :])
    at = layers * Y_ROWS
    put(at, jnp.sqrt(before_ref[packed:, :]))
    put(at + HALO, jnp.sqrt(metric_ref[...]))
    put(at + HALO + rows, jnp.sqrt(after_ref[packed:, :]))
    for j in range(0, 8, 2):
        pair = jnp.dot(parts_ref[...], to_blocked(j), preferred_element_type=jnp.float32)
        pair = pair[:total] + pair[total:]
        for i in range(2):
            tile = pair[:, LANES * i : LANES * (i + 1)]
            for z in range(layers):
                wide_ref[z, j + i] = tile[Y_ROWS * z : Y_ROWS * (z + 1)]
            root_ref[j + i] = tile[layers * Y_ROWS :]


def regroup(block, metric, before, after):
    layers, rows, cols = block.shape
    return pl.pallas_call(
        regroup_kernel,
        out_shape=(f32(layers, 8, Y_ROWS, LANES), f32(8, ROWS, LANES)),
        in_specs=[VMEM] * 4,
        out_specs=(VMEM, VMEM),
        scratch_shapes=[pltpu.VMEM((2 * (Y_ROWS * layers + ROWS), cols), jnp.bfloat16)],
        compiler_params=params(32),
        cost_estimate=cost(6),
        name="regroup",
    )(block, metric, before, after)


def plain_columns(select_ref, parts, rows, write):
    for q in range(4):
        at = slice(256 * q, 256 * (q + 1))
        value = jnp.dot(parts, select_ref[:, at], preferred_element_type=jnp.float32)
        write(at, value[:rows] + value[rows:])


def face_kernel(
    where_ref, count_ref, area_ref, speed_ref, node_ref, block_ref, metric_ref,
    keep_ref, send_ref, up_ref, down_ref, area, speed, nodes, acc_ref, sems,
):
    slots = area_ref.shape[1]
    fetches = [
        pltpu.make_async_copy(source, target, sems.at[i])
        for i, (source, target) in enumerate(((area_ref, area), (speed_ref, speed), (node_ref, nodes)))
    ]
    for fetch in fetches:
        fetch.start()
    layers, rows, _ = block_ref.shape
    copies = []
    for out_ref, row, root_row in ((up_ref, rows - DEEP, rows - HALO), (down_ref, 0, 0)):
        for z in range(layers):
            part = block_ref.at[z, pl.ds(row, DEEP), :]
            copies.append((part, out_ref.at[pl.ds(DEEP * z, DEEP), :]))
        part = metric_ref.at[pl.ds(root_row, HALO), :]
        copies.append((part, out_ref.at[pl.ds(DEEP * layers, HALO), :]))
    copies = [pltpu.make_async_copy(*pair, sems.at[i + 3]) for i, pair in enumerate(copies)]
    for copy in copies:
        copy.start()
    chunk = min(4096, slots)
    core = where_ref[0, 0]
    ids = lax.broadcasted_iota(jnp.int32, (256, chunk), 0)
    ids = ids.astype(jnp.float32).astype(jnp.bfloat16)
    zero = jnp.zeros((), jnp.bfloat16)
    one = jnp.ones((), jnp.bfloat16)
    contract = (((1,), (1,)), ((), ()))
    acc_ref[...] = jnp.zeros_like(acc_ref)
    for fetch in fetches:
        fetch.wait()

    def wide(x):
        return jnp.broadcast_to(x.astype(jnp.bfloat16), (256, chunk))

    def body(step, carry):
        at = pl.ds(pl.multiple_of(step * chunk, chunk), chunk)
        slot = lax.broadcasted_iota(jnp.int32, (1, chunk), 1) + step * chunk
        value = jnp.where(slot < count_ref[0, 0], area[:, at] * speed[:, at], 0.0)
        node = nodes[:, at]
        low = (((node & 1) << 7) + ((node >> 3) & 127)).astype(jnp.float32)
        high = (((node >> 1) & 3) * 64 + (node >> 10)).astype(jnp.float32)
        first = value.astype(jnp.bfloat16)
        second = value - first.astype(jnp.float32)
        here = wide(high) == ids
        upper = jnp.where(here, wide(first), zero)
        lower = jnp.where(here, wide(second), zero)
        columns = jnp.where(wide(low) == ids, one, zero)
        both = jnp.concatenate([upper, lower], axis=0)
        acc_ref[...] += lax.dot_general(both, columns, contract, preferred_element_type=jnp.float32)
        return carry

    lax.fori_loop(0, slots // chunk, body, 0)
    for j in range(8):
        at, lanes = 64 * (j // 2), slice(LANES * (j % 2), LANES * (j % 2 + 1))
        near, far = at + 32 * core, at + 32 - 32 * core
        keep_ref[j] = acc_ref[pl.ds(near, 32), lanes] + acc_ref[pl.ds(256 + near, 32), lanes]
        send_ref[j] = acc_ref[pl.ds(far, 32), lanes] + acc_ref[pl.ds(256 + far, 32), lanes]
    for copy in copies:
        copy.wait()


def face_sums(where, count, area, speed, node, block, metric):
    half = f32(8, 32, LANES)
    layers, _, cols = block.shape
    rows = f32(DEEP * layers + HALO, cols)
    return pl.pallas_call(
        face_kernel,
        out_shape=(half, half, rows, rows),
        in_specs=[SMEM, SMEM] + [HBM] * 5,
        out_specs=(VMEM, VMEM, VMEM, VMEM),
        scratch_shapes=[
            pltpu.VMEM(area.shape, jnp.float32),
            pltpu.VMEM(area.shape, jnp.float32),
            pltpu.VMEM(area.shape, jnp.int32),
            pltpu.VMEM((512, 256), jnp.float32),
            pltpu.SemaphoreType.DMA((2 * layers + 5,)),
        ],
        compiler_params=params(56),
        cost_estimate=cost(7),
        name="face_sums",
    )(where, count, area, speed, node, block, metric)


def basis_kernel(
    where_ref, own_ref, other_ref, same_ref, cross_ref, root_ref,
    field, sums_ref, rows, root, outer, line, partial,
):
    core = where_ref[0, 0]
    centre = (BASIS_LOW + BASIS_HIGH) / 2
    scale = 2 / (BASIS_HIGH - BASIS_LOW)
    for t in range(8):
        rows[t, pl.ds(32 + 32 * core, 32), :] = own_ref[t]
        rows[t, pl.ds(64 - 32 * core, 32), :] = other_ref[t]
        rows[t, pl.ds(96 * core, 32), :] = cross_ref[t]
        rows[t, pl.ds(96 - 96 * core, 32), :] = same_ref[t]
    for t in range(8):
        for ys in range(GROUPS):
            field[0, t, ys] = rows[t, pl.ds(ys, SUB, stride=GROUPS), :]
            value = root_ref[t, pl.ds(ys, SUB, stride=GROUPS), :]
            root[t, ys] = value
            outer[t, ys] = value * (2 * scale * 4.0 / 225.0)

    group = lax.broadcasted_iota(jnp.int32, (SUB, LANES), 0)
    own_rows = jnp.where((group >= 2) & (group < 6), 1.0, 0.0).astype(jnp.float32)

    def step(k, begin, end):
        def put(k, t, ys, value):
            if not end:
                field[k, t, ys] = value

        for ys in range(GROUPS):
            padded = column_ring([field[k, t, ys] * root[t, ys] for t in range(8)])
            for t in range(8):
                line[ys, t] = mass_line(padded, t)
        squares, shifts = [], []
        for t in range(8):
            square = jnp.zeros((SUB, LANES), jnp.float32)
            shifted = jnp.zeros((SUB, LANES), jnp.float32)
            padded = row_ring([line[ys, t] for ys in range(GROUPS)])
            for ys in range(GROUPS):
                now = field[k, t, ys]
                later = outer[t, ys] * mass_line(padded, ys) - (2 * centre * scale) * now
                later = 0.5 * later if begin else later - field[k - 1, t, ys]
                put(k + 1, t, ys, later)
                square = square + now * now
                shifted = shifted + later * now
            squares.append(square)
            shifts.append(shifted)

        def add(parts):
            while len(parts) > 1:
                parts = [parts[i] + parts[i + 1] for i in range(0, len(parts), 2)]
            return jnp.sum(parts[0] * own_rows, axis=0, keepdims=True)

        partial[pl.ds(2 * k, 1), :] = add(squares)
        partial[pl.ds(2 * k + 1, 1), :] = add(shifts)

    def later_step(k, carry):
        step(k, False, False)
        return carry

    partial[...] = jnp.zeros_like(partial)
    step(0, True, False)
    lax.fori_loop(1, ITERS - 1, later_step, 0)
    step(ITERS - 1, False, True)
    whole = jnp.sum(partial[...], axis=1, keepdims=True)
    row = lax.broadcasted_iota(jnp.int32, partial.shape, 0)
    lane = lax.broadcasted_iota(jnp.int32, partial.shape, 1)
    line_of = jnp.sum(jnp.where(row == lane, whole, 0.0), axis=0, keepdims=True)
    sums_ref[...] = jnp.broadcast_to(line_of[None], sums_ref.shape)


def surface_basis(where, vols, own, other, same, cross, root):
    return pl.pallas_call(
        basis_kernel,
        out_shape=(f32(ITERS, 8, GROUPS, SUB, LANES), f32(vols, SUB, LANES)),
        in_specs=[SMEM] + [VMEM] * 5,
        out_specs=(VMEM, VMEM),
        scratch_shapes=[
            pltpu.VMEM((8, ROWS, LANES), jnp.float32),
            pltpu.VMEM((8, GROUPS, SUB, LANES), jnp.float32),
            pltpu.VMEM((8, GROUPS, SUB, LANES), jnp.float32),
            pltpu.VMEM((GROUPS, 8, SUB, LANES), jnp.float32),
            pltpu.VMEM((24, LANES), jnp.float32),
        ],
        compiler_params=params(24),
        cost_estimate=cost(7),
        name="surface_basis",
    )(where, own, other, same, cross, root)


def solve_weights():
    n = ITERS
    moment = np.zeros((2 * n, 2 * n))
    for m in range(2 * n):
        if m < 2:
            moment[m, m] = 1.0
        else:
            moment[m, m] = 2.0
            moment[m, m % 2] = -1.0
    centre, half = (BASIS_LOW + BASIS_HIGH) / 2, (BASIS_HIGH - BASIS_LOW) / 2
    weights = np.zeros((2 * n, 16, LANES))
    for i in range(n):
        for j in range(n):
            lower = abs(j - 1)
            for factor, index in (
                (centre / 2, i + j),
                (centre / 2, abs(i - j)),
                (half / 4, i + j + 1),
                (half / 4, abs(i - j - 1)),
                (half / 4, i + lower),
                (half / 4, abs(i - lower)),
            ):
                weights[:, i, j] += factor * moment[index]
        weights[:, i, n] += moment[i]
    return weights.astype(np.float32)


def solve_kernel(part_ref, sums_ref, weights_ref, out_ref, flag_ref, rows):
    n = ITERS
    total = sums_ref[0]
    for i in range(1, sums_ref.shape[0]):
        total = total + sums_ref[i]
    row = lax.broadcasted_iota(jnp.int32, (16, LANES), 0)
    lane = lax.broadcasted_iota(jnp.int32, (16, LANES), 1)
    system = jnp.where((lane == row + 16) & (row < n), 1.0, 0.0).astype(jnp.float32)
    for m in range(2 * n):
        system = system + weights_ref[m] * total[0:1, m : m + 1]
    centre = jnp.sum(jnp.where(lane == row, system, 0.0), axis=1, keepdims=True)
    for k in range(n):
        pivot_row = system[k : k + 1, :] / system[k : k + 1, k : k + 1]
        column = system[:, k : k + 1]
        system = jnp.where(row == k, pivot_row, system - column * pivot_row)
    inverse = jnp.sum(jnp.where(lane == row + 16, system, 0.0), axis=1, keepdims=True)
    figure = jnp.broadcast_to(centre * inverse, (16, LANES))
    inside = (row < n) & (lane == 0)
    least = jnp.min(jnp.where(inside, figure, 1.0))
    whole = jnp.sum(jnp.where(inside, figure, 0.0))
    flag_ref[0, 0] = jnp.where((least > 0.5) & (whole < CONDITION_MAX), 1, 0).astype(jnp.int32)
    weights = [jnp.broadcast_to(system[k : k + 1, n : n + 1], (SUB, LANES)) for k in range(n)]
    for t in range(8):
        for ys in range(GROUPS):
            value = weights[0] * part_ref[0, t, ys]
            for k in range(1, n):
                value = value + weights[k] * part_ref[k, t, ys]
            rows[t, pl.ds(ys, SUB, stride=GROUPS), :] = value
        out_ref[t] = rows[t, HALO - DEEP : HALO - DEEP + Y_ROWS, :]


def surface_solve(basis, sums):
    return pl.pallas_call(
        solve_kernel,
        out_shape=(f32(8, Y_ROWS, LANES), jax.ShapeDtypeStruct((1, 1), jnp.int32)),
        in_specs=[VMEM, VMEM, VMEM],
        out_specs=(VMEM, SMEM),
        scratch_shapes=[pltpu.VMEM((8, ROWS, LANES), jnp.float32)],
        compiler_params=params(24),
        cost_estimate=cost(3),
        name="surface_solve",
    )(basis, sums, jnp.asarray(solve_weights()))


def fill_factors(factor, where_ref, rows):
    vol, vols = where_ref[0, 3], where_ref[0, 4]
    group = lax.broadcasted_iota(jnp.int32, (SUB, LANES), 0)
    mass, stiff = (8.0, 16.0), (14.0, 16.0)
    for ys in range(Y_GROUPS):
        row = group * Y_GROUPS + ys
        outside = ((vol == 0) & (row < DEEP)) | ((vol == vols - 1) & (row >= DEEP + rows))
        py = ys % 2
        for pz in range(2):
            for px in range(2):
                value = -12.0 / (
                    stiff[pz] * mass[py] * mass[px]
                    + mass[pz] * (stiff[py] * mass[px] + mass[py] * stiff[px])
                )
                factor[pz, px, ys] = jnp.where(outside, 0.0, jnp.float32(value))


def lateral_lines(get, line_a, line_b, put):
    for ys in range(Y_GROUPS):
        padded = column_ring([get(t, ys) for t in range(8)])
        for t in range(8):
            m = mass_line(padded, t)
            line_a[t, ys] = m
            line_b[t, ys] = both_line(padded, t) - m
    for t in range(8):
        a = row_ring([line_a[t, ys] for ys in range(Y_GROUPS)])
        b = row_ring([line_b[t, ys] for ys in range(Y_GROUPS)])
        for ys in range(Y_GROUPS):
            put(t, ys, mass_line(a, ys), both_line(a, ys) + mass_line(b, ys))


def pair_steps(w, c):
    near = c[1] + c[3]
    even = (11.0 / 3.0 * w[1] - (w[0] + w[2])) + ((near + 4.0 * c[2]) - 0.5 * (c[0] + c[4]))
    near = c[2] + c[4]
    odd = (16.0 / 3.0 * w[2] - (w[1] + w[3])) + (near + 8.0 * c[3])
    return even, odd


def strided(ys):
    return pl.ds(ys, SUB, stride=Y_GROUPS)


def change_kernel(
    where_ref, speed_ref, out_ref, cells, along, cross, line_a, line_b, factor, plain, sem,
):
    col = where_ref[0, 1]
    layers, _, rows, _ = out_ref.shape

    def lateral(z, carry):
        def put(t, ys, w, c):
            along[z, t, ys] = w
            cross[z, t, ys] = c

        lateral_lines(lambda t, ys: cells[z, t, ys], line_a, line_b, put)
        return carry

    def set_top():
        for t in range(8):
            for ys in range(Y_GROUPS):
                cells[2, t, ys] = 0.5 * speed_ref[t, strided(ys), :]

    def send(count):
        for z in range(count):
            for t in range(8):
                for ys in range(Y_GROUPS):
                    plain[z, t, strided(ys), :] = cells[z + 2, t, ys]
        copy = pltpu.make_async_copy(
            plain.at[pl.ds(0, count), :, pl.ds(DEEP, rows), :], out_ref.at[pl.ds(0, count)], sem
        )
        copy.start()
        copy.wait()

    @pl.when(col == 0)
    def _():
        fill_factors(factor, where_ref, rows)
        set_top()
        clear = jnp.zeros((8, Y_GROUPS, SUB, LANES), jnp.float32)
        for z in range(layers + 3):
            if z != 2:
                cross[z] = clear
                if z:
                    along[z] = clear
        for z in range(3, layers + 2):
            cells[z] = clear

        def update(pair, carry):
            z = 2 * pair + 2
            for ys in range(Y_GROUPS):
                factors = [[factor[pz, px, ys] for px in range(2)] for pz in range(2)]
                for t in range(8):
                    even, odd = pair_steps(
                        [along[z + i, t, ys] for i in range(-1, 3)],
                        [cross[z + i, t, ys] for i in range(-2, 3)],
                    )
                    cells[z, t, ys] += factors[0][t % 2] * even
                    cells[z + 1, t, ys] += factors[1][t % 2] * odd
            return carry

        def one_sweep(sweep, carry):
            lax.fori_loop(2, 2 * sweep + 3, lateral, 0)
            lax.fori_loop(0, jnp.minimum(sweep + 2, layers // 2), update, 0)
            set_top()
            return carry

        lax.fori_loop(0, SWEEPS, one_sweep, 0)
        send(layers)

    @pl.when(col == 1)
    def _():
        fill_factors(factor, where_ref, rows)
        set_top()

        def one_sweep(sweep, carry):
            lateral(2, 0)
            for t in range(8):
                for ys in range(Y_GROUPS):
                    cells[2, t, ys] = factor[0, t % 2, ys] * (-0.5 * cross[2, t, ys])
            return carry

        lax.fori_loop(0, SWEEPS, one_sweep, 0)
        send(1)


def surface_change(where, speed, layers, rows):
    work = pltpu.VMEM((layers + 4, 8, Y_GROUPS, SUB, LANES), jnp.float32)
    line = pltpu.VMEM((8, Y_GROUPS, SUB, LANES), jnp.float32)
    return pl.pallas_call(
        change_kernel,
        out_shape=f32(layers, 8, rows, LANES),
        in_specs=[SMEM, VMEM],
        out_specs=HBM,
        scratch_shapes=[
            pltpu.VMEM((layers + 2, 8, Y_GROUPS, SUB, LANES), jnp.float32),
            work, work, line, line,
            pltpu.VMEM((2, 2, Y_GROUPS, SUB, LANES), jnp.float32),
            pltpu.VMEM((layers, 8, Y_ROWS, LANES), jnp.float32),
            pltpu.SemaphoreType.DMA,
        ],
        compiler_params=params(32),
        cost_estimate=cost(8),
        name="surface_change",
    )(where, speed)


def base_kernel(
    where_ref, wide_ref, zlow_ref, zhigh_ref, change_ref, speed_ref, select_ref,
    velocity_ref, out_ref, field, along, cross, line_a, line_b, factor, change, parts, sems,
):
    col, cols = where_ref[0, 1], where_ref[0, 2]
    layers, _, rows, _ = change_ref.shape
    total = layers + 2 * DEEP
    own = pltpu.make_async_copy(wide_ref, field.at[pl.ds(DEEP, layers)], sems.at[0])
    low = pltpu.make_async_copy(zlow_ref, field.at[pl.ds(0, DEEP)], sems.at[1])
    high = pltpu.make_async_copy(zhigh_ref, field.at[pl.ds(DEEP + layers, DEEP)], sems.at[2])
    all_change = pltpu.make_async_copy(change_ref, change, sems.at[3])
    one_change = pltpu.make_async_copy(
        change_ref.at[pl.ds(0, 1)], change.at[pl.ds(0, 1)], sems.at[4]
    )
    own.start()
    low.start()
    high.start()
    pl.when(col == 0)(all_change.start)
    pl.when(col == 1)(one_change.start)
    fill_factors(factor, where_ref, rows)
    count = (layers + 1) * rows

    def cut(value, at, t):
        first, second = split(value)
        lanes = slice(LANES * t, LANES * (t + 1))
        parts[at : at + rows, lanes] = first
        parts[count + at : count + at + rows, lanes] = second

    for t in range(8):
        cut(speed_ref[t, DEEP : DEEP + rows, :], 0, t)

    def lateral(z, carry):
        def put(t, ys, w, c):
            along[z, t, ys] = w
            cross[z, t, ys] = c

        lateral_lines(lambda t, ys: field[z, t, strided(ys), :], line_a, line_b, put)
        return carry

    def update(pair, carry):
        z = 2 * pair
        for ys in range(Y_GROUPS):
            factors = [[factor[pz, px, ys] for px in range(2)] for pz in range(2)]
            for t in range(8):
                even, odd = pair_steps(
                    [along[z + i, t, ys] for i in range(-1, 3)], [cross[z + i, t, ys] for i in range(-2, 3)]
                )
                scale = jnp.where((col == 0) & (z == DEEP), 0.0, factors[0][t % 2])
                even = field[z, t, strided(ys), :] + scale * even
                odd = field[z + 1, t, strided(ys), :] + factors[1][t % 2] * odd
                field[z, t, strided(ys), :] = even
                field[z + 1, t, strided(ys), :] = odd
        return carry

    begin = jnp.where(col == 0, DEEP, 0)
    end = jnp.where(col == cols - 1, DEEP + layers + 1, total - 1)

    def one_sweep(sweep, carry):
        first = jnp.maximum(begin, 2 * sweep)
        last = jnp.minimum(end, total - 2 * sweep - 1)

        @pl.when(sweep == 0)
        def _():
            own.wait()

        lax.fori_loop(jnp.where(sweep == 0, DEEP, first), jnp.where(sweep == 0, DEEP + layers, last), lateral, 0)

        @pl.when(sweep == 0)
        def _():
            low.wait()
            high.wait()

        lax.fori_loop(jnp.where(sweep == 0, first, DEEP), DEEP, lateral, 0)
        lax.fori_loop(jnp.where(sweep == 0, DEEP + layers, last), last, lateral, 0)
        low_pair = jnp.where(col == 0, DEEP // 2, sweep + 1)
        high_pair = jnp.where(col == cols - 1, (DEEP + layers) // 2, total // 2 - sweep - 1)
        lax.fori_loop(low_pair, high_pair, update, 0)
        return carry

    @pl.when(col == 0)
    def _():
        clear = jnp.zeros((8, Y_GROUPS, SUB, LANES), jnp.float32)
        for z in (DEEP - 2, DEEP - 1):
            along[z] = clear
            cross[z] = clear

    lax.fori_loop(0, SWEEPS, one_sweep, 0)

    @pl.when(col == 0)
    def _():
        all_change.wait()
        for z in range(layers):
            for t in range(8):
                field[DEEP + z, t, DEEP : DEEP + rows, :] += change[z, t]

    @pl.when(col == 1)
    def _():
        one_change.wait()
        for t in range(8):
            field[DEEP, t, DEEP : DEEP + rows, :] += change[0, t]

    for z in range(layers):
        for t in range(8):
            cut(field[DEEP + z, t, DEEP : DEEP + rows, :], rows * (z + 1), t)

    def write(at, value):
        velocity_ref[:, at] = value[:rows]
        out_ref[:, :, at] = value[rows:].reshape(layers, rows, 256)

    plain_columns(select_ref, parts[...], count, write)


def base_sweeps(where, wide, zlow, zhigh, change, speed, select):
    layers, _, rows, _ = change.shape
    total = layers + 2 * DEEP
    work = pltpu.VMEM((total, 8, Y_GROUPS, SUB, LANES), jnp.float32)
    line = pltpu.VMEM((8, Y_GROUPS, SUB, LANES), jnp.float32)
    return pl.pallas_call(
        base_kernel,
        out_shape=(f32(rows, 8 * LANES), f32(layers, rows, 8 * LANES)),
        in_specs=[SMEM] + [HBM] * 4 + [VMEM] * 2,
        out_specs=(VMEM, VMEM),
        scratch_shapes=[
            pltpu.VMEM((total, 8, Y_ROWS, LANES), jnp.float32),
            work, work, line, line,
            pltpu.VMEM((2, 2, Y_GROUPS, SUB, LANES), jnp.float32),
            pltpu.VMEM((layers, 8, rows, LANES), jnp.float32),
            pltpu.VMEM((2 * (layers + 1) * rows, 8 * LANES), jnp.bfloat16),
            pltpu.SemaphoreType.DMA((5,)),
        ],
        compiler_params=params(50),
        cost_estimate=cost(25),
        name="base_sweeps",
    )(where, wide, zlow, zhigh, change, speed, select)


mass_even = (-1.0 / 15.0, 2.0 / 15.0, 8.0 / 15.0, 2.0 / 15.0, -1.0 / 15.0)
mass_odd = (0.0, 2.0 / 15.0, 16.0 / 15.0, 2.0 / 15.0, 0.0)


def mass_along(padded, axis):
    count = padded.shape[axis] - 4
    pieces = [lax.slice_in_dim(padded, i, i + count, axis=axis) for i in range(5)]
    even = sum(mass_even[i] * pieces[i] for i in range(5))
    odd = sum(mass_odd[i] * pieces[i] for i in range(1, 4))
    at_even = lax.broadcasted_iota(jnp.int32, even.shape, axis) % 2 == 0
    return jnp.where(at_even, even, odd)


def with_rows(x, width):
    size = lax.axis_size("vol")
    up = [(i, i + 1) for i in range(size - 1)]
    down = [(j, i) for i, j in up]
    before = lax.ppermute(x[-width:], "vol", up)
    after = lax.ppermute(x[:width], "vol", down)
    return jnp.concatenate([before, x, after], axis=0)


def stepwise(flux, metric):
    root = jnp.sqrt(metric)

    def dot(a, b):
        return lax.psum(jnp.sum(a * b), "vol")

    def step(_, state):
        solved, residual, direction, norm = state
        padded = jnp.pad(with_rows(root * direction, 2), ((0, 0), (2, 2)))
        image = root * mass_along(mass_along(padded, 1), 0)
        alpha = norm / dot(direction, image)
        solved = solved + alpha * direction
        residual = residual - alpha * image
        after = dot(residual, residual)
        direction = residual + after / norm * direction
        return solved, residual, direction, after

    state = (jnp.zeros_like(flux), flux, flux, dot(flux, flux))
    return with_rows(lax.fori_loop(0, ITERS, step, state)[0], DEEP)


def after(x, *others):
    return lax.optimization_barrier((x,) + others)[0]


def on_device(face_area, face_speed, face_node, face_count, surface_metric, displacement):
    vols, cols = lax.axis_size("vol"), lax.axis_size("col")
    vol, col = lax.axis_index("vol"), lax.axis_index("col")
    core = col % 2
    where = jnp.stack([core, col, jnp.int32(cols), vol, jnp.int32(vols)]).astype(jnp.int32).reshape(1, 5)
    up = [(i, i + 1) for i in range(vols - 1)]
    down = [(j, i) for i, j in up]
    col_up = [(i, i + 1) for i in range(cols - 1)]
    col_down = [(j, i) for i, j in col_up]
    packed = displacement.shape[0] * DEEP

    select = plain_selection()

    def moved(x, steps):
        dv, dc = steps
        pairs = [
            (i * cols + j, (i + dv) * cols + j + dc)
            for i in range(vols)
            for j in range(cols)
            if 0 <= i + dv < vols and 0 <= j + dc < cols
        ]
        return lax.ppermute(x, ("vol", "col"), pairs)

    keep, send, rows_up, rows_down = face_sums(
        where, face_count, face_area, face_speed, face_node, displacement, surface_metric
    )
    with jax.named_scope("flux_sum"):
        keep = keep + lax.ppermute(send, "col", [(j, j ^ 1) for j in range(cols)])
        turned = [
            lax.ppermute(keep, "col", [(j, (j + 2 * k) % cols) for j in range(cols)]) for k in (1, 2, 3)
        ]
    with jax.named_scope("row_halo"):
        rows_before, rows_after = moved(rows_up, (1, 0)), moved(rows_down, (-1, 0))
    wide, root = regroup(displacement, surface_metric, rows_before, rows_after)
    with jax.named_scope("flux_sum"):
        turned = lax.optimization_barrier((*turned, wide))
        own = (keep + turned[1]) + (turned[0] + turned[2])
    with jax.named_scope("flux_halo"):
        other = lax.ppermute(own, "col", [(j, j ^ 1) for j in range(cols)])
        pairs = []
        for i in range(vols):
            for j in range(cols):
                to = i - 1 if j % 2 == 0 else i + 1
                if 0 <= to < vols:
                    pairs.append((i * cols + j, to * cols + j))
        same = lax.ppermute(own, ("vol", "col"), pairs)
        cross = lax.ppermute(same, "col", [(j, j ^ 1) for j in range(cols)])

    with jax.named_scope("depth_halo"):
        sent = after(wide, other)
        zlow, zhigh = moved(sent, (0, 1)), moved(sent, (0, -1))
    basis, spread = surface_basis(where, vols, own, other, same, cross, root)
    with jax.named_scope("gather_sums"):
        gathered = lax.all_to_all(spread, "vol", 0, 0)
    speed, flag = surface_solve(basis, gathered)

    def finish(speed):
        change = surface_change(where, speed, displacement.shape[0], displacement.shape[1])
        return base_sweeps(where, wide, zlow, zhigh, change, speed, select)

    def step_by_step():
        low = jnp.where(core == 0, own, other)
        high = jnp.where(core == 0, other, own)
        flux = jnp.concatenate([low, high], axis=1)
        flux = flux.transpose(1, 2, 0).reshape(surface_metric.shape)
        solved = stepwise(flux, surface_metric)
        return finish(solved.reshape(Y_ROWS, LANES, 8).transpose(2, 0, 1))

    return lax.cond(flag[0, 0] > 0, lambda: finish(speed), step_by_step)


def solution(mesh):
    in_specs = (
        P("vol", "col"),
        P("vol", "col"),
        P("vol", "col"),
        P("vol", "col"),
        P("vol", None),
        P("col", "vol", None),
    )
    out_specs = (P("vol", None), P("col", "vol", None))
    return jax.shard_map(
        on_device, mesh=mesh, in_specs=in_specs, out_specs=out_specs, check_vma=False
    )
```

```python
import jax
import jax.numpy as jnp
import numpy as np
from jax import lax
from jax.experimental import pallas as pl
from jax.experimental.pallas import tpu as pltpu
from jax.sharding import PartitionSpec as P

ITERS = 10
SWEEPS = 4
LANES = 128
SUB = 8
MIB = 1024 * 1024
DEEP = 2 * SWEEPS
HALO = 32
ROWS = 128
GROUPS = 16
Y_GROUPS = 10
Y_ROWS = 80

BASIS_LOW = 0.1
BASIS_HIGH = 12.0
CONDITION_MAX = 2000.0


def rolled(x, shift, axis):
    return pltpu.roll(x, shift % x.shape[axis], axis)


def column_ring(tiles):
    n = len(tiles)
    lane = lax.broadcasted_iota(jnp.int32, tiles[0].shape, 1)
    first, last = lane == 0, lane == LANES - 1
    return (
        [jnp.where(first, 0.0, rolled(tiles[j], 1, 1)) for j in (n - 2, n - 1)]
        + list(tiles)
        + [jnp.where(last, 0.0, rolled(tiles[j], -1, 1)) for j in (0, 1)]
    )


def row_ring(rows):
    n = len(rows)
    return (
        [rolled(rows[j], 1, 0) for j in (n - 2, n - 1)]
        + list(rows)
        + [rolled(rows[j], -1, 0) for j in (0, 1)]
    )


def mass_line(padded, index):
    i = index + 2
    near = padded[i - 1] + padded[i + 1]
    if index % 2:
        return near + 4.0 * padded[i]
    return (near + 8.0 * padded[i]) - (padded[i - 2] + padded[i + 2])


def both_line(padded, index):
    i = index + 2
    near = padded[i - 1] + padded[i + 1]
    return (8.0 / 3.0 if index % 2 else 22.0 / 3.0) * padded[i] - near


def stored(parity):
    return 1.0 if parity else 0.5


def given(parity):
    return 0.5 if parity else 1.0


SMEM = pl.BlockSpec(memory_space=pltpu.SMEM)
VMEM = pl.BlockSpec(memory_space=pltpu.VMEM)
HBM = pl.BlockSpec(memory_space=pltpu.HBM)


def f32(*shape):
    return jax.ShapeDtypeStruct(shape, jnp.float32)


def params(mib):
    return pltpu.CompilerParams(vmem_limit_bytes=mib * MIB)


def cost(us):
    return pl.CostEstimate(flops=0, bytes_accessed=int(us * 100_000), transcendentals=0)


def split(x):
    first = x.astype(jnp.bfloat16)
    return first, (x - first.astype(jnp.float32)).astype(jnp.bfloat16)


def to_blocked(j):
    x = lax.broadcasted_iota(jnp.int32, (1024, 256), 0)
    n = lax.broadcasted_iota(jnp.int32, (1024, 256), 1)
    hit = x == 8 * (n & 127) + j + (n >> 7)
    return jnp.where(hit, 1.0, 0.0).astype(jnp.bfloat16)


def plain_selection():
    k = np.arange(1024)
    out = np.zeros((1024, 1024), np.float32)
    out[k, 8 * (k % LANES) + k // LANES] = 1.0
    return jnp.asarray(out, jnp.bfloat16)


def regroup_kernel(block_ref, metric_ref, before_ref, after_ref, wide_ref, root_ref, parts_ref):
    layers, rows, _ = block_ref.shape
    packed = DEEP * layers
    total = layers * Y_ROWS + ROWS

    def put(at, value):
        first, second = split(value)
        parts_ref[at : at + value.shape[0], :] = first
        parts_ref[total + at : total + at + value.shape[0], :] = second

    for z in range(layers):
        put(Y_ROWS * z, before_ref[DEEP * z : DEEP * (z + 1), :])
        put(Y_ROWS * z + DEEP, block_ref[z])
        put(Y_ROWS * z + DEEP + rows, after_ref[DEEP * z : DEEP * (z + 1), :])
    row = lax.broadcasted_iota(jnp.int32, (Y_ROWS, LANES), 0)
    by_row = jnp.where(row % 2 == 0, stored(0), stored(1)).astype(jnp.float32)
    at = layers * Y_ROWS
    put(at, jnp.sqrt(before_ref[packed:, :]))
    put(at + HALO, jnp.sqrt(metric_ref[...]))
    put(at + HALO + rows, jnp.sqrt(after_ref[packed:, :]))
    for j in range(0, 8, 2):
        pair = jnp.dot(parts_ref[...], to_blocked(j), preferred_element_type=jnp.float32)
        pair = pair[:total] + pair[total:]
        for i in range(2):
            tile = pair[:, LANES * i : LANES * (i + 1)]
            for z in range(layers):
                wide_ref[z, j + i] = tile[Y_ROWS * z : Y_ROWS * (z + 1)] * (by_row * (stored(z % 2) * stored(i)))
            root_ref[j + i] = tile[layers * Y_ROWS :]


def regroup(block, metric, before, after):
    layers, rows, cols = block.shape
    return pl.pallas_call(
        regroup_kernel,
        out_shape=(f32(layers, 8, Y_ROWS, LANES), f32(8, ROWS, LANES)),
        in_specs=[VMEM] * 4,
        out_specs=(VMEM, VMEM),
        scratch_shapes=[pltpu.VMEM((2 * (Y_ROWS * layers + ROWS), cols), jnp.bfloat16)],
        compiler_params=params(32),
        cost_estimate=cost(6),
        name="regroup",
    )(block, metric, before, after)


def plain_columns(select_ref, parts, rows, write):
    for q in range(4):
        at = slice(256 * q, 256 * (q + 1))
        value = jnp.dot(parts, select_ref[:, at], preferred_element_type=jnp.float32)
        write(at, value[:rows] + value[rows:])


def face_kernel(
    where_ref, count_ref, area_ref, speed_ref, node_ref, block_ref, metric_ref,
    keep_ref, send_ref, up_ref, down_ref, area, speed, nodes, acc_ref, sems,
):
    slots = area_ref.shape[1]
    fetches = [
        pltpu.make_async_copy(source, target, sems.at[i])
        for i, (source, target) in enumerate(((area_ref, area), (speed_ref, speed), (node_ref, nodes)))
    ]
    for fetch in fetches:
        fetch.start()
    layers, rows, _ = block_ref.shape
    copies = []
    for out_ref, row, root_row in ((up_ref, rows - DEEP, rows - HALO), (down_ref, 0, 0)):
        for z in range(layers):
            part = block_ref.at[z, pl.ds(row, DEEP), :]
            copies.append((part, out_ref.at[pl.ds(DEEP * z, DEEP), :]))
        part = metric_ref.at[pl.ds(root_row, HALO), :]
        copies.append((part, out_ref.at[pl.ds(DEEP * layers, HALO), :]))
    copies = [pltpu.make_async_copy(*pair, sems.at[i + 3]) for i, pair in enumerate(copies)]
    for copy in copies:
        copy.start()
    chunk = min(4096, slots)
    core = where_ref[0, 0]
    ids = lax.broadcasted_iota(jnp.int32, (256, chunk), 0)
    ids = ids.astype(jnp.float32).astype(jnp.bfloat16)
    zero = jnp.zeros((), jnp.bfloat16)
    one = jnp.ones((), jnp.bfloat16)
    contract = (((1,), (1,)), ((), ()))
    acc_ref[...] = jnp.zeros_like(acc_ref)
    for fetch in fetches:
        fetch.wait()

    def wide(x):
        return jnp.broadcast_to(x.astype(jnp.bfloat16), (256, chunk))

    def body(step, carry):
        at = pl.ds(pl.multiple_of(step * chunk, chunk), chunk)
        slot = lax.broadcasted_iota(jnp.int32, (1, chunk), 1) + step * chunk
        value = jnp.where(slot < count_ref[0, 0], area[:, at] * speed[:, at], 0.0)
        node = nodes[:, at]
        low = (((node & 1) << 7) + ((node >> 3) & 127)).astype(jnp.float32)
        high = (((node >> 1) & 3) * 64 + (node >> 10)).astype(jnp.float32)
        first = value.astype(jnp.bfloat16)
        second = value - first.astype(jnp.float32)
        here = wide(high) == ids
        upper = jnp.where(here, wide(first), zero)
        lower = jnp.where(here, wide(second), zero)
        columns = jnp.where(wide(low) == ids, one, zero)
        both = jnp.concatenate([upper, lower], axis=0)
        acc_ref[...] += lax.dot_general(both, columns, contract, preferred_element_type=jnp.float32)
        return carry

    lax.fori_loop(0, slots // chunk, body, 0)
    for j in range(8):
        at, lanes = 64 * (j // 2), slice(LANES * (j % 2), LANES * (j % 2 + 1))
        near, far = at + 32 * core, at + 32 - 32 * core
        keep_ref[j] = acc_ref[pl.ds(near, 32), lanes] + acc_ref[pl.ds(256 + near, 32), lanes]
        send_ref[j] = acc_ref[pl.ds(far, 32), lanes] + acc_ref[pl.ds(256 + far, 32), lanes]
    for copy in copies:
        copy.wait()


def face_sums(where, count, area, speed, node, block, metric):
    half = f32(8, 32, LANES)
    layers, _, cols = block.shape
    rows = f32(DEEP * layers + HALO, cols)
    return pl.pallas_call(
        face_kernel,
        out_shape=(half, half, rows, rows),
        in_specs=[SMEM, SMEM] + [HBM] * 5,
        out_specs=(VMEM, VMEM, VMEM, VMEM),
        scratch_shapes=[
            pltpu.VMEM(area.shape, jnp.float32),
            pltpu.VMEM(area.shape, jnp.float32),
            pltpu.VMEM(area.shape, jnp.int32),
            pltpu.VMEM((512, 256), jnp.float32),
            pltpu.SemaphoreType.DMA((2 * layers + 5,)),
        ],
        compiler_params=params(56),
        cost_estimate=cost(7),
        name="face_sums",
    )(where, count, area, speed, node, block, metric)


def basis_kernel(
    where_ref, own_ref, other_ref, same_ref, cross_ref, root_ref,
    field, sums_ref, rows, root, outer, line, partial,
):
    core = where_ref[0, 0]
    centre = (BASIS_LOW + BASIS_HIGH) / 2
    scale = 2 / (BASIS_HIGH - BASIS_LOW)
    for t in range(8):
        rows[t, pl.ds(32 + 32 * core, 32), :] = own_ref[t]
        rows[t, pl.ds(64 - 32 * core, 32), :] = other_ref[t]
        rows[t, pl.ds(96 * core, 32), :] = cross_ref[t]
        rows[t, pl.ds(96 - 96 * core, 32), :] = same_ref[t]
    for t in range(8):
        for ys in range(GROUPS):
            field[0, t, ys] = rows[t, pl.ds(ys, SUB, stride=GROUPS), :]
            value = root_ref[t, pl.ds(ys, SUB, stride=GROUPS), :]
            root[t, ys] = value * (stored(t % 2) * stored(ys % 2))
            outer[t, ys] = value * (2 * scale * 4.0 / 225.0 / (given(t % 2) * given(ys % 2)))

    group = lax.broadcasted_iota(jnp.int32, (SUB, LANES), 0)
    own_rows = jnp.where((group >= 2) & (group < 6), 1.0, 0.0).astype(jnp.float32)

    def step(k, begin, end):
        def put(k, t, ys, value):
            if not end:
                field[k, t, ys] = value

        for ys in range(GROUPS):
            padded = column_ring([field[k, t, ys] * root[t, ys] for t in range(8)])
            for t in range(8):
                line[ys, t] = mass_line(padded, t)
        squares, shifts = [], []
        for t in range(8):
            square = jnp.zeros((SUB, LANES), jnp.float32)
            shifted = jnp.zeros((SUB, LANES), jnp.float32)
            padded = row_ring([line[ys, t] for ys in range(GROUPS)])
            for ys in range(GROUPS):
                now = field[k, t, ys]
                later = outer[t, ys] * mass_line(padded, ys) - (2 * centre * scale) * now
                later = 0.5 * later if begin else later - field[k - 1, t, ys]
                put(k + 1, t, ys, later)
                square = square + now * now
                shifted = shifted + later * now
            squares.append(square)
            shifts.append(shifted)

        def add(parts):
            while len(parts) > 1:
                parts = [parts[i] + parts[i + 1] for i in range(0, len(parts), 2)]
            return jnp.sum(parts[0] * own_rows, axis=0, keepdims=True)

        partial[pl.ds(2 * k, 1), :] = add(squares)
        partial[pl.ds(2 * k + 1, 1), :] = add(shifts)

    def later_step(k, carry):
        step(k, False, False)
        return carry

    partial[...] = jnp.zeros_like(partial)
    step(0, True, False)
    lax.fori_loop(1, ITERS - 1, later_step, 0)
    step(ITERS - 1, False, True)
    whole = jnp.sum(partial[...], axis=1, keepdims=True)
    row = lax.broadcasted_iota(jnp.int32, partial.shape, 0)
    lane = lax.broadcasted_iota(jnp.int32, partial.shape, 1)
    line_of = jnp.sum(jnp.where(row == lane, whole, 0.0), axis=0, keepdims=True)
    sums_ref[...] = jnp.broadcast_to(line_of[None], sums_ref.shape)


def surface_basis(where, vols, own, other, same, cross, root):
    return pl.pallas_call(
        basis_kernel,
        out_shape=(f32(ITERS, 8, GROUPS, SUB, LANES), f32(vols, SUB, LANES)),
        in_specs=[SMEM] + [VMEM] * 5,
        out_specs=(VMEM, VMEM),
        scratch_shapes=[
            pltpu.VMEM((8, ROWS, LANES), jnp.float32),
            pltpu.VMEM((8, GROUPS, SUB, LANES), jnp.float32),
            pltpu.VMEM((8, GROUPS, SUB, LANES), jnp.float32),
            pltpu.VMEM((GROUPS, 8, SUB, LANES), jnp.float32),
            pltpu.VMEM((24, LANES), jnp.float32),
        ],
        compiler_params=params(24),
        cost_estimate=cost(7),
        name="surface_basis",
    )(where, own, other, same, cross, root)


def solve_weights():
    n = ITERS
    moment = np.zeros((2 * n, 2 * n))
    for m in range(2 * n):
        if m < 2:
            moment[m, m] = 1.0
        else:
            moment[m, m] = 2.0
            moment[m, m % 2] = -1.0
    centre, half = (BASIS_LOW + BASIS_HIGH) / 2, (BASIS_HIGH - BASIS_LOW) / 2
    weights = np.zeros((2 * n, 16, LANES))
    for i in range(n):
        for j in range(n):
            lower = abs(j - 1)
            for factor, index in (
                (centre / 2, i + j),
                (centre / 2, abs(i - j)),
                (half / 4, i + j + 1),
                (half / 4, abs(i - j - 1)),
                (half / 4, i + lower),
                (half / 4, abs(i - lower)),
            ):
                weights[:, i, j] += factor * moment[index]
        weights[:, i, n] += moment[i]
    return weights.astype(np.float32)


def solve_kernel(part_ref, sums_ref, weights_ref, out_ref, flag_ref, rows):
    n = ITERS
    total = sums_ref[0]
    for i in range(1, sums_ref.shape[0]):
        total = total + sums_ref[i]
    row = lax.broadcasted_iota(jnp.int32, (16, LANES), 0)
    lane = lax.broadcasted_iota(jnp.int32, (16, LANES), 1)
    system = jnp.where((lane == row + 16) & (row < n), 1.0, 0.0).astype(jnp.float32)
    for m in range(2 * n):
        system = system + weights_ref[m] * total[0:1, m : m + 1]
    centre = jnp.sum(jnp.where(lane == row, system, 0.0), axis=1, keepdims=True)
    for k in range(n):
        pivot_row = system[k : k + 1, :] / system[k : k + 1, k : k + 1]
        column = system[:, k : k + 1]
        system = jnp.where(row == k, pivot_row, system - column * pivot_row)
    inverse = jnp.sum(jnp.where(lane == row + 16, system, 0.0), axis=1, keepdims=True)
    figure = jnp.broadcast_to(centre * inverse, (16, LANES))
    inside = (row < n) & (lane == 0)
    least = jnp.min(jnp.where(inside, figure, 1.0))
    whole = jnp.sum(jnp.where(inside, figure, 0.0))
    flag_ref[0, 0] = jnp.where((least > 0.5) & (whole < CONDITION_MAX), 1, 0).astype(jnp.int32)
    weights = [jnp.broadcast_to(system[k : k + 1, n : n + 1], (SUB, LANES)) for k in range(n)]
    for t in range(8):
        for ys in range(GROUPS):
            value = weights[0] * part_ref[0, t, ys]
            for k in range(1, n):
                value = value + weights[k] * part_ref[k, t, ys]
            rows[t, pl.ds(ys, SUB, stride=GROUPS), :] = value
        out_ref[t] = rows[t, HALO - DEEP : HALO - DEEP + Y_ROWS, :]


def surface_solve(basis, sums):
    return pl.pallas_call(
        solve_kernel,
        out_shape=(f32(8, Y_ROWS, LANES), jax.ShapeDtypeStruct((1, 1), jnp.int32)),
        in_specs=[VMEM, VMEM, VMEM],
        out_specs=(VMEM, SMEM),
        scratch_shapes=[pltpu.VMEM((8, ROWS, LANES), jnp.float32)],
        compiler_params=params(24),
        cost_estimate=cost(3),
        name="surface_solve",
    )(basis, sums, jnp.asarray(solve_weights()))


def factor_kernel(where_ref, factor):
    vol, vols, rows = where_ref[0, 3], where_ref[0, 4], where_ref[0, 5]
    group = lax.broadcasted_iota(jnp.int32, (SUB, LANES), 0)
    mass, stiff = (8.0, 16.0), (14.0, 16.0)
    for ys in range(Y_GROUPS):
        row = group * Y_GROUPS + ys
        outside = ((vol == 0) & (row < DEEP)) | ((vol == vols - 1) & (row >= DEEP + rows))
        py = ys % 2
        for pz in range(2):
            for px in range(2):
                value = -12.0 / (
                    stiff[pz] * mass[py] * mass[px]
                    + mass[pz] * (stiff[py] * mass[px] + mass[py] * stiff[px])
                )
                for p in (pz, py, px):
                    value = value * stored(p) / given(p)
                factor[pz, px, ys] = jnp.where(outside, 0.0, jnp.float32(value))


def relaxation_factors(where):
    return pl.pallas_call(
        factor_kernel,
        out_shape=f32(2, 2, Y_GROUPS, SUB, LANES),
        in_specs=[SMEM],
        out_specs=VMEM,
        compiler_params=params(16),
        cost_estimate=cost(1),
        name="relaxation_factors",
    )(where)


def lateral_lines(get, line_a, line_b, put):
    for ys in range(Y_GROUPS):
        padded = column_ring([get(t, ys) for t in range(8)])
        for t in range(8):
            m = mass_line(padded, t)
            line_a[t, ys] = m
            line_b[t, ys] = both_line(padded, t) - m
    for t in range(8):
        a = row_ring([line_a[t, ys] for ys in range(Y_GROUPS)])
        b = row_ring([line_b[t, ys] for ys in range(Y_GROUPS)])
        for ys in range(Y_GROUPS):
            put(t, ys, mass_line(a, ys), both_line(a, ys) + mass_line(b, ys))


def even_step(w, c):
    near = c[1] + c[3]
    return (22.0 / 3.0 * w[1] - (w[0] + w[2])) + ((near + 8.0 * c[2]) - (c[0] + c[4]))


def odd_step(w, c):
    return (8.0 / 3.0 * w[1] - (w[0] + w[2])) + ((c[0] + c[2]) + 4.0 * c[1])


def strided(ys):
    return pl.ds(ys, SUB, stride=Y_GROUPS)


def change_kernel(
    where_ref, factor, speed_ref, out_ref, cells, along, cross, line_a, line_b, plain, sems,
):
    col = where_ref[0, 1]
    layers, _, rows, _ = out_ref.shape

    def lateral(z, carry):
        def put(t, ys, w, c):
            along[z, t, ys] = w
            cross[z, t, ys] = c

        lateral_lines(lambda t, ys: cells[z, t, ys], line_a, line_b, put)
        return carry

    def set_top():
        for t in range(8):
            for ys in range(Y_GROUPS):
                scale = 0.5 * stored(0) * stored(t % 2) * stored(ys % 2)
                cells[2, t, ys] = scale * speed_ref[t, strided(ys), :]

    def send(first, count):
        copies = []
        for z in range(first, first + count):
            for t in range(8):
                for ys in range(Y_GROUPS):
                    plain[z, t, strided(ys), :] = cells[z + 2, t, ys]
            copy = pltpu.make_async_copy(
                plain.at[z, :, pl.ds(DEEP, rows), :], out_ref.at[z], sems.at[z]
            )
            copy.start()
            copies.append(copy)
        for copy in copies:
            copy.wait()

    @pl.when(col == 0)
    def _():
        set_top()
        clear = jnp.zeros((8, Y_GROUPS, SUB, LANES), jnp.float32)
        for z in range(2):
            cross[z] = clear
            along[z] = clear

        def update(pair, carry):
            z = 2 * pair + 2
            for ys in range(Y_GROUPS):
                factors = [[factor[pz, px, ys] for px in range(2)] for pz in range(2)]
                for t in range(8):
                    w = [along[z + i, t, ys] for i in range(-1, 3)]
                    c = [cross[z + i, t, ys] for i in range(-2, 3)]
                    cells[z, t, ys] += factors[0][t % 2] * even_step(w, c)
                    cells[z + 1, t, ys] += factors[1][t % 2] * odd_step(w[1:], c[2:])
            return carry

        def one_sweep(sweep, carry):
            front = 2 * sweep + 2
            lax.fori_loop(2, front + 1, lateral, 0)
            lax.fori_loop(0, sweep, update, 0)
            for ys in range(Y_GROUPS):
                factors = [[factor[pz, px, ys] for px in range(2)] for pz in range(2)]
                for t in range(8):
                    w0, w1 = along[front - 1, t, ys], along[front, t, ys]
                    c0, c1, c2 = [cross[front + i, t, ys] for i in range(-2, 1)]
                    step = (22.0 / 3.0 * w1 - w0) + ((c1 + 8.0 * c2) - c0)
                    cells[front, t, ys] += factors[0][t % 2] * step
                    cells[front + 1, t, ys] = factors[1][t % 2] * (c2 - w1)
                    cells[front + 2, t, ys] = -factors[0][t % 2] * c2
            set_top()
            return carry

        lax.fori_loop(0, SWEEPS, one_sweep, 0)
        send(1, layers - 1)

    @pl.when(col == 1)
    def _():
        set_top()

        def one_sweep(sweep, carry):
            lateral(2, 0)
            for t in range(8):
                for ys in range(Y_GROUPS):
                    cells[2, t, ys] = -factor[0, t % 2, ys] * cross[2, t, ys]
            return carry

        lax.fori_loop(0, SWEEPS, one_sweep, 0)
        send(0, 1)


def surface_change(where, factor, speed, layers, rows):
    work = pltpu.VMEM((layers + 2, 8, Y_GROUPS, SUB, LANES), jnp.float32)
    line = pltpu.VMEM((8, Y_GROUPS, SUB, LANES), jnp.float32)
    return pl.pallas_call(
        change_kernel,
        out_shape=f32(layers, 8, rows, LANES),
        in_specs=[SMEM, VMEM, VMEM],
        out_specs=HBM,
        scratch_shapes=[
            pltpu.VMEM((layers + 3, 8, Y_GROUPS, SUB, LANES), jnp.float32),
            work, work, line, line,
            pltpu.VMEM((layers, 8, Y_ROWS, LANES), jnp.float32),
            pltpu.SemaphoreType.DMA((layers,)),
        ],
        compiler_params=params(32),
        cost_estimate=cost(8),
        name="surface_change",
    )(where, factor, speed)


def base_kernel(
    where_ref, factor, wide_ref, zlow_ref, zhigh_ref, change_ref, speed_ref, select_ref,
    velocity_ref, out_ref, field, along, cross, line_a, line_b, change, parts, sems,
):
    col, cols = where_ref[0, 1], where_ref[0, 2]
    layers, _, rows, _ = change_ref.shape
    total = layers + 2 * DEEP
    own = pltpu.make_async_copy(wide_ref, field.at[pl.ds(DEEP, layers)], sems.at[0])
    low = pltpu.make_async_copy(zlow_ref, field.at[pl.ds(0, DEEP)], sems.at[1])
    high = pltpu.make_async_copy(zhigh_ref, field.at[pl.ds(DEEP + layers, DEEP)], sems.at[2])
    all_change = pltpu.make_async_copy(
        change_ref.at[pl.ds(1, layers - 1)], change.at[pl.ds(1, layers - 1)], sems.at[3]
    )
    one_change = pltpu.make_async_copy(
        change_ref.at[pl.ds(0, 1)], change.at[pl.ds(0, 1)], sems.at[4]
    )
    own.start()
    low.start()
    high.start()
    pl.when(col == 0)(all_change.start)
    pl.when(col == 1)(one_change.start)
    count = (layers + 1) * rows

    def cut(value, at, t):
        first, second = split(value)
        lanes = slice(LANES * t, LANES * (t + 1))
        parts[at : at + rows, lanes] = first
        parts[count + at : count + at + rows, lanes] = second

    for t in range(8):
        cut(speed_ref[t, DEEP : DEEP + rows, :], 0, t)

    def lateral(z, carry):
        def put(t, ys, w, c):
            along[z, t, ys] = w
            cross[z, t, ys] = c

        lateral_lines(lambda t, ys: field[z, t, strided(ys), :], line_a, line_b, put)
        return carry

    def update(pair, carry):
        z = 2 * pair
        for ys in range(Y_GROUPS):
            factors = [[factor[pz, px, ys] for px in range(2)] for pz in range(2)]
            for t in range(8):
                w = [along[z + i, t, ys] for i in range(-1, 3)]
                c = [cross[z + i, t, ys] for i in range(-2, 3)]
                even, odd = even_step(w, c), odd_step(w[1:], c[2:])
                scale = jnp.where((col == 0) & (z == DEEP), 0.0, factors[0][t % 2])
                even = field[z, t, strided(ys), :] + scale * even
                odd = field[z + 1, t, strided(ys), :] + factors[1][t % 2] * odd
                field[z, t, strided(ys), :] = even
                field[z + 1, t, strided(ys), :] = odd
        return carry

    begin = jnp.where(col == 0, DEEP, 0)
    end = jnp.where(col == cols - 1, DEEP + layers + 1, total - 1)

    def one_sweep(sweep, carry):
        first = jnp.maximum(begin, 2 * sweep)
        last = jnp.minimum(end, total - 2 * sweep - 1)

        @pl.when(sweep == 0)
        def _():
            own.wait()

        lax.fori_loop(jnp.where(sweep == 0, DEEP, first), jnp.where(sweep == 0, DEEP + layers, last), lateral, 0)

        @pl.when(sweep == 0)
        def _():
            low.wait()
            high.wait()

        lax.fori_loop(jnp.where(sweep == 0, first, DEEP), DEEP, lateral, 0)
        lax.fori_loop(jnp.where(sweep == 0, DEEP + layers, last), last, lateral, 0)
        low_pair = jnp.where(col == 0, DEEP // 2, sweep + 1)
        high_pair = jnp.where(col == cols - 1, (DEEP + layers) // 2, total // 2 - sweep - 1)
        lax.fori_loop(low_pair, high_pair, update, 0)
        return carry

    @pl.when(col == 0)
    def _():
        clear = jnp.zeros((8, Y_GROUPS, SUB, LANES), jnp.float32)
        for z in (DEEP - 2, DEEP - 1):
            along[z] = clear
            cross[z] = clear

    lax.fori_loop(0, SWEEPS, one_sweep, 0)

    row = lax.broadcasted_iota(jnp.int32, (rows, LANES), 0)
    by_row = jnp.where(row % 2 == 0, stored(0), stored(1)).astype(jnp.float32)
    back_row = jnp.where(row % 2 == 0, 1 / stored(0), 1 / stored(1)).astype(jnp.float32)

    @pl.when(col == 0)
    def _():
        all_change.wait()
        for t in range(8):
            top = speed_ref[t, DEEP : DEEP + rows, :] * (by_row * (0.5 * stored(0) * stored(t % 2)))
            field[DEEP, t, DEEP : DEEP + rows, :] += top
            for z in range(1, layers):
                field[DEEP + z, t, DEEP : DEEP + rows, :] += change[z, t]

    @pl.when(col == 1)
    def _():
        one_change.wait()
        for t in range(8):
            field[DEEP, t, DEEP : DEEP + rows, :] += change[0, t]

    for z in range(layers):
        for t in range(8):
            value = field[DEEP + z, t, DEEP : DEEP + rows, :]
            cut(value * (back_row * (1 / (stored(z % 2) * stored(t % 2)))), rows * (z + 1), t)

    def write(at, value):
        velocity_ref[:, at] = value[:rows]
        out_ref[:, :, at] = value[rows:].reshape(layers, rows, 256)

    plain_columns(select_ref, parts[...], count, write)


def base_sweeps(where, factor, wide, zlow, zhigh, change, speed, select):
    layers, _, rows, _ = change.shape
    total = layers + 2 * DEEP
    work = pltpu.VMEM((total, 8, Y_GROUPS, SUB, LANES), jnp.float32)
    line = pltpu.VMEM((8, Y_GROUPS, SUB, LANES), jnp.float32)
    return pl.pallas_call(
        base_kernel,
        out_shape=(f32(rows, 8 * LANES), f32(layers, rows, 8 * LANES)),
        in_specs=[SMEM, VMEM] + [HBM] * 4 + [VMEM] * 2,
        out_specs=(VMEM, VMEM),
        scratch_shapes=[
            pltpu.VMEM((total, 8, Y_ROWS, LANES), jnp.float32),
            work, work, line, line,
            pltpu.VMEM((layers, 8, rows, LANES), jnp.float32),
            pltpu.VMEM((2 * (layers + 1) * rows, 8 * LANES), jnp.bfloat16),
            pltpu.SemaphoreType.DMA((5,)),
        ],
        compiler_params=params(50),
        cost_estimate=cost(25),
        name="base_sweeps",
    )(where, factor, wide, zlow, zhigh, change, speed, select)


mass_even = (-1.0 / 15.0, 2.0 / 15.0, 8.0 / 15.0, 2.0 / 15.0, -1.0 / 15.0)
mass_odd = (0.0, 2.0 / 15.0, 16.0 / 15.0, 2.0 / 15.0, 0.0)


def mass_along(padded, axis):
    count = padded.shape[axis] - 4
    pieces = [lax.slice_in_dim(padded, i, i + count, axis=axis) for i in range(5)]
    even = sum(mass_even[i] * pieces[i] for i in range(5))
    odd = sum(mass_odd[i] * pieces[i] for i in range(1, 4))
    at_even = lax.broadcasted_iota(jnp.int32, even.shape, axis) % 2 == 0
    return jnp.where(at_even, even, odd)


def with_rows(x, width):
    size = lax.axis_size("vol")
    up = [(i, i + 1) for i in range(size - 1)]
    down = [(j, i) for i, j in up]
    before = lax.ppermute(x[-width:], "vol", up)
    after = lax.ppermute(x[:width], "vol", down)
    return jnp.concatenate([before, x, after], axis=0)


def stepwise(flux, metric):
    root = jnp.sqrt(metric)

    def dot(a, b):
        return lax.psum(jnp.sum(a * b), "vol")

    def step(_, state):
        solved, residual, direction, norm = state
        padded = jnp.pad(with_rows(root * direction, 2), ((0, 0), (2, 2)))
        image = root * mass_along(mass_along(padded, 1), 0)
        alpha = norm / dot(direction, image)
        solved = solved + alpha * direction
        residual = residual - alpha * image
        after = dot(residual, residual)
        direction = residual + after / norm * direction
        return solved, residual, direction, after

    state = (jnp.zeros_like(flux), flux, flux, dot(flux, flux))
    return with_rows(lax.fori_loop(0, ITERS, step, state)[0], DEEP)


def after(x, *others):
    return lax.optimization_barrier((x,) + others)[0]


def on_device(face_area, face_speed, face_node, face_count, surface_metric, displacement):
    vols, cols = lax.axis_size("vol"), lax.axis_size("col")
    vol, col = lax.axis_index("vol"), lax.axis_index("col")
    core = col % 2
    where = [core, col, jnp.int32(cols), vol, jnp.int32(vols), jnp.int32(displacement.shape[1])]
    where = jnp.stack(where).astype(jnp.int32).reshape(1, 6)
    up = [(i, i + 1) for i in range(vols - 1)]
    down = [(j, i) for i, j in up]
    col_up = [(i, i + 1) for i in range(cols - 1)]
    col_down = [(j, i) for i, j in col_up]
    packed = displacement.shape[0] * DEEP

    select = plain_selection()

    def moved(x, steps):
        dv, dc = steps
        pairs = [
            (i * cols + j, (i + dv) * cols + j + dc)
            for i in range(vols)
            for j in range(cols)
            if 0 <= i + dv < vols and 0 <= j + dc < cols
        ]
        return lax.ppermute(x, ("vol", "col"), pairs)

    keep, send, rows_up, rows_down = face_sums(
        where, face_count, face_area, face_speed, face_node, displacement, surface_metric
    )
    with jax.named_scope("flux_sum"):
        keep = keep + lax.ppermute(send, "col", [(j, j ^ 1) for j in range(cols)])
        turned = [
            lax.ppermute(keep, "col", [(j, (j + 2 * k) % cols) for j in range(cols)]) for k in (1, 2, 3)
        ]
    with jax.named_scope("row_halo"):
        rows_before, rows_after = moved(rows_up, (1, 0)), moved(rows_down, (-1, 0))
    wide, root = regroup(displacement, surface_metric, rows_before, rows_after)
    with jax.named_scope("flux_sum"):
        turned = lax.optimization_barrier((*turned, wide))
        own = (keep + turned[1]) + (turned[0] + turned[2])
    with jax.named_scope("flux_halo"):
        other = lax.ppermute(own, "col", [(j, j ^ 1) for j in range(cols)])
        pairs = []
        for i in range(vols):
            for j in range(cols):
                to = i - 1 if j % 2 == 0 else i + 1
                if 0 <= to < vols:
                    pairs.append((i * cols + j, to * cols + j))
        same = lax.ppermute(own, ("vol", "col"), pairs)
        cross = lax.ppermute(same, "col", [(j, j ^ 1) for j in range(cols)])

    with jax.named_scope("depth_halo"):
        sent = after(wide, own)
        zlow, zhigh = moved(sent, (0, 1)), moved(sent, (0, -1))
    basis, spread = surface_basis(where, vols, own, other, same, cross, root)
    with jax.named_scope("gather_sums"):
        gathered = lax.all_to_all(spread, "vol", 0, 0)
    factor = relaxation_factors(after(where, spread))
    speed, flag = surface_solve(basis, gathered)

    def finish(speed):
        change = surface_change(where, factor, speed, displacement.shape[0], displacement.shape[1])
        return base_sweeps(where, factor, wide, zlow, zhigh, change, speed, select)

    def step_by_step():
        low = jnp.where(core == 0, own, other)
        high = jnp.where(core == 0, other, own)
        flux = jnp.concatenate([low, high], axis=1)
        flux = flux.transpose(1, 2, 0).reshape(surface_metric.shape)
        solved = stepwise(flux, surface_metric)
        return finish(solved.reshape(Y_ROWS, LANES, 8).transpose(2, 0, 1))

    return lax.cond(flag[0, 0] > 0, lambda: finish(speed), step_by_step)


def solution(mesh):
    in_specs = (
        P("vol", "col"),
        P("vol", "col"),
        P("vol", "col"),
        P("vol", "col"),
        P("vol", None),
        P("col", "vol", None),
    )
    out_specs = (P("vol", None), P("col", "vol", None))
    return jax.shard_map(
        on_device, mesh=mesh, in_specs=in_specs, out_specs=out_specs, check_vma=False
    )
```

```python
import jax
import jax.numpy as jnp
import numpy as np
from jax import lax
from jax.experimental import pallas as pl
from jax.experimental.pallas import tpu as pltpu
from jax.sharding import PartitionSpec as P

ITERS = 10
SWEEPS = 4
LANES = 128
SUB = 8
MIB = 1024 * 1024
DEEP = 2 * SWEEPS
HALO = 32
ROWS = 128
GROUPS = 16
Y_GROUPS = 10
Y_ROWS = 80

BASIS_LOW = 0.1
BASIS_HIGH = 12.0
CONDITION_MAX = 2000.0


def rolled(x, shift, axis):
    return pltpu.roll(x, shift % x.shape[axis], axis)


def column_ring(tiles):
    n = len(tiles)
    lane = lax.broadcasted_iota(jnp.int32, tiles[0].shape, 1)
    first, last = lane == 0, lane == LANES - 1
    return (
        [jnp.where(first, 0.0, rolled(tiles[j], 1, 1)) for j in (n - 2, n - 1)]
        + list(tiles)
        + [jnp.where(last, 0.0, rolled(tiles[j], -1, 1)) for j in (0, 1)]
    )


def row_ring(rows):
    n = len(rows)
    return (
        [rolled(rows[j], 1, 0) for j in (n - 2, n - 1)]
        + list(rows)
        + [rolled(rows[j], -1, 0) for j in (0, 1)]
    )


def mass_line(padded, index):
    i = index + 2
    near = padded[i - 1] + padded[i + 1]
    if index % 2:
        return near + 4.0 * padded[i]
    return (near + 8.0 * padded[i]) - (padded[i - 2] + padded[i + 2])


def both_line(padded, index):
    i = index + 2
    near = padded[i - 1] + padded[i + 1]
    return (8.0 / 3.0 if index % 2 else 22.0 / 3.0) * padded[i] - near


def stored(parity):
    return 1.0 if parity else 0.5


def given(parity):
    return 0.5 if parity else 1.0


SMEM = pl.BlockSpec(memory_space=pltpu.SMEM)
VMEM = pl.BlockSpec(memory_space=pltpu.VMEM)
HBM = pl.BlockSpec(memory_space=pltpu.HBM)


def f32(*shape):
    return jax.ShapeDtypeStruct(shape, jnp.float32)


def params(mib):
    return pltpu.CompilerParams(vmem_limit_bytes=mib * MIB)


def cost(us):
    return pl.CostEstimate(flops=0, bytes_accessed=int(us * 100_000), transcendentals=0)


def split(x):
    first = x.astype(jnp.bfloat16)
    return first, (x - first.astype(jnp.float32)).astype(jnp.bfloat16)


def to_blocked(j):
    x = lax.broadcasted_iota(jnp.int32, (1024, 256), 0)
    n = lax.broadcasted_iota(jnp.int32, (1024, 256), 1)
    hit = x == 8 * (n & 127) + j + (n >> 7)
    return jnp.where(hit, 1.0, 0.0).astype(jnp.bfloat16)


def plain_selection():
    k = np.arange(1024)
    out = np.zeros((1024, 1024), np.float32)
    out[k, 8 * (k % LANES) + k // LANES] = 1.0
    return jnp.asarray(out, jnp.bfloat16)


def regroup_kernel(block_ref, metric_ref, before_ref, after_ref, wide_ref, root_ref, parts_ref):
    layers, rows, _ = block_ref.shape
    packed = DEEP * layers
    total = layers * Y_ROWS + ROWS

    def put(at, value):
        first, second = split(value)
        parts_ref[at : at + value.shape[0], :] = first
        parts_ref[total + at : total + at + value.shape[0], :] = second

    for z in range(layers):
        put(Y_ROWS * z, before_ref[DEEP * z : DEEP * (z + 1), :])
        put(Y_ROWS * z + DEEP, block_ref[z])
        put(Y_ROWS * z + DEEP + rows, after_ref[DEEP * z : DEEP * (z + 1), :])
    row = lax.broadcasted_iota(jnp.int32, (Y_ROWS, LANES), 0)
    by_row = jnp.where(row % 2 == 0, stored(0), stored(1)).astype(jnp.float32)
    at = layers * Y_ROWS
    put(at, jnp.sqrt(before_ref[packed:, :]))
    put(at + HALO, jnp.sqrt(metric_ref[...]))
    put(at + HALO + rows, jnp.sqrt(after_ref[packed:, :]))
    for j in range(0, 8, 2):
        pair = jnp.dot(parts_ref[...], to_blocked(j), preferred_element_type=jnp.float32)
        pair = pair[:total] + pair[total:]
        for i in range(2):
            tile = pair[:, LANES * i : LANES * (i + 1)]
            for z in range(layers):
                wide_ref[z, j + i] = tile[Y_ROWS * z : Y_ROWS * (z + 1)] * (by_row * (stored(z % 2) * stored(i)))
            root_ref[j + i] = tile[layers * Y_ROWS :]


def regroup(block, metric, before, after):
    layers, rows, cols = block.shape
    return pl.pallas_call(
        regroup_kernel,
        out_shape=(f32(layers, 8, Y_ROWS, LANES), f32(8, ROWS, LANES)),
        in_specs=[VMEM] * 4,
        out_specs=(VMEM, VMEM),
        scratch_shapes=[pltpu.VMEM((2 * (Y_ROWS * layers + ROWS), cols), jnp.bfloat16)],
        compiler_params=params(32),
        cost_estimate=cost(150),
        name="regroup",
    )(block, metric, before, after)


def plain_columns(select_ref, parts, rows, write):
    for q in range(4):
        at = slice(256 * q, 256 * (q + 1))
        value = jnp.dot(parts, select_ref[:, at], preferred_element_type=jnp.float32)
        write(at, value[:rows] + value[rows:])


def face_kernel(
    where_ref, count_ref, area_ref, speed_ref, node_ref, block_ref, metric_ref,
    keep_ref, send_ref, up_ref, down_ref, area, speed, nodes, acc_ref, sems,
):
    slots = area_ref.shape[1]
    fetches = [
        pltpu.make_async_copy(source, target, sems.at[i])
        for i, (source, target) in enumerate(((area_ref, area), (speed_ref, speed), (node_ref, nodes)))
    ]
    for fetch in fetches:
        fetch.start()
    layers, rows, _ = block_ref.shape
    copies = []
    for out_ref, row, root_row in ((up_ref, rows - DEEP, rows - HALO), (down_ref, 0, 0)):
        for z in range(layers):
            part = block_ref.at[z, pl.ds(row, DEEP), :]
            copies.append((part, out_ref.at[pl.ds(DEEP * z, DEEP), :]))
        part = metric_ref.at[pl.ds(root_row, HALO), :]
        copies.append((part, out_ref.at[pl.ds(DEEP * layers, HALO), :]))
    copies = [pltpu.make_async_copy(*pair, sems.at[i + 3]) for i, pair in enumerate(copies)]
    for copy in copies:
        copy.start()
    chunk = min(4096, slots)
    core = where_ref[0, 0]
    ids = lax.broadcasted_iota(jnp.int32, (256, chunk), 0)
    ids = ids.astype(jnp.float32).astype(jnp.bfloat16)
    zero = jnp.zeros((), jnp.bfloat16)
    one = jnp.ones((), jnp.bfloat16)
    contract = (((1,), (1,)), ((), ()))
    acc_ref[...] = jnp.zeros_like(acc_ref)
    for fetch in fetches:
        fetch.wait()

    def wide(x):
        return jnp.broadcast_to(x.astype(jnp.bfloat16), (256, chunk))

    def body(step, carry):
        at = pl.ds(pl.multiple_of(step * chunk, chunk), chunk)
        slot = lax.broadcasted_iota(jnp.int32, (1, chunk), 1) + step * chunk
        value = jnp.where(slot < count_ref[0, 0], area[:, at] * speed[:, at], 0.0)
        node = nodes[:, at]
        low = (((node & 1) << 7) + ((node >> 3) & 127)).astype(jnp.float32)
        high = (((node >> 1) & 3) * 64 + (node >> 10)).astype(jnp.float32)
        first = value.astype(jnp.bfloat16)
        second = value - first.astype(jnp.float32)
        here = wide(high) == ids
        upper = jnp.where(here, wide(first), zero)
        lower = jnp.where(here, wide(second), zero)
        columns = jnp.where(wide(low) == ids, one, zero)
        both = jnp.concatenate([upper, lower], axis=0)
        acc_ref[...] += lax.dot_general(both, columns, contract, preferred_element_type=jnp.float32)
        return carry

    lax.fori_loop(0, slots // chunk, body, 0)
    for j in range(8):
        at, lanes = 64 * (j // 2), slice(LANES * (j % 2), LANES * (j % 2 + 1))
        near, far = at + 32 * core, at + 32 - 32 * core
        keep_ref[j] = acc_ref[pl.ds(near, 32), lanes] + acc_ref[pl.ds(256 + near, 32), lanes]
        send_ref[j] = acc_ref[pl.ds(far, 32), lanes] + acc_ref[pl.ds(256 + far, 32), lanes]
    for copy in copies:
        copy.wait()


def face_sums(where, count, area, speed, node, block, metric):
    half = f32(8, 32, LANES)
    layers, _, cols = block.shape
    rows = f32(DEEP * layers + HALO, cols)
    return pl.pallas_call(
        face_kernel,
        out_shape=(half, half, rows, rows),
        in_specs=[SMEM, SMEM] + [HBM] * 5,
        out_specs=(VMEM, VMEM, VMEM, VMEM),
        scratch_shapes=[
            pltpu.VMEM(area.shape, jnp.float32),
            pltpu.VMEM(area.shape, jnp.float32),
            pltpu.VMEM(area.shape, jnp.int32),
            pltpu.VMEM((512, 256), jnp.float32),
            pltpu.SemaphoreType.DMA((2 * layers + 5,)),
        ],
        compiler_params=params(56),
        cost_estimate=cost(7),
        name="face_sums",
    )(where, count, area, speed, node, block, metric)


def basis_kernel(
    where_ref, own_ref, other_ref, same_ref, cross_ref, root_ref,
    field, sums_ref, rows, root, outer, line, partial,
):
    core = where_ref[0, 0]
    centre = (BASIS_LOW + BASIS_HIGH) / 2
    scale = 2 / (BASIS_HIGH - BASIS_LOW)
    for t in range(8):
        rows[t, pl.ds(32 + 32 * core, 32), :] = own_ref[t]
        rows[t, pl.ds(64 - 32 * core, 32), :] = other_ref[t]
        rows[t, pl.ds(96 * core, 32), :] = cross_ref[t]
        rows[t, pl.ds(96 - 96 * core, 32), :] = same_ref[t]
    for t in range(8):
        for ys in range(GROUPS):
            field[0, t, ys] = rows[t, pl.ds(ys, SUB, stride=GROUPS), :]
            value = root_ref[t, pl.ds(ys, SUB, stride=GROUPS), :]
            root[t, ys] = value * (stored(t % 2) * stored(ys % 2))
            outer[t, ys] = value * (2 * scale * 4.0 / 225.0 / (given(t % 2) * given(ys % 2)))

    group = lax.broadcasted_iota(jnp.int32, (SUB, LANES), 0)
    own_rows = jnp.where((group >= 2) & (group < 6), 1.0, 0.0).astype(jnp.float32)

    def step(k, begin, end):
        def put(k, t, ys, value):
            if not end:
                field[k, t, ys] = value

        for ys in range(GROUPS):
            padded = column_ring([field[k, t, ys] * root[t, ys] for t in range(8)])
            for t in range(8):
                line[ys, t] = mass_line(padded, t)
        squares, shifts = [], []
        for t in range(8):
            square = jnp.zeros((SUB, LANES), jnp.float32)
            shifted = jnp.zeros((SUB, LANES), jnp.float32)
            padded = row_ring([line[ys, t] for ys in range(GROUPS)])
            for ys in range(GROUPS):
                now = field[k, t, ys]
                later = outer[t, ys] * mass_line(padded, ys) - (2 * centre * scale) * now
                later = 0.5 * later if begin else later - field[k - 1, t, ys]
                put(k + 1, t, ys, later)
                square = square + now * now
                shifted = shifted + later * now
            squares.append(square)
            shifts.append(shifted)

        def add(parts):
            while len(parts) > 1:
                parts = [parts[i] + parts[i + 1] for i in range(0, len(parts), 2)]
            return jnp.sum(parts[0] * own_rows, axis=0, keepdims=True)

        partial[pl.ds(2 * k, 1), :] = add(squares)
        partial[pl.ds(2 * k + 1, 1), :] = add(shifts)

    def later_step(k, carry):
        step(k, False, False)
        return carry

    partial[...] = jnp.zeros_like(partial)
    step(0, True, False)
    lax.fori_loop(1, ITERS - 1, later_step, 0)
    step(ITERS - 1, False, True)
    whole = jnp.sum(partial[...], axis=1, keepdims=True)
    row = lax.broadcasted_iota(jnp.int32, partial.shape, 0)
    lane = lax.broadcasted_iota(jnp.int32, partial.shape, 1)
    line_of = jnp.sum(jnp.where(row == lane, whole, 0.0), axis=0, keepdims=True)
    sums_ref[...] = jnp.broadcast_to(line_of[None], sums_ref.shape)


def surface_basis(where, vols, own, other, same, cross, root):
    return pl.pallas_call(
        basis_kernel,
        out_shape=(f32(ITERS, 8, GROUPS, SUB, LANES), f32(vols, SUB, LANES)),
        in_specs=[SMEM] + [VMEM] * 5,
        out_specs=(VMEM, VMEM),
        scratch_shapes=[
            pltpu.VMEM((8, ROWS, LANES), jnp.float32),
            pltpu.VMEM((8, GROUPS, SUB, LANES), jnp.float32),
            pltpu.VMEM((8, GROUPS, SUB, LANES), jnp.float32),
            pltpu.VMEM((GROUPS, 8, SUB, LANES), jnp.float32),
            pltpu.VMEM((24, LANES), jnp.float32),
        ],
        compiler_params=params(24),
        cost_estimate=cost(7),
        name="surface_basis",
    )(where, own, other, same, cross, root)


def solve_weights():
    n = ITERS
    moment = np.zeros((2 * n, 2 * n))
    for m in range(2 * n):
        if m < 2:
            moment[m, m] = 1.0
        else:
            moment[m, m] = 2.0
            moment[m, m % 2] = -1.0
    centre, half = (BASIS_LOW + BASIS_HIGH) / 2, (BASIS_HIGH - BASIS_LOW) / 2
    weights = np.zeros((2 * n, 16, LANES))
    for i in range(n):
        for j in range(n):
            lower = abs(j - 1)
            for factor, index in (
                (centre / 2, i + j),
                (centre / 2, abs(i - j)),
                (half / 4, i + j + 1),
                (half / 4, abs(i - j - 1)),
                (half / 4, i + lower),
                (half / 4, abs(i - lower)),
            ):
                weights[:, i, j] += factor * moment[index]
        weights[:, i, n] += moment[i]
    return weights.astype(np.float32)


def solve_kernel(part_ref, sums_ref, weights_ref, out_ref, flag_ref, rows):
    n = ITERS
    total = sums_ref[0]
    for i in range(1, sums_ref.shape[0]):
        total = total + sums_ref[i]
    row = lax.broadcasted_iota(jnp.int32, (16, LANES), 0)
    lane = lax.broadcasted_iota(jnp.int32, (16, LANES), 1)
    system = jnp.where((lane == row + 16) & (row < n), 1.0, 0.0).astype(jnp.float32)
    for m in range(2 * n):
        system = system + weights_ref[m] * total[0:1, m : m + 1]
    centre = jnp.sum(jnp.where(lane == row, system, 0.0), axis=1, keepdims=True)
    for k in range(n):
        pivot_row = system[k : k + 1, :] / system[k : k + 1, k : k + 1]
        column = system[:, k : k + 1]
        system = jnp.where(row == k, pivot_row, system - column * pivot_row)
    inverse = jnp.sum(jnp.where(lane == row + 16, system, 0.0), axis=1, keepdims=True)
    figure = jnp.broadcast_to(centre * inverse, (16, LANES))
    inside = (row < n) & (lane == 0)
    least = jnp.min(jnp.where(inside, figure, 1.0))
    whole = jnp.sum(jnp.where(inside, figure, 0.0))
    flag_ref[0, 0] = jnp.where((least > 0.5) & (whole < CONDITION_MAX), 1, 0).astype(jnp.int32)
    weights = [jnp.broadcast_to(system[k : k + 1, n : n + 1], (SUB, LANES)) for k in range(n)]
    for t in range(8):
        for ys in range(GROUPS):
            value = weights[0] * part_ref[0, t, ys]
            for k in range(1, n):
                value = value + weights[k] * part_ref[k, t, ys]
            rows[t, pl.ds(ys, SUB, stride=GROUPS), :] = value
        out_ref[t] = rows[t, HALO - DEEP : HALO - DEEP + Y_ROWS, :]


def surface_solve(basis, sums):
    return pl.pallas_call(
        solve_kernel,
        out_shape=(f32(8, Y_ROWS, LANES), jax.ShapeDtypeStruct((1, 1), jnp.int32)),
        in_specs=[VMEM, VMEM, VMEM],
        out_specs=(VMEM, SMEM),
        scratch_shapes=[pltpu.VMEM((8, ROWS, LANES), jnp.float32)],
        compiler_params=params(24),
        cost_estimate=cost(3),
        name="surface_solve",
    )(basis, sums, jnp.asarray(solve_weights()))


def factor_kernel(where_ref, factor):
    vol, vols, rows = where_ref[0, 3], where_ref[0, 4], where_ref[0, 5]
    group = lax.broadcasted_iota(jnp.int32, (SUB, LANES), 0)
    mass, stiff = (8.0, 16.0), (14.0, 16.0)
    for ys in range(Y_GROUPS):
        row = group * Y_GROUPS + ys
        outside = ((vol == 0) & (row < DEEP)) | ((vol == vols - 1) & (row >= DEEP + rows))
        py = ys % 2
        for pz in range(2):
            for px in range(2):
                value = -12.0 / (
                    stiff[pz] * mass[py] * mass[px]
                    + mass[pz] * (stiff[py] * mass[px] + mass[py] * stiff[px])
                )
                for p in (pz, py, px):
                    value = value * stored(p) / given(p)
                factor[pz, px, ys] = jnp.where(outside, 0.0, jnp.float32(value))


def relaxation_factors(where):
    return pl.pallas_call(
        factor_kernel,
        out_shape=f32(2, 2, Y_GROUPS, SUB, LANES),
        in_specs=[SMEM],
        out_specs=VMEM,
        compiler_params=params(16),
        cost_estimate=cost(1),
        name="relaxation_factors",
    )(where)


def lateral_lines(get, line_a, line_b, put):
    for t in range(8):
        u = row_ring([get(t, ys) for ys in range(Y_GROUPS)])
        for ys in range(Y_GROUPS):
            m = mass_line(u, ys)
            line_a[t, ys] = m
            line_b[t, ys] = both_line(u, ys) - m
    for ys in range(Y_GROUPS):
        a = column_ring([line_a[t, ys] for t in range(8)])
        b = column_ring([line_b[t, ys] for t in range(8)])
        for t in range(8):
            put(t, ys, mass_line(a, t), both_line(a, t) + mass_line(b, t))


def even_step(w, c):
    near = c[1] + c[3]
    return (22.0 / 3.0 * w[1] - (w[0] + w[2])) + ((near + 8.0 * c[2]) - (c[0] + c[4]))


def odd_step(w, c):
    return (8.0 / 3.0 * w[1] - (w[0] + w[2])) + ((c[0] + c[2]) + 4.0 * c[1])


def strided(ys):
    return pl.ds(ys, SUB, stride=Y_GROUPS)


def change_kernel(
    where_ref, factor, speed_ref, out_ref, cells, along, cross, line_a, line_b, plain, sems,
):
    col = where_ref[0, 1]
    layers, _, rows, _ = out_ref.shape

    def lateral(z, carry):
        def put(t, ys, w, c):
            along[z, t, ys] = w
            cross[z, t, ys] = c

        lateral_lines(lambda t, ys: cells[z, t, ys], line_a, line_b, put)
        return carry

    def set_top():
        for t in range(8):
            for ys in range(Y_GROUPS):
                scale = 0.5 * stored(0) * stored(t % 2) * stored(ys % 2)
                cells[2, t, ys] = scale * speed_ref[t, strided(ys), :]

    def send(first, count):
        copies = []
        for z in range(first, first + count):
            for t in range(8):
                for ys in range(Y_GROUPS):
                    plain[z, t, strided(ys), :] = cells[z + 2, t, ys]
            copy = pltpu.make_async_copy(
                plain.at[z, :, pl.ds(DEEP, rows), :], out_ref.at[z], sems.at[z]
            )
            copy.start()
            copies.append(copy)
        for copy in copies:
            copy.wait()

    @pl.when(col == 0)
    def _():
        set_top()
        clear = jnp.zeros((8, Y_GROUPS, SUB, LANES), jnp.float32)
        for z in range(2):
            cross[z] = clear
            along[z] = clear

        def update(pair, carry):
            z = 2 * pair + 2
            for ys in range(Y_GROUPS):
                factors = [[factor[pz, px, ys] for px in range(2)] for pz in range(2)]
                for t in range(8):
                    w = [along[z + i, t, ys] for i in range(-1, 3)]
                    c = [cross[z + i, t, ys] for i in range(-2, 3)]
                    cells[z, t, ys] += factors[0][t % 2] * even_step(w, c)
                    cells[z + 1, t, ys] += factors[1][t % 2] * odd_step(w[1:], c[2:])
            return carry

        def one_sweep(sweep, carry):
            front = 2 * sweep + 2
            lax.fori_loop(2, front + 1, lateral, 0)
            lax.fori_loop(0, sweep, update, 0)
            for ys in range(Y_GROUPS):
                factors = [[factor[pz, px, ys] for px in range(2)] for pz in range(2)]
                for t in range(8):
                    w0, w1 = along[front - 1, t, ys], along[front, t, ys]
                    c0, c1, c2 = [cross[front + i, t, ys] for i in range(-2, 1)]
                    step = (22.0 / 3.0 * w1 - w0) + ((c1 + 8.0 * c2) - c0)
                    cells[front, t, ys] += factors[0][t % 2] * step
                    cells[front + 1, t, ys] = factors[1][t % 2] * (c2 - w1)
                    cells[front + 2, t, ys] = -factors[0][t % 2] * c2
            set_top()
            return carry

        lax.fori_loop(0, SWEEPS, one_sweep, 0)
        send(1, layers - 1)

    @pl.when(col == 1)
    def _():
        set_top()

        def one_sweep(sweep, carry):
            lateral(2, 0)
            for t in range(8):
                for ys in range(Y_GROUPS):
                    cells[2, t, ys] = -factor[0, t % 2, ys] * cross[2, t, ys]
            return carry

        lax.fori_loop(0, SWEEPS, one_sweep, 0)
        send(0, 1)


def surface_change(where, factor, speed, layers, rows):
    work = pltpu.VMEM((layers + 2, 8, Y_GROUPS, SUB, LANES), jnp.float32)
    line = pltpu.VMEM((8, Y_GROUPS, SUB, LANES), jnp.float32)
    return pl.pallas_call(
        change_kernel,
        out_shape=f32(layers, 8, rows, LANES),
        in_specs=[SMEM, VMEM, VMEM],
        out_specs=HBM,
        scratch_shapes=[
            pltpu.VMEM((layers + 3, 8, Y_GROUPS, SUB, LANES), jnp.float32),
            work, work, line, line,
            pltpu.VMEM((layers, 8, Y_ROWS, LANES), jnp.float32),
            pltpu.SemaphoreType.DMA((layers,)),
        ],
        compiler_params=params(32),
        cost_estimate=cost(8),
        name="surface_change",
    )(where, factor, speed)


def base_kernel(
    where_ref, factor, wide_ref, zlow_ref, zhigh_ref, change_ref, speed_ref, select_ref,
    velocity_ref, out_ref, field, along, cross, line_a, line_b, change, parts, sems,
):
    col, cols = where_ref[0, 1], where_ref[0, 2]
    layers, _, rows, _ = change_ref.shape
    total = layers + 2 * DEEP
    own = pltpu.make_async_copy(wide_ref, field.at[pl.ds(DEEP, layers)], sems.at[0])
    low = pltpu.make_async_copy(zlow_ref, field.at[pl.ds(0, DEEP)], sems.at[1])
    high = pltpu.make_async_copy(zhigh_ref, field.at[pl.ds(DEEP + layers, DEEP)], sems.at[2])
    all_change = pltpu.make_async_copy(
        change_ref.at[pl.ds(1, layers - 1)], change.at[pl.ds(1, layers - 1)], sems.at[3]
    )
    one_change = pltpu.make_async_copy(
        change_ref.at[pl.ds(0, 1)], change.at[pl.ds(0, 1)], sems.at[4]
    )
    own.start()
    low.start()
    high.start()
    pl.when(col == 0)(all_change.start)
    pl.when(col == 1)(one_change.start)
    count = (layers + 1) * rows

    def cut(value, at, t):
        first, second = split(value)
        lanes = slice(LANES * t, LANES * (t + 1))
        parts[at : at + rows, lanes] = first
        parts[count + at : count + at + rows, lanes] = second

    for t in range(8):
        cut(speed_ref[t, DEEP : DEEP + rows, :], 0, t)

    def lateral(z, carry):
        def put(t, ys, w, c):
            along[z, t, ys] = w
            cross[z, t, ys] = c

        lateral_lines(lambda t, ys: field[z, t, strided(ys), :], line_a, line_b, put)
        return carry

    def update(pair, carry):
        z = 2 * pair
        for ys in range(Y_GROUPS):
            factors = [[factor[pz, px, ys] for px in range(2)] for pz in range(2)]
            for t in range(8):
                w = [along[z + i, t, ys] for i in range(-1, 3)]
                c = [cross[z + i, t, ys] for i in range(-2, 3)]
                even, odd = even_step(w, c), odd_step(w[1:], c[2:])
                scale = jnp.where((col == 0) & (z == DEEP), 0.0, factors[0][t % 2])
                even = field[z, t, strided(ys), :] + scale * even
                odd = field[z + 1, t, strided(ys), :] + factors[1][t % 2] * odd
                field[z, t, strided(ys), :] = even
                field[z + 1, t, strided(ys), :] = odd
        return carry

    begin = jnp.where(col == 0, DEEP, 0)
    end = jnp.where(col == cols - 1, DEEP + layers + 1, total - 1)

    def one_sweep(sweep, carry):
        first = jnp.maximum(begin, 2 * sweep)
        last = jnp.minimum(end, total - 2 * sweep - 1)

        @pl.when(sweep == 0)
        def _():
            own.wait()

        lax.fori_loop(jnp.where(sweep == 0, DEEP, first), jnp.where(sweep == 0, DEEP + layers, last), lateral, 0)

        @pl.when(sweep == 0)
        def _():
            low.wait()
            high.wait()

        lax.fori_loop(jnp.where(sweep == 0, first, DEEP), DEEP, lateral, 0)
        lax.fori_loop(jnp.where(sweep == 0, DEEP + layers, last), last, lateral, 0)
        low_pair = jnp.where(col == 0, DEEP // 2, sweep + 1)
        high_pair = jnp.where(col == cols - 1, (DEEP + layers) // 2, total // 2 - sweep - 1)
        lax.fori_loop(low_pair, high_pair, update, 0)
        return carry

    @pl.when(col == 0)
    def _():
        clear = jnp.zeros((8, Y_GROUPS, SUB, LANES), jnp.float32)
        for z in (DEEP - 2, DEEP - 1):
            along[z] = clear
            cross[z] = clear

    lax.fori_loop(0, SWEEPS, one_sweep, 0)

    row = lax.broadcasted_iota(jnp.int32, (rows, LANES), 0)
    by_row = jnp.where(row % 2 == 0, stored(0), stored(1)).astype(jnp.float32)
    back_row = jnp.where(row % 2 == 0, 1 / stored(0), 1 / stored(1)).astype(jnp.float32)

    @pl.when(col == 0)
    def _():
        all_change.wait()
        for t in range(8):
            top = speed_ref[t, DEEP : DEEP + rows, :] * (by_row * (0.5 * stored(0) * stored(t % 2)))
            field[DEEP, t, DEEP : DEEP + rows, :] += top
            for z in range(1, layers):
                field[DEEP + z, t, DEEP : DEEP + rows, :] += change[z, t]

    @pl.when(col == 1)
    def _():
        one_change.wait()
        for t in range(8):
            field[DEEP, t, DEEP : DEEP + rows, :] += change[0, t]

    for z in range(layers):
        for t in range(8):
            value = field[DEEP + z, t, DEEP : DEEP + rows, :]
            cut(value * (back_row * (1 / (stored(z % 2) * stored(t % 2)))), rows * (z + 1), t)

    def write(at, value):
        velocity_ref[:, at] = value[:rows]
        out_ref[:, :, at] = value[rows:].reshape(layers, rows, 256)

    plain_columns(select_ref, parts[...], count, write)


def base_sweeps(where, factor, wide, zlow, zhigh, change, speed, select):
    layers, _, rows, _ = change.shape
    total = layers + 2 * DEEP
    work = pltpu.VMEM((total, 8, Y_GROUPS, SUB, LANES), jnp.float32)
    line = pltpu.VMEM((8, Y_GROUPS, SUB, LANES), jnp.float32)
    return pl.pallas_call(
        base_kernel,
        out_shape=(f32(rows, 8 * LANES), f32(layers, rows, 8 * LANES)),
        in_specs=[SMEM, VMEM] + [HBM] * 4 + [VMEM] * 2,
        out_specs=(VMEM, VMEM),
        scratch_shapes=[
            pltpu.VMEM((total, 8, Y_ROWS, LANES), jnp.float32),
            work, work, line, line,
            pltpu.VMEM((layers, 8, rows, LANES), jnp.float32),
            pltpu.VMEM((2 * (layers + 1) * rows, 8 * LANES), jnp.bfloat16),
            pltpu.SemaphoreType.DMA((5,)),
        ],
        compiler_params=params(50),
        cost_estimate=cost(25),
        name="base_sweeps",
    )(where, factor, wide, zlow, zhigh, change, speed, select)


mass_even = (-1.0 / 15.0, 2.0 / 15.0, 8.0 / 15.0, 2.0 / 15.0, -1.0 / 15.0)
mass_odd = (0.0, 2.0 / 15.0, 16.0 / 15.0, 2.0 / 15.0, 0.0)


def mass_along(padded, axis):
    count = padded.shape[axis] - 4
    pieces = [lax.slice_in_dim(padded, i, i + count, axis=axis) for i in range(5)]
    even = sum(mass_even[i] * pieces[i] for i in range(5))
    odd = sum(mass_odd[i] * pieces[i] for i in range(1, 4))
    at_even = lax.broadcasted_iota(jnp.int32, even.shape, axis) % 2 == 0
    return jnp.where(at_even, even, odd)


def with_rows(x, width):
    size = lax.axis_size("vol")
    up = [(i, i + 1) for i in range(size - 1)]
    down = [(j, i) for i, j in up]
    before = lax.ppermute(x[-width:], "vol", up)
    after = lax.ppermute(x[:width], "vol", down)
    return jnp.concatenate([before, x, after], axis=0)


def stepwise(flux, metric):
    root = jnp.sqrt(metric)

    def dot(a, b):
        return lax.psum(jnp.sum(a * b), "vol")

    def step(_, state):
        solved, residual, direction, norm = state
        padded = jnp.pad(with_rows(root * direction, 2), ((0, 0), (2, 2)))
        image = root * mass_along(mass_along(padded, 1), 0)
        alpha = norm / dot(direction, image)
        solved = solved + alpha * direction
        residual = residual - alpha * image
        after = dot(residual, residual)
        direction = residual + after / norm * direction
        return solved, residual, direction, after

    state = (jnp.zeros_like(flux), flux, flux, dot(flux, flux))
    return with_rows(lax.fori_loop(0, ITERS, step, state)[0], DEEP)


def after(x, *others):
    return lax.optimization_barrier((x,) + others)[0]


def on_device(face_area, face_speed, face_node, face_count, surface_metric, displacement):
    vols, cols = lax.axis_size("vol"), lax.axis_size("col")
    vol, col = lax.axis_index("vol"), lax.axis_index("col")
    core = col % 2
    where = [core, col, jnp.int32(cols), vol, jnp.int32(vols), jnp.int32(displacement.shape[1])]
    where = jnp.stack(where).astype(jnp.int32).reshape(1, 6)
    up = [(i, i + 1) for i in range(vols - 1)]
    down = [(j, i) for i, j in up]
    col_up = [(i, i + 1) for i in range(cols - 1)]
    col_down = [(j, i) for i, j in col_up]
    packed = displacement.shape[0] * DEEP

    select = plain_selection()

    def moved(x, steps):
        dv, dc = steps
        pairs = [
            (i * cols + j, (i + dv) * cols + j + dc)
            for i in range(vols)
            for j in range(cols)
            if 0 <= i + dv < vols and 0 <= j + dc < cols
        ]
        return lax.ppermute(x, ("vol", "col"), pairs)

    keep, send, rows_up, rows_down = face_sums(
        where, face_count, face_area, face_speed, face_node, displacement, surface_metric
    )
    with jax.named_scope("flux_sum"):
        keep = keep + lax.ppermute(send, "col", [(j, j ^ 1) for j in range(cols)])
        turned = [
            lax.ppermute(keep, "col", [(j, (j + 2 * k) % cols) for j in range(cols)]) for k in (1, 2, 3)
        ]
        own = (keep + turned[1]) + (turned[0] + turned[2])
    with jax.named_scope("row_halo"):
        rows_before, rows_after = moved(after(rows_up, keep), (1, 0)), moved(after(rows_down, keep), (-1, 0))
    wide, root = regroup(displacement, surface_metric, after(rows_before, own), rows_after)
    with jax.named_scope("flux_halo"):
        other = lax.ppermute(own, "col", [(j, j ^ 1) for j in range(cols)])
        pairs = []
        for i in range(vols):
            for j in range(cols):
                to = i - 1 if j % 2 == 0 else i + 1
                if 0 <= to < vols:
                    pairs.append((i * cols + j, to * cols + j))
        same = lax.ppermute(own, ("vol", "col"), pairs)
        cross = lax.ppermute(same, "col", [(j, j ^ 1) for j in range(cols)])

    with jax.named_scope("depth_halo"):
        zlow, zhigh = moved(wide, (0, 1)), moved(wide, (0, -1))
    basis, spread = surface_basis(where, vols, own, other, same, cross, root)
    with jax.named_scope("gather_sums"):
        gathered = lax.all_to_all(spread, "vol", 0, 0)
    factor = relaxation_factors(after(where, own))
    speed, flag = surface_solve(basis, gathered)

    def finish(speed):
        change = surface_change(where, factor, speed, displacement.shape[0], displacement.shape[1])
        return base_sweeps(where, factor, wide, zlow, zhigh, change, speed, select)

    def step_by_step():
        low = jnp.where(core == 0, own, other)
        high = jnp.where(core == 0, other, own)
        flux = jnp.concatenate([low, high], axis=1)
        flux = flux.transpose(1, 2, 0).reshape(surface_metric.shape)
        solved = stepwise(flux, surface_metric)
        return finish(solved.reshape(Y_ROWS, LANES, 8).transpose(2, 0, 1))

    return lax.cond(flag[0, 0] > 0, lambda: finish(speed), step_by_step)


def solution(mesh):
    in_specs = (
        P("vol", "col"),
        P("vol", "col"),
        P("vol", "col"),
        P("vol", "col"),
        P("vol", None),
        P("col", "vol", None),
    )
    out_specs = (P("vol", None), P("col", "vol", None))
    return jax.shard_map(
        on_device, mesh=mesh, in_specs=in_specs, out_specs=out_specs, check_vma=False
    )
```

```python
import jax
import jax.numpy as jnp
import numpy as np
from jax import lax
from jax.experimental import pallas as pl
from jax.experimental.pallas import tpu as pltpu
from jax.sharding import PartitionSpec as P

ITERS = 10
SWEEPS = 4
LANES = 128
SUB = 8
MIB = 1024 * 1024
DEEP = 2 * SWEEPS
HALO = 32
ROWS = 128
GROUPS = 16
Y_GROUPS = 10
Y_ROWS = 80

BASIS_LOW = 0.1
BASIS_HIGH = 12.0
CONDITION_MAX = 2000.0


def rolled(x, shift, axis):
    return pltpu.roll(x, shift % x.shape[axis], axis)


def column_ring(tiles):
    n = len(tiles)
    lane = lax.broadcasted_iota(jnp.int32, tiles[0].shape, 1)
    first, last = lane == 0, lane == LANES - 1
    return (
        [jnp.where(first, 0.0, rolled(tiles[j], 1, 1)) for j in (n - 2, n - 1)]
        + list(tiles)
        + [jnp.where(last, 0.0, rolled(tiles[j], -1, 1)) for j in (0, 1)]
    )


def row_ring(rows):
    n = len(rows)
    return (
        [rolled(rows[j], 1, 0) for j in (n - 2, n - 1)]
        + list(rows)
        + [rolled(rows[j], -1, 0) for j in (0, 1)]
    )


def mass_line(padded, index):
    i = index + 2
    near = padded[i - 1] + padded[i + 1]
    if index % 2:
        return near + 4.0 * padded[i]
    return (near + 8.0 * padded[i]) - (padded[i - 2] + padded[i + 2])


def both_line(padded, index):
    i = index + 2
    near = padded[i - 1] + padded[i + 1]
    return (8.0 / 3.0 if index % 2 else 22.0 / 3.0) * padded[i] - near


def stored(parity):
    return 1.0 if parity else 0.5


def given(parity):
    return 0.5 if parity else 1.0


SMEM = pl.BlockSpec(memory_space=pltpu.SMEM)
VMEM = pl.BlockSpec(memory_space=pltpu.VMEM)
HBM = pl.BlockSpec(memory_space=pltpu.HBM)


def f32(*shape):
    return jax.ShapeDtypeStruct(shape, jnp.float32)


def params(mib):
    return pltpu.CompilerParams(vmem_limit_bytes=mib * MIB)


def cost(us):
    return pl.CostEstimate(flops=0, bytes_accessed=int(us * 100_000), transcendentals=0)


def split(x):
    first = x.astype(jnp.bfloat16)
    return first, (x - first.astype(jnp.float32)).astype(jnp.bfloat16)


def to_blocked(j):
    x = lax.broadcasted_iota(jnp.int32, (1024, 256), 0)
    n = lax.broadcasted_iota(jnp.int32, (1024, 256), 1)
    hit = x == 8 * (n & 127) + j + (n >> 7)
    return jnp.where(hit, 1.0, 0.0).astype(jnp.bfloat16)


def plain_selection():
    k = np.arange(1024)
    out = np.zeros((1024, 1024), np.float32)
    out[k, 8 * (k % LANES) + k // LANES] = 1.0
    return jnp.asarray(out, jnp.bfloat16)


def regroup_kernel(block_ref, metric_ref, before_ref, after_ref, wide_ref, root_ref, parts_ref):
    layers, rows, _ = block_ref.shape
    packed = DEEP * layers
    total = layers * Y_ROWS + ROWS

    def put(at, value):
        first, second = split(value)
        parts_ref[at : at + value.shape[0], :] = first
        parts_ref[total + at : total + at + value.shape[0], :] = second

    for z in range(layers):
        put(Y_ROWS * z, before_ref[DEEP * z : DEEP * (z + 1), :])
        put(Y_ROWS * z + DEEP, block_ref[z])
        put(Y_ROWS * z + DEEP + rows, after_ref[DEEP * z : DEEP * (z + 1), :])
    row = lax.broadcasted_iota(jnp.int32, (Y_ROWS, LANES), 0)
    by_row = jnp.where(row % 2 == 0, stored(0), stored(1)).astype(jnp.float32)
    at = layers * Y_ROWS
    put(at, jnp.sqrt(before_ref[packed:, :]))
    put(at + HALO, jnp.sqrt(metric_ref[...]))
    put(at + HALO + rows, jnp.sqrt(after_ref[packed:, :]))
    for j in range(0, 8, 2):
        pair = jnp.dot(parts_ref[...], to_blocked(j), preferred_element_type=jnp.float32)
        pair = pair[:total] + pair[total:]
        for i in range(2):
            tile = pair[:, LANES * i : LANES * (i + 1)]
            for z in range(layers):
                wide_ref[z, j + i] = tile[Y_ROWS * z : Y_ROWS * (z + 1)] * (by_row * (stored(z % 2) * stored(i)))
            root_ref[j + i] = tile[layers * Y_ROWS :]


def regroup(block, metric, before, after):
    layers, rows, cols = block.shape
    return pl.pallas_call(
        regroup_kernel,
        out_shape=(f32(layers, 8, Y_ROWS, LANES), f32(8, ROWS, LANES)),
        in_specs=[VMEM] * 4,
        out_specs=(VMEM, VMEM),
        scratch_shapes=[pltpu.VMEM((2 * (Y_ROWS * layers + ROWS), cols), jnp.bfloat16)],
        compiler_params=params(32),
        cost_estimate=cost(150),
        name="regroup",
    )(block, metric, before, after)


def plain_columns(select_ref, parts, rows, write):
    for q in range(4):
        at = slice(256 * q, 256 * (q + 1))
        value = jnp.dot(parts, select_ref[:, at], preferred_element_type=jnp.float32)
        write(at, value[:rows] + value[rows:])


def face_kernel(
    where_ref, count_ref, area_ref, speed_ref, node_ref, block_ref, metric_ref,
    keep_ref, send_ref, up_ref, down_ref, area, speed, nodes, acc_ref, sems,
):
    slots = area_ref.shape[1]
    fetches = [
        pltpu.make_async_copy(source, target, sems.at[i])
        for i, (source, target) in enumerate(((area_ref, area), (speed_ref, speed), (node_ref, nodes)))
    ]
    for fetch in fetches:
        fetch.start()
    layers, rows, _ = block_ref.shape
    copies = []
    for out_ref, row, root_row in ((up_ref, rows - DEEP, rows - HALO), (down_ref, 0, 0)):
        for z in range(layers):
            part = block_ref.at[z, pl.ds(row, DEEP), :]
            copies.append((part, out_ref.at[pl.ds(DEEP * z, DEEP), :]))
        part = metric_ref.at[pl.ds(root_row, HALO), :]
        copies.append((part, out_ref.at[pl.ds(DEEP * layers, HALO), :]))
    copies = [pltpu.make_async_copy(*pair, sems.at[i + 3]) for i, pair in enumerate(copies)]
    for copy in copies:
        copy.start()
    chunk = min(4096, slots)
    core = where_ref[0, 0]
    ids = lax.broadcasted_iota(jnp.int32, (256, chunk), 0)
    ids = ids.astype(jnp.float32).astype(jnp.bfloat16)
    zero = jnp.zeros((), jnp.bfloat16)
    one = jnp.ones((), jnp.bfloat16)
    contract = (((1,), (1,)), ((), ()))
    acc_ref[...] = jnp.zeros_like(acc_ref)
    for fetch in fetches:
        fetch.wait()

    def wide(x):
        return jnp.broadcast_to(x.astype(jnp.bfloat16), (256, chunk))

    def body(step, carry):
        at = pl.ds(pl.multiple_of(step * chunk, chunk), chunk)
        slot = lax.broadcasted_iota(jnp.int32, (1, chunk), 1) + step * chunk
        value = jnp.where(slot < count_ref[0, 0], area[:, at] * speed[:, at], 0.0)
        node = nodes[:, at]
        low = (((node & 1) << 7) + ((node >> 3) & 127)).astype(jnp.float32)
        high = (((node >> 1) & 3) * 64 + (node >> 10)).astype(jnp.float32)
        first = value.astype(jnp.bfloat16)
        second = value - first.astype(jnp.float32)
        here = wide(high) == ids
        upper = jnp.where(here, wide(first), zero)
        lower = jnp.where(here, wide(second), zero)
        columns = jnp.where(wide(low) == ids, one, zero)
        both = jnp.concatenate([upper, lower], axis=0)
        acc_ref[...] += lax.dot_general(both, columns, contract, preferred_element_type=jnp.float32)
        return carry

    lax.fori_loop(0, slots // chunk, body, 0)
    for j in range(8):
        at, lanes = 64 * (j // 2), slice(LANES * (j % 2), LANES * (j % 2 + 1))
        near, far = at + 32 * core, at + 32 - 32 * core
        keep_ref[j] = acc_ref[pl.ds(near, 32), lanes] + acc_ref[pl.ds(256 + near, 32), lanes]
        send_ref[j] = acc_ref[pl.ds(far, 32), lanes] + acc_ref[pl.ds(256 + far, 32), lanes]
    for copy in copies:
        copy.wait()


def face_sums(where, count, area, speed, node, block, metric):
    half = f32(8, 32, LANES)
    layers, _, cols = block.shape
    rows = f32(DEEP * layers + HALO, cols)
    return pl.pallas_call(
        face_kernel,
        out_shape=(half, half, rows, rows),
        in_specs=[SMEM, SMEM] + [HBM] * 5,
        out_specs=(VMEM, VMEM, VMEM, VMEM),
        scratch_shapes=[
            pltpu.VMEM(area.shape, jnp.float32),
            pltpu.VMEM(area.shape, jnp.float32),
            pltpu.VMEM(area.shape, jnp.int32),
            pltpu.VMEM((512, 256), jnp.float32),
            pltpu.SemaphoreType.DMA((2 * layers + 5,)),
        ],
        compiler_params=params(56),
        cost_estimate=cost(7),
        name="face_sums",
    )(where, count, area, speed, node, block, metric)


def basis_kernel(
    where_ref, own_ref, other_ref, same_ref, cross_ref, root_ref,
    field, sums_ref, rows, root, outer, line, partial,
):
    core = where_ref[0, 0]
    centre = (BASIS_LOW + BASIS_HIGH) / 2
    scale = 2 / (BASIS_HIGH - BASIS_LOW)
    for t in range(8):
        rows[t, pl.ds(32 + 32 * core, 32), :] = own_ref[t]
        rows[t, pl.ds(64 - 32 * core, 32), :] = other_ref[t]
        rows[t, pl.ds(96 * core, 32), :] = cross_ref[t]
        rows[t, pl.ds(96 - 96 * core, 32), :] = same_ref[t]
    for t in range(8):
        for ys in range(GROUPS):
            field[0, t, ys] = rows[t, pl.ds(ys, SUB, stride=GROUPS), :]
            value = root_ref[t, pl.ds(ys, SUB, stride=GROUPS), :]
            root[t, ys] = value * (stored(t % 2) * stored(ys % 2))
            outer[t, ys] = value * (2 * scale * 4.0 / 225.0 / (given(t % 2) * given(ys % 2)))

    group = lax.broadcasted_iota(jnp.int32, (SUB, LANES), 0)
    own_rows = jnp.where((group >= 2) & (group < 6), 1.0, 0.0).astype(jnp.float32)

    def step(k, begin, end):
        def put(k, t, ys, value):
            if not end:
                field[k, t, ys] = value

        for ys in range(GROUPS):
            padded = column_ring([field[k, t, ys] * root[t, ys] for t in range(8)])
            for t in range(8):
                line[ys, t] = mass_line(padded, t)
        squares, shifts = [], []
        for t in range(8):
            square = jnp.zeros((SUB, LANES), jnp.float32)
            shifted = jnp.zeros((SUB, LANES), jnp.float32)
            padded = row_ring([line[ys, t] for ys in range(GROUPS)])
            for ys in range(GROUPS):
                now = field[k, t, ys]
                later = outer[t, ys] * mass_line(padded, ys) - (2 * centre * scale) * now
                later = 0.5 * later if begin else later - field[k - 1, t, ys]
                put(k + 1, t, ys, later)
                square = square + now * now
                shifted = shifted + later * now
            squares.append(square)
            shifts.append(shifted)

        def add(parts):
            while len(parts) > 1:
                parts = [parts[i] + parts[i + 1] for i in range(0, len(parts), 2)]
            return jnp.sum(parts[0] * own_rows, axis=0, keepdims=True)

        partial[pl.ds(2 * k, 1), :] = add(squares)
        partial[pl.ds(2 * k + 1, 1), :] = add(shifts)

    def later_step(k, carry):
        step(k, False, False)
        return carry

    partial[...] = jnp.zeros_like(partial)
    step(0, True, False)
    lax.fori_loop(1, ITERS - 1, later_step, 0)
    step(ITERS - 1, False, True)
    whole = jnp.sum(partial[...], axis=1, keepdims=True)
    row = lax.broadcasted_iota(jnp.int32, partial.shape, 0)
    lane = lax.broadcasted_iota(jnp.int32, partial.shape, 1)
    line_of = jnp.sum(jnp.where(row == lane, whole, 0.0), axis=0, keepdims=True)
    sums_ref[...] = jnp.broadcast_to(line_of[None], sums_ref.shape)


def surface_basis(where, vols, own, other, same, cross, root):
    return pl.pallas_call(
        basis_kernel,
        out_shape=(f32(ITERS, 8, GROUPS, SUB, LANES), f32(vols, SUB, LANES)),
        in_specs=[SMEM] + [VMEM] * 5,
        out_specs=(VMEM, VMEM),
        scratch_shapes=[
            pltpu.VMEM((8, ROWS, LANES), jnp.float32),
            pltpu.VMEM((8, GROUPS, SUB, LANES), jnp.float32),
            pltpu.VMEM((8, GROUPS, SUB, LANES), jnp.float32),
            pltpu.VMEM((GROUPS, 8, SUB, LANES), jnp.float32),
            pltpu.VMEM((24, LANES), jnp.float32),
        ],
        compiler_params=params(24),
        cost_estimate=cost(7),
        name="surface_basis",
    )(where, own, other, same, cross, root)


def solve_weights():
    n = ITERS
    moment = np.zeros((2 * n, 2 * n))
    for m in range(2 * n):
        if m < 2:
            moment[m, m] = 1.0
        else:
            moment[m, m] = 2.0
            moment[m, m % 2] = -1.0
    centre, half = (BASIS_LOW + BASIS_HIGH) / 2, (BASIS_HIGH - BASIS_LOW) / 2
    weights = np.zeros((2 * n, 16, LANES))
    for i in range(n):
        for j in range(n):
            lower = abs(j - 1)
            for factor, index in (
                (centre / 2, i + j),
                (centre / 2, abs(i - j)),
                (half / 4, i + j + 1),
                (half / 4, abs(i - j - 1)),
                (half / 4, i + lower),
                (half / 4, abs(i - lower)),
            ):
                weights[:, i, j] += factor * moment[index]
        weights[:, i, n] += moment[i]
    return weights.astype(np.float32)


def solve_kernel(part_ref, sums_ref, weights_ref, out_ref, flag_ref, rows):
    n = ITERS
    total = sums_ref[0]
    for i in range(1, sums_ref.shape[0]):
        total = total + sums_ref[i]
    row = lax.broadcasted_iota(jnp.int32, (16, LANES), 0)
    lane = lax.broadcasted_iota(jnp.int32, (16, LANES), 1)
    system = jnp.where((lane == row + 16) & (row < n), 1.0, 0.0).astype(jnp.float32)
    for m in range(2 * n):
        system = system + weights_ref[m] * total[0:1, m : m + 1]
    centre = jnp.sum(jnp.where(lane == row, system, 0.0), axis=1, keepdims=True)
    for k in range(n):
        pivot_row = system[k : k + 1, :] / system[k : k + 1, k : k + 1]
        column = system[:, k : k + 1]
        system = jnp.where(row == k, pivot_row, system - column * pivot_row)
    inverse = jnp.sum(jnp.where(lane == row + 16, system, 0.0), axis=1, keepdims=True)
    figure = jnp.broadcast_to(centre * inverse, (16, LANES))
    inside = (row < n) & (lane == 0)
    least = jnp.min(jnp.where(inside, figure, 1.0))
    whole = jnp.sum(jnp.where(inside, figure, 0.0))
    flag_ref[0, 0] = jnp.where((least > 0.5) & (whole < CONDITION_MAX), 1, 0).astype(jnp.int32)
    weights = [jnp.broadcast_to(system[k : k + 1, n : n + 1], (SUB, LANES)) for k in range(n)]
    for t in range(8):
        for ys in range(GROUPS):
            value = weights[0] * part_ref[0, t, ys]
            for k in range(1, n):
                value = value + weights[k] * part_ref[k, t, ys]
            rows[t, pl.ds(ys, SUB, stride=GROUPS), :] = value
        out_ref[t] = rows[t, HALO - DEEP : HALO - DEEP + Y_ROWS, :]


def surface_solve(basis, sums):
    return pl.pallas_call(
        solve_kernel,
        out_shape=(f32(8, Y_ROWS, LANES), jax.ShapeDtypeStruct((1, 1), jnp.int32)),
        in_specs=[VMEM, VMEM, VMEM],
        out_specs=(VMEM, SMEM),
        scratch_shapes=[pltpu.VMEM((8, ROWS, LANES), jnp.float32)],
        compiler_params=params(24),
        cost_estimate=cost(3),
        name="surface_solve",
    )(basis, sums, jnp.asarray(solve_weights()))


def fill_factors(where_ref, factor):
    vol, vols, rows = where_ref[0, 3], where_ref[0, 4], where_ref[0, 5]
    group = lax.broadcasted_iota(jnp.int32, (SUB, LANES), 0)
    mass, stiff = (8.0, 16.0), (14.0, 16.0)
    for ys in range(Y_GROUPS):
        row = group * Y_GROUPS + ys
        outside = ((vol == 0) & (row < DEEP)) | ((vol == vols - 1) & (row >= DEEP + rows))
        py = ys % 2
        for pz in range(2):
            for px in range(2):
                value = -12.0 / (
                    stiff[pz] * mass[py] * mass[px]
                    + mass[pz] * (stiff[py] * mass[px] + mass[py] * stiff[px])
                )
                for p in (pz, py, px):
                    value = value * stored(p) / given(p)
                factor[pz, px, ys] = jnp.where(outside, 0.0, jnp.float32(value))


def lateral_lines(get, line_a, line_b, put):
    for t in range(8):
        u = row_ring([get(t, ys) for ys in range(Y_GROUPS)])
        for ys in range(Y_GROUPS):
            m = mass_line(u, ys)
            line_a[t, ys] = m
            line_b[t, ys] = both_line(u, ys) - m
    for ys in range(Y_GROUPS):
        a = column_ring([line_a[t, ys] for t in range(8)])
        b = column_ring([line_b[t, ys] for t in range(8)])
        for t in range(8):
            put(t, ys, mass_line(a, t), both_line(a, t) + mass_line(b, t))


def even_step(w, c):
    near = c[1] + c[3]
    return (22.0 / 3.0 * w[1] - (w[0] + w[2])) + ((near + 8.0 * c[2]) - (c[0] + c[4]))


def odd_step(w, c):
    return (8.0 / 3.0 * w[1] - (w[0] + w[2])) + ((c[0] + c[2]) + 4.0 * c[1])


def strided(ys):
    return pl.ds(ys, SUB, stride=Y_GROUPS)


def change_kernel(
    where_ref, speed_ref, out_ref, cells, along, cross, line_a, line_b, factor, plain, sems,
):
    col = where_ref[0, 1]
    layers, _, rows, _ = out_ref.shape

    def lateral(z, carry):
        def put(t, ys, w, c):
            along[z, t, ys] = w
            cross[z, t, ys] = c

        lateral_lines(lambda t, ys: cells[z, t, ys], line_a, line_b, put)
        return carry

    def set_top():
        for t in range(8):
            for ys in range(Y_GROUPS):
                scale = 0.5 * stored(0) * stored(t % 2) * stored(ys % 2)
                cells[2, t, ys] = scale * speed_ref[t, strided(ys), :]

    def send(first, count):
        copies = []
        for z in range(first, first + count):
            for t in range(8):
                for ys in range(Y_GROUPS):
                    plain[z, t, strided(ys), :] = cells[z + 2, t, ys]
            copy = pltpu.make_async_copy(
                plain.at[z, :, pl.ds(DEEP, rows), :], out_ref.at[z], sems.at[z]
            )
            copy.start()
            copies.append(copy)
        for copy in copies:
            copy.wait()

    @pl.when(col == 0)
    def _():
        fill_factors(where_ref, factor)
        set_top()
        clear = jnp.zeros((8, Y_GROUPS, SUB, LANES), jnp.float32)
        for z in range(2):
            cross[z] = clear
            along[z] = clear

        def update(pair, carry):
            z = 2 * pair + 2
            for ys in range(Y_GROUPS):
                factors = [[factor[pz, px, ys] for px in range(2)] for pz in range(2)]
                for t in range(8):
                    w = [along[z + i, t, ys] for i in range(-1, 3)]
                    c = [cross[z + i, t, ys] for i in range(-2, 3)]
                    cells[z, t, ys] += factors[0][t % 2] * even_step(w, c)
                    cells[z + 1, t, ys] += factors[1][t % 2] * odd_step(w[1:], c[2:])
            return carry

        def one_sweep(sweep, carry):
            front = 2 * sweep + 2
            lax.fori_loop(2, front + 1, lateral, 0)
            lax.fori_loop(0, sweep, update, 0)
            for ys in range(Y_GROUPS):
                factors = [[factor[pz, px, ys] for px in range(2)] for pz in range(2)]
                for t in range(8):
                    w0, w1 = along[front - 1, t, ys], along[front, t, ys]
                    c0, c1, c2 = [cross[front + i, t, ys] for i in range(-2, 1)]
                    step = (22.0 / 3.0 * w1 - w0) + ((c1 + 8.0 * c2) - c0)
                    cells[front, t, ys] += factors[0][t % 2] * step
                    cells[front + 1, t, ys] = factors[1][t % 2] * (c2 - w1)
                    cells[front + 2, t, ys] = -factors[0][t % 2] * c2
            set_top()
            return carry

        lax.fori_loop(0, SWEEPS, one_sweep, 0)
        send(1, layers - 1)

    @pl.when(col == 1)
    def _():
        fill_factors(where_ref, factor)
        set_top()

        def one_sweep(sweep, carry):
            lateral(2, 0)
            for t in range(8):
                for ys in range(Y_GROUPS):
                    cells[2, t, ys] = -factor[0, t % 2, ys] * cross[2, t, ys]
            return carry

        lax.fori_loop(0, SWEEPS, one_sweep, 0)
        send(0, 1)


def surface_change(where, speed, layers, rows):
    work = pltpu.VMEM((layers + 2, 8, Y_GROUPS, SUB, LANES), jnp.float32)
    line = pltpu.VMEM((8, Y_GROUPS, SUB, LANES), jnp.float32)
    return pl.pallas_call(
        change_kernel,
        out_shape=f32(layers, 8, rows, LANES),
        in_specs=[SMEM, VMEM],
        out_specs=HBM,
        scratch_shapes=[
            pltpu.VMEM((layers + 3, 8, Y_GROUPS, SUB, LANES), jnp.float32),
            work, work, line, line,
            pltpu.VMEM((2, 2, Y_GROUPS, SUB, LANES), jnp.float32),
            pltpu.VMEM((layers, 8, Y_ROWS, LANES), jnp.float32),
            pltpu.SemaphoreType.DMA((layers,)),
        ],
        compiler_params=params(32),
        cost_estimate=cost(8),
        name="surface_change",
    )(where, speed)


def base_kernel(
    where_ref, wide_ref, zlow_ref, zhigh_ref, change_ref, speed_ref, select_hbm_ref,
    velocity_ref, out_ref, field, along, cross, line_a, line_b, factor, change, select, parts, sems,
):
    col, cols = where_ref[0, 1], where_ref[0, 2]
    layers, _, rows, _ = change_ref.shape
    total = layers + 2 * DEEP
    arrivals = []
    for i in range(total):
        z = (i + DEEP) % total
        source = wide_ref if i < layers else zhigh_ref if i < layers + DEEP else zlow_ref
        arrivals.append(pltpu.make_async_copy(source.at[i % DEEP], field.at[z], sems.at[z]))
    for arrival in arrivals:
        arrival.start()
    choose = pltpu.make_async_copy(select_hbm_ref, select, sems.at[total + 2])
    choose.start()
    all_change = pltpu.make_async_copy(
        change_ref.at[pl.ds(1, layers - 1)], change.at[pl.ds(1, layers - 1)], sems.at[total]
    )
    one_change = pltpu.make_async_copy(
        change_ref.at[pl.ds(0, 1)], change.at[pl.ds(0, 1)], sems.at[total + 1]
    )
    pl.when(col == 0)(all_change.start)
    pl.when(col == 1)(one_change.start)
    fill_factors(where_ref, factor)
    count = (layers + 1) * rows

    def cut(value, at, t):
        first, second = split(value)
        lanes = slice(LANES * t, LANES * (t + 1))
        parts[at : at + rows, lanes] = first
        parts[count + at : count + at + rows, lanes] = second

    for t in range(8):
        cut(speed_ref[t, DEEP : DEEP + rows, :], 0, t)

    def lateral(z, carry):
        def put(t, ys, w, c):
            along[z, t, ys] = w
            cross[z, t, ys] = c

        lateral_lines(lambda t, ys: field[z, t, strided(ys), :], line_a, line_b, put)
        return carry

    def update(pair, carry):
        z = 2 * pair
        for ys in range(Y_GROUPS):
            factors = [[factor[pz, px, ys] for px in range(2)] for pz in range(2)]
            for t in range(8):
                w = [along[z + i, t, ys] for i in range(-1, 3)]
                c = [cross[z + i, t, ys] for i in range(-2, 3)]
                even, odd = even_step(w, c), odd_step(w[1:], c[2:])
                scale = jnp.where((col == 0) & (z == DEEP), 0.0, factors[0][t % 2])
                even = field[z, t, strided(ys), :] + scale * even
                odd = field[z + 1, t, strided(ys), :] + factors[1][t % 2] * odd
                field[z, t, strided(ys), :] = even
                field[z + 1, t, strided(ys), :] = odd
        return carry

    def update_all(sweep):
        low_pair = jnp.where(col == 0, DEEP // 2, sweep + 1)
        high_pair = jnp.where(col == cols - 1, (DEEP + layers) // 2, total // 2 - sweep - 1)
        lax.fori_loop(low_pair, high_pair, update, 0)

    begin = jnp.where(col == 0, DEEP, 0)
    end = jnp.where(col == cols - 1, DEEP + layers + 1, total - 1)

    def first_lateral(i, carry):
        z = lax.rem(i + DEEP, total)
        pltpu.make_async_copy(wide_ref.at[0], field.at[z], sems.at[z]).wait()

        @pl.when((z >= begin) & (z < end))
        def _():
            lateral(z, 0)

        return carry

    def later_sweep(sweep, carry):
        lax.fori_loop(
            jnp.maximum(begin, 2 * sweep), jnp.minimum(end, total - 2 * sweep - 1), lateral, 0
        )
        update_all(sweep)
        return carry

    @pl.when(col == 0)
    def _():
        clear = jnp.zeros((8, Y_GROUPS, SUB, LANES), jnp.float32)
        for z in (DEEP - 2, DEEP - 1):
            along[z] = clear
            cross[z] = clear

    lax.fori_loop(0, total, first_lateral, 0)
    update_all(0)
    lax.fori_loop(1, SWEEPS, later_sweep, 0)

    row = lax.broadcasted_iota(jnp.int32, (rows, LANES), 0)
    by_row = jnp.where(row % 2 == 0, stored(0), stored(1)).astype(jnp.float32)
    back_row = jnp.where(row % 2 == 0, 1 / stored(0), 1 / stored(1)).astype(jnp.float32)

    @pl.when(col == 0)
    def _():
        all_change.wait()
        for t in range(8):
            top = speed_ref[t, DEEP : DEEP + rows, :] * (by_row * (0.5 * stored(0) * stored(t % 2)))
            field[DEEP, t, DEEP : DEEP + rows, :] += top
            for z in range(1, layers):
                field[DEEP + z, t, DEEP : DEEP + rows, :] += change[z, t]

    @pl.when(col == 1)
    def _():
        one_change.wait()
        for t in range(8):
            field[DEEP, t, DEEP : DEEP + rows, :] += change[0, t]

    for z in range(layers):
        for t in range(8):
            value = field[DEEP + z, t, DEEP : DEEP + rows, :]
            cut(value * (back_row * (1 / (stored(z % 2) * stored(t % 2)))), rows * (z + 1), t)

    def write(at, value):
        velocity_ref[:, at] = value[:rows]
        out_ref[:, :, at] = value[rows:].reshape(layers, rows, 256)

    choose.wait()
    plain_columns(select, parts[...], count, write)


def base_sweeps(where, wide, zlow, zhigh, change, speed, select):
    layers, _, rows, _ = change.shape
    total = layers + 2 * DEEP
    work = pltpu.VMEM((total, 8, Y_GROUPS, SUB, LANES), jnp.float32)
    line = pltpu.VMEM((8, Y_GROUPS, SUB, LANES), jnp.float32)
    return pl.pallas_call(
        base_kernel,
        out_shape=(f32(rows, 8 * LANES), f32(layers, rows, 8 * LANES)),
        in_specs=[SMEM] + [HBM] * 4 + [VMEM, HBM],
        out_specs=(VMEM, VMEM),
        scratch_shapes=[
            pltpu.VMEM((total, 8, Y_ROWS, LANES), jnp.float32),
            work, work, line, line,
            pltpu.VMEM((2, 2, Y_GROUPS, SUB, LANES), jnp.float32),
            pltpu.VMEM((layers, 8, rows, LANES), jnp.float32),
            pltpu.VMEM(select.shape, jnp.bfloat16),
            pltpu.VMEM((2 * (layers + 1) * rows, 8 * LANES), jnp.bfloat16),
            pltpu.SemaphoreType.DMA((total + 3,)),
        ],
        compiler_params=params(50),
        cost_estimate=cost(25),
        name="base_sweeps",
    )(where, wide, zlow, zhigh, change, speed, select)


mass_even = (-1.0 / 15.0, 2.0 / 15.0, 8.0 / 15.0, 2.0 / 15.0, -1.0 / 15.0)
mass_odd = (0.0, 2.0 / 15.0, 16.0 / 15.0, 2.0 / 15.0, 0.0)


def mass_along(padded, axis):
    count = padded.shape[axis] - 4
    pieces = [lax.slice_in_dim(padded, i, i + count, axis=axis) for i in range(5)]
    even = sum(mass_even[i] * pieces[i] for i in range(5))
    odd = sum(mass_odd[i] * pieces[i] for i in range(1, 4))
    at_even = lax.broadcasted_iota(jnp.int32, even.shape, axis) % 2 == 0
    return jnp.where(at_even, even, odd)


def with_rows(x, width):
    size = lax.axis_size("vol")
    up = [(i, i + 1) for i in range(size - 1)]
    down = [(j, i) for i, j in up]
    before = lax.ppermute(x[-width:], "vol", up)
    after = lax.ppermute(x[:width], "vol", down)
    return jnp.concatenate([before, x, after], axis=0)


def stepwise(flux, metric):
    root = jnp.sqrt(metric)

    def dot(a, b):
        return lax.psum(jnp.sum(a * b), "vol")

    def step(_, state):
        solved, residual, direction, norm = state
        padded = jnp.pad(with_rows(root * direction, 2), ((0, 0), (2, 2)))
        image = root * mass_along(mass_along(padded, 1), 0)
        alpha = norm / dot(direction, image)
        solved = solved + alpha * direction
        residual = residual - alpha * image
        after = dot(residual, residual)
        direction = residual + after / norm * direction
        return solved, residual, direction, after

    state = (jnp.zeros_like(flux), flux, flux, dot(flux, flux))
    return with_rows(lax.fori_loop(0, ITERS, step, state)[0], DEEP)


def after(x, *others):
    return lax.optimization_barrier((x,) + others)[0]


def on_device(face_area, face_speed, face_node, face_count, surface_metric, displacement):
    vols, cols = lax.axis_size("vol"), lax.axis_size("col")
    vol, col = lax.axis_index("vol"), lax.axis_index("col")
    core = col % 2
    where = [core, col, jnp.int32(cols), vol, jnp.int32(vols), jnp.int32(displacement.shape[1])]
    where = jnp.stack(where).astype(jnp.int32).reshape(1, 6)
    up = [(i, i + 1) for i in range(vols - 1)]
    down = [(j, i) for i, j in up]
    col_up = [(i, i + 1) for i in range(cols - 1)]
    col_down = [(j, i) for i, j in col_up]
    packed = displacement.shape[0] * DEEP

    select = plain_selection()

    def moved(x, steps):
        dv, dc = steps
        pairs = [
            (i * cols + j, (i + dv) * cols + j + dc)
            for i in range(vols)
            for j in range(cols)
            if 0 <= i + dv < vols and 0 <= j + dc < cols
        ]
        return lax.ppermute(x, ("vol", "col"), pairs)

    keep, send, rows_up, rows_down = face_sums(
        where, face_count, face_area, face_speed, face_node, displacement, surface_metric
    )
    with jax.named_scope("flux_sum"):
        keep = keep + lax.ppermute(send, "col", [(j, j ^ 1) for j in range(cols)])
        turned = [
            lax.ppermute(keep, "col", [(j, (j + 2 * k) % cols) for j in range(cols)]) for k in (1, 2, 3)
        ]
    with jax.named_scope("row_halo"):
        rows_before, rows_after = moved(rows_up, (1, 0)), moved(rows_down, (-1, 0))
    wide, root = regroup(displacement, surface_metric, rows_before, rows_after)
    with jax.named_scope("flux_sum"):
        turned = lax.optimization_barrier((*turned, wide))
        own = (keep + turned[1]) + (turned[0] + turned[2])
    with jax.named_scope("flux_halo"):
        other = lax.ppermute(own, "col", [(j, j ^ 1) for j in range(cols)])
        pairs = []
        for i in range(vols):
            for j in range(cols):
                to = i - 1 if j % 2 == 0 else i + 1
                if 0 <= to < vols:
                    pairs.append((i * cols + j, to * cols + j))
        same = lax.ppermute(own, ("vol", "col"), pairs)
        cross = lax.ppermute(same, "col", [(j, j ^ 1) for j in range(cols)])

    with jax.named_scope("depth_halo"):
        sent = after(wide, own)
        zlow, zhigh = moved(sent, (0, 1)), moved(sent, (0, -1))
    basis, spread = surface_basis(where, vols, own, other, same, cross, root)
    with jax.named_scope("gather_sums"):
        gathered = lax.all_to_all(spread, "vol", 0, 0)
    speed, flag = surface_solve(basis, gathered)

    def finish(speed):
        change = surface_change(where, speed, displacement.shape[0], displacement.shape[1])
        return base_sweeps(where, wide, zlow, zhigh, change, speed, select)

    def step_by_step():
        low = jnp.where(core == 0, own, other)
        high = jnp.where(core == 0, other, own)
        flux = jnp.concatenate([low, high], axis=1)
        flux = flux.transpose(1, 2, 0).reshape(surface_metric.shape)
        solved = stepwise(flux, surface_metric)
        return finish(solved.reshape(Y_ROWS, LANES, 8).transpose(2, 0, 1))

    return lax.cond(flag[0, 0] > 0, lambda: finish(speed), step_by_step)


def solution(mesh):
    in_specs = (
        P("vol", "col"),
        P("vol", "col"),
        P("vol", "col"),
        P("vol", "col"),
        P("vol", None),
        P("col", "vol", None),
    )
    out_specs = (P("vol", None), P("col", "vol", None))
    return jax.shard_map(
        on_device, mesh=mesh, in_specs=in_specs, out_specs=out_specs, check_vma=False
    )
```

```python
import jax
import jax.numpy as jnp
import numpy as np
from jax import lax
from jax.experimental import pallas as pl
from jax.experimental.pallas import tpu as pltpu
from jax.sharding import PartitionSpec as P

ITERS = 10
SWEEPS = 4
LANES = 128
SUB = 8
MIB = 1024 * 1024
DEEP = 2 * SWEEPS
HALO = 32
ROWS = 128
GROUPS = 16
Y_GROUPS = 10
Y_ROWS = 80

BASIS_LOW = 0.1
BASIS_HIGH = 12.0
CONDITION_MAX = 2000.0


def rolled(x, shift, axis):
    return pltpu.roll(x, shift % x.shape[axis], axis)


def column_ring(tiles):
    n = len(tiles)
    lane = lax.broadcasted_iota(jnp.int32, tiles[0].shape, 1)
    first, last = lane == 0, lane == LANES - 1
    return (
        [jnp.where(first, 0.0, rolled(tiles[j], 1, 1)) for j in (n - 2, n - 1)]
        + list(tiles)
        + [jnp.where(last, 0.0, rolled(tiles[j], -1, 1)) for j in (0, 1)]
    )


def row_ring(rows):
    n = len(rows)
    return (
        [rolled(rows[j], 1, 0) for j in (n - 2, n - 1)]
        + list(rows)
        + [rolled(rows[j], -1, 0) for j in (0, 1)]
    )


def mass_line(padded, index):
    i = index + 2
    near = padded[i - 1] + padded[i + 1]
    if index % 2:
        return near + 4.0 * padded[i]
    return (near + 8.0 * padded[i]) - (padded[i - 2] + padded[i + 2])


def both_line(padded, index):
    i = index + 2
    near = padded[i - 1] + padded[i + 1]
    return (8.0 / 3.0 if index % 2 else 22.0 / 3.0) * padded[i] - near


def stored(parity):
    return 1.0 if parity else 0.5


def given(parity):
    return 0.5 if parity else 1.0


SMEM = pl.BlockSpec(memory_space=pltpu.SMEM)
VMEM = pl.BlockSpec(memory_space=pltpu.VMEM)
HBM = pl.BlockSpec(memory_space=pltpu.HBM)


def f32(*shape):
    return jax.ShapeDtypeStruct(shape, jnp.float32)


def params(mib):
    return pltpu.CompilerParams(vmem_limit_bytes=mib * MIB)


def cost(us):
    return pl.CostEstimate(flops=0, bytes_accessed=int(us * 100_000), transcendentals=0)


def split(x):
    first = x.astype(jnp.bfloat16)
    return first, (x - first.astype(jnp.float32)).astype(jnp.bfloat16)


def to_blocked(j):
    x = lax.broadcasted_iota(jnp.int32, (1024, 256), 0)
    n = lax.broadcasted_iota(jnp.int32, (1024, 256), 1)
    hit = x == 8 * (n & 127) + j + (n >> 7)
    return jnp.where(hit, 1.0, 0.0).astype(jnp.bfloat16)


def plain_selection():
    k = np.arange(1024)
    out = np.zeros((1024, 1024), np.float32)
    out[k, 8 * (k % LANES) + k // LANES] = 1.0
    return jnp.asarray(out, jnp.bfloat16)


def regroup_kernel(block_ref, metric_ref, before_ref, after_ref, wide_ref, root_ref, parts_ref):
    layers, rows, _ = block_ref.shape
    packed = DEEP * layers
    total = layers * Y_ROWS + ROWS

    def put(at, value):
        first, second = split(value)
        parts_ref[at : at + value.shape[0], :] = first
        parts_ref[total + at : total + at + value.shape[0], :] = second

    for z in range(layers):
        put(Y_ROWS * z, before_ref[DEEP * z : DEEP * (z + 1), :])
        put(Y_ROWS * z + DEEP, block_ref[z])
        put(Y_ROWS * z + DEEP + rows, after_ref[DEEP * z : DEEP * (z + 1), :])
    row = lax.broadcasted_iota(jnp.int32, (Y_ROWS, LANES), 0)
    by_row = jnp.where(row % 2 == 0, stored(0), stored(1)).astype(jnp.float32)
    at = layers * Y_ROWS
    put(at, jnp.sqrt(before_ref[packed:, :]))
    put(at + HALO, jnp.sqrt(metric_ref[...]))
    put(at + HALO + rows, jnp.sqrt(after_ref[packed:, :]))
    for j in range(0, 8, 2):
        pair = jnp.dot(parts_ref[...], to_blocked(j), preferred_element_type=jnp.float32)
        pair = pair[:total] + pair[total:]
        for i in range(2):
            tile = pair[:, LANES * i : LANES * (i + 1)]
            for z in range(layers):
                wide_ref[z, j + i] = tile[Y_ROWS * z : Y_ROWS * (z + 1)] * (by_row * (stored(z % 2) * stored(i)))
            root_ref[j + i] = tile[layers * Y_ROWS :]


def regroup(block, metric, before, after):
    layers, rows, cols = block.shape
    return pl.pallas_call(
        regroup_kernel,
        out_shape=(f32(layers, 8, Y_ROWS, LANES), f32(8, ROWS, LANES)),
        in_specs=[VMEM] * 4,
        out_specs=(VMEM, VMEM),
        scratch_shapes=[pltpu.VMEM((2 * (Y_ROWS * layers + ROWS), cols), jnp.bfloat16)],
        compiler_params=params(32),
        cost_estimate=cost(150),
        name="regroup",
    )(block, metric, before, after)


def plain_columns(select_ref, parts, rows, write):
    for q in range(4):
        at = slice(256 * q, 256 * (q + 1))
        value = jnp.dot(parts, select_ref[:, at], preferred_element_type=jnp.float32)
        write(at, value[:rows] + value[rows:])


def face_kernel(
    where_ref, count_ref, area_ref, speed_ref, node_ref,
    keep_ref, send_ref, area, speed, nodes, acc_ref, sems,
):
    slots = area_ref.shape[1]
    fetches = [
        pltpu.make_async_copy(source, target, sems.at[i])
        for i, (source, target) in enumerate(((area_ref, area), (speed_ref, speed), (node_ref, nodes)))
    ]
    for fetch in fetches:
        fetch.start()
    chunk = min(4096, slots)
    core = where_ref[0, 0]
    ids = lax.broadcasted_iota(jnp.int32, (256, chunk), 0)
    ids = ids.astype(jnp.float32).astype(jnp.bfloat16)
    zero = jnp.zeros((), jnp.bfloat16)
    one = jnp.ones((), jnp.bfloat16)
    contract = (((1,), (1,)), ((), ()))
    acc_ref[...] = jnp.zeros_like(acc_ref)
    for fetch in fetches:
        fetch.wait()

    def wide(x):
        return jnp.broadcast_to(x.astype(jnp.bfloat16), (256, chunk))

    def body(step, carry):
        at = pl.ds(pl.multiple_of(step * chunk, chunk), chunk)
        slot = lax.broadcasted_iota(jnp.int32, (1, chunk), 1) + step * chunk
        value = jnp.where(slot < count_ref[0, 0], area[:, at] * speed[:, at], 0.0)
        node = nodes[:, at]
        low = (((node & 1) << 7) + ((node >> 3) & 127)).astype(jnp.float32)
        high = (((node >> 1) & 3) * 64 + (node >> 10)).astype(jnp.float32)
        first = value.astype(jnp.bfloat16)
        second = value - first.astype(jnp.float32)
        here = wide(high) == ids
        upper = jnp.where(here, wide(first), zero)
        lower = jnp.where(here, wide(second), zero)
        columns = jnp.where(wide(low) == ids, one, zero)
        both = jnp.concatenate([upper, lower], axis=0)
        acc_ref[...] += lax.dot_general(both, columns, contract, preferred_element_type=jnp.float32)
        return carry

    lax.fori_loop(0, slots // chunk, body, 0)
    for j in range(8):
        at, lanes = 64 * (j // 2), slice(LANES * (j % 2), LANES * (j % 2 + 1))
        near, far = at + 32 * core, at + 32 - 32 * core
        keep_ref[j] = acc_ref[pl.ds(near, 32), lanes] + acc_ref[pl.ds(256 + near, 32), lanes]
        send_ref[j] = acc_ref[pl.ds(far, 32), lanes] + acc_ref[pl.ds(256 + far, 32), lanes]


def face_sums(where, count, area, speed, node):
    half = f32(8, 32, LANES)
    return pl.pallas_call(
        face_kernel,
        out_shape=(half, half),
        in_specs=[SMEM, SMEM] + [HBM] * 3,
        out_specs=(VMEM, VMEM),
        scratch_shapes=[
            pltpu.VMEM(area.shape, jnp.float32),
            pltpu.VMEM(area.shape, jnp.float32),
            pltpu.VMEM(area.shape, jnp.int32),
            pltpu.VMEM((512, 256), jnp.float32),
            pltpu.SemaphoreType.DMA((3,)),
        ],
        compiler_params=params(56),
        cost_estimate=cost(7),
        name="face_sums",
    )(where, count, area, speed, node)


def cut_kernel(block_ref, metric_ref, up_ref, down_ref, sems):
    layers, rows, _ = block_ref.shape
    copies = []
    for out_ref, row, root_row in ((up_ref, rows - DEEP, rows - HALO), (down_ref, 0, 0)):
        for z in range(layers):
            part = block_ref.at[z, pl.ds(row, DEEP), :]
            copies.append((part, out_ref.at[pl.ds(DEEP * z, DEEP), :]))
        part = metric_ref.at[pl.ds(root_row, HALO), :]
        copies.append((part, out_ref.at[pl.ds(DEEP * layers, HALO), :]))
    copies = [pltpu.make_async_copy(*pair, sems.at[i]) for i, pair in enumerate(copies)]
    for copy in copies:
        copy.start()
    for copy in copies:
        copy.wait()


def outgoing_rows(block, metric):
    layers, _, cols = block.shape
    rows = f32(DEEP * layers + HALO, cols)
    return pl.pallas_call(
        cut_kernel,
        out_shape=(rows, rows),
        in_specs=[HBM, HBM],
        out_specs=(VMEM, VMEM),
        scratch_shapes=[pltpu.SemaphoreType.DMA((2 * layers + 2,))],
        compiler_params=params(56),
        cost_estimate=cost(1),
        name="outgoing_rows",
    )(block, metric)


def basis_kernel(
    where_ref, own_ref, other_ref, same_ref, cross_ref, root_ref,
    field, sums_ref, rows, root, outer, line, partial,
):
    core = where_ref[0, 0]
    centre = (BASIS_LOW + BASIS_HIGH) / 2
    scale = 2 / (BASIS_HIGH - BASIS_LOW)
    for t in range(8):
        rows[t, pl.ds(32 + 32 * core, 32), :] = own_ref[t]
        rows[t, pl.ds(64 - 32 * core, 32), :] = other_ref[t]
        rows[t, pl.ds(96 * core, 32), :] = cross_ref[t]
        rows[t, pl.ds(96 - 96 * core, 32), :] = same_ref[t]
    for t in range(8):
        for ys in range(GROUPS):
            field[0, t, ys] = rows[t, pl.ds(ys, SUB, stride=GROUPS), :]
            value = root_ref[t, pl.ds(ys, SUB, stride=GROUPS), :]
            root[t, ys] = value * (stored(t % 2) * stored(ys % 2))
            outer[t, ys] = value * (2 * scale * 4.0 / 225.0 / (given(t % 2) * given(ys % 2)))

    group = lax.broadcasted_iota(jnp.int32, (SUB, LANES), 0)
    own_rows = jnp.where((group >= 2) & (group < 6), 1.0, 0.0).astype(jnp.float32)

    def step(k, begin, end):
        def put(k, t, ys, value):
            if not end:
                field[k, t, ys] = value

        for ys in range(GROUPS):
            padded = column_ring([field[k, t, ys] * root[t, ys] for t in range(8)])
            for t in range(8):
                line[ys, t] = mass_line(padded, t)
        squares, shifts = [], []
        for t in range(8):
            square = jnp.zeros((SUB, LANES), jnp.float32)
            shifted = jnp.zeros((SUB, LANES), jnp.float32)
            padded = row_ring([line[ys, t] for ys in range(GROUPS)])
            for ys in range(GROUPS):
                now = field[k, t, ys]
                later = outer[t, ys] * mass_line(padded, ys) - (2 * centre * scale) * now
                later = 0.5 * later if begin else later - field[k - 1, t, ys]
                put(k + 1, t, ys, later)
                square = square + now * now
                shifted = shifted + later * now
            squares.append(square)
            shifts.append(shifted)

        def add(parts):
            while len(parts) > 1:
                parts = [parts[i] + parts[i + 1] for i in range(0, len(parts), 2)]
            return jnp.sum(parts[0] * own_rows, axis=0, keepdims=True)

        partial[pl.ds(2 * k, 1), :] = add(squares)
        partial[pl.ds(2 * k + 1, 1), :] = add(shifts)

    def later_step(k, carry):
        step(k, False, False)
        return carry

    partial[...] = jnp.zeros_like(partial)
    step(0, True, False)
    lax.fori_loop(1, ITERS - 1, later_step, 0)
    step(ITERS - 1, False, True)
    whole = jnp.sum(partial[...], axis=1, keepdims=True)
    row = lax.broadcasted_iota(jnp.int32, partial.shape, 0)
    lane = lax.broadcasted_iota(jnp.int32, partial.shape, 1)
    line_of = jnp.sum(jnp.where(row == lane, whole, 0.0), axis=0, keepdims=True)
    sums_ref[...] = jnp.broadcast_to(line_of[None], sums_ref.shape)


def surface_basis(where, vols, own, other, same, cross, root):
    return pl.pallas_call(
        basis_kernel,
        out_shape=(f32(ITERS, 8, GROUPS, SUB, LANES), f32(vols, SUB, LANES)),
        in_specs=[SMEM] + [VMEM] * 5,
        out_specs=(VMEM, VMEM),
        scratch_shapes=[
            pltpu.VMEM((8, ROWS, LANES), jnp.float32),
            pltpu.VMEM((8, GROUPS, SUB, LANES), jnp.float32),
            pltpu.VMEM((8, GROUPS, SUB, LANES), jnp.float32),
            pltpu.VMEM((GROUPS, 8, SUB, LANES), jnp.float32),
            pltpu.VMEM((24, LANES), jnp.float32),
        ],
        compiler_params=params(24),
        cost_estimate=cost(7),
        name="surface_basis",
    )(where, own, other, same, cross, root)


def solve_weights():
    n = ITERS
    moment = np.zeros((2 * n, 2 * n))
    for m in range(2 * n):
        if m < 2:
            moment[m, m] = 1.0
        else:
            moment[m, m] = 2.0
            moment[m, m % 2] = -1.0
    centre, half = (BASIS_LOW + BASIS_HIGH) / 2, (BASIS_HIGH - BASIS_LOW) / 2
    weights = np.zeros((2 * n, 16, LANES))
    for i in range(n):
        for j in range(n):
            lower = abs(j - 1)
            for factor, index in (
                (centre / 2, i + j),
                (centre / 2, abs(i - j)),
                (half / 4, i + j + 1),
                (half / 4, abs(i - j - 1)),
                (half / 4, i + lower),
                (half / 4, abs(i - lower)),
            ):
                weights[:, i, j] += factor * moment[index]
        weights[:, i, n] += moment[i]
    return weights.astype(np.float32)


def solve_kernel(part_ref, sums_ref, weights_ref, out_ref, flag_ref, rows):
    n = ITERS
    total = sums_ref[0]
    for i in range(1, sums_ref.shape[0]):
        total = total + sums_ref[i]
    row = lax.broadcasted_iota(jnp.int32, (16, LANES), 0)
    lane = lax.broadcasted_iota(jnp.int32, (16, LANES), 1)
    system = jnp.where((lane == row + 16) & (row < n), 1.0, 0.0).astype(jnp.float32)
    for m in range(2 * n):
        system = system + weights_ref[m] * total[0:1, m : m + 1]
    centre = jnp.sum(jnp.where(lane == row, system, 0.0), axis=1, keepdims=True)
    for k in range(n):
        pivot_row = system[k : k + 1, :] / system[k : k + 1, k : k + 1]
        column = system[:, k : k + 1]
        system = jnp.where(row == k, pivot_row, system - column * pivot_row)
    inverse = jnp.sum(jnp.where(lane == row + 16, system, 0.0), axis=1, keepdims=True)
    figure = jnp.broadcast_to(centre * inverse, (16, LANES))
    inside = (row < n) & (lane == 0)
    least = jnp.min(jnp.where(inside, figure, 1.0))
    whole = jnp.sum(jnp.where(inside, figure, 0.0))
    flag_ref[0, 0] = jnp.where((least > 0.5) & (whole < CONDITION_MAX), 1, 0).astype(jnp.int32)
    weights = [jnp.broadcast_to(system[k : k + 1, n : n + 1], (SUB, LANES)) for k in range(n)]
    for t in range(8):
        for ys in range(GROUPS):
            value = weights[0] * part_ref[0, t, ys]
            for k in range(1, n):
                value = value + weights[k] * part_ref[k, t, ys]
            rows[t, pl.ds(ys, SUB, stride=GROUPS), :] = value
        out_ref[t] = rows[t, HALO - DEEP : HALO - DEEP + Y_ROWS, :]


def surface_solve(basis, sums):
    return pl.pallas_call(
        solve_kernel,
        out_shape=(f32(8, Y_ROWS, LANES), jax.ShapeDtypeStruct((1, 1), jnp.int32)),
        in_specs=[VMEM, VMEM, VMEM],
        out_specs=(VMEM, SMEM),
        scratch_shapes=[pltpu.VMEM((8, ROWS, LANES), jnp.float32)],
        compiler_params=params(24),
        cost_estimate=cost(3),
        name="surface_solve",
    )(basis, sums, jnp.asarray(solve_weights()))


def fill_factors(where_ref, factor):
    vol, vols, rows = where_ref[0, 3], where_ref[0, 4], where_ref[0, 5]
    group = lax.broadcasted_iota(jnp.int32, (SUB, LANES), 0)
    mass, stiff = (8.0, 16.0), (14.0, 16.0)
    for ys in range(Y_GROUPS):
        row = group * Y_GROUPS + ys
        outside = ((vol == 0) & (row < DEEP)) | ((vol == vols - 1) & (row >= DEEP + rows))
        py = ys % 2
        for pz in range(2):
            for px in range(2):
                value = -12.0 / (
                    stiff[pz] * mass[py] * mass[px]
                    + mass[pz] * (stiff[py] * mass[px] + mass[py] * stiff[px])
                )
                for p in (pz, py, px):
                    value = value * stored(p) / given(p)
                factor[pz, px, ys] = jnp.where(outside, 0.0, jnp.float32(value))


def lateral_lines(get, line_a, line_b, put):
    for t in range(8):
        u = row_ring([get(t, ys) for ys in range(Y_GROUPS)])
        for ys in range(Y_GROUPS):
            m = mass_line(u, ys)
            line_a[t, ys] = m
            line_b[t, ys] = both_line(u, ys) - m
    for ys in range(Y_GROUPS):
        a = column_ring([line_a[t, ys] for t in range(8)])
        b = column_ring([line_b[t, ys] for t in range(8)])
        for t in range(8):
            put(t, ys, mass_line(a, t), both_line(a, t) + mass_line(b, t))


def even_step(w, c):
    near = c[1] + c[3]
    return (22.0 / 3.0 * w[1] - (w[0] + w[2])) + ((near + 8.0 * c[2]) - (c[0] + c[4]))


def odd_step(w, c):
    return (8.0 / 3.0 * w[1] - (w[0] + w[2])) + ((c[0] + c[2]) + 4.0 * c[1])


def strided(ys):
    return pl.ds(ys, SUB, stride=Y_GROUPS)


def change_kernel(
    where_ref, speed_ref, out_ref, cells, along, cross, line_a, line_b, factor, plain, sems,
):
    col = where_ref[0, 1]
    layers, _, rows, _ = out_ref.shape

    def lateral(z, carry):
        def put(t, ys, w, c):
            along[z, t, ys] = w
            cross[z, t, ys] = c

        lateral_lines(lambda t, ys: cells[z, t, ys], line_a, line_b, put)
        return carry

    def set_top():
        for t in range(8):
            for ys in range(Y_GROUPS):
                scale = 0.5 * stored(0) * stored(t % 2) * stored(ys % 2)
                cells[2, t, ys] = scale * speed_ref[t, strided(ys), :]

    def send(first, count):
        copies = []
        for z in range(first, first + count):
            for t in range(8):
                for ys in range(Y_GROUPS):
                    plain[z, t, strided(ys), :] = cells[z + 2, t, ys]
            copy = pltpu.make_async_copy(
                plain.at[z, :, pl.ds(DEEP, rows), :], out_ref.at[z], sems.at[z]
            )
            copy.start()
            copies.append(copy)
        for copy in copies:
            copy.wait()

    @pl.when(col == 0)
    def _():
        fill_factors(where_ref, factor)
        set_top()
        clear = jnp.zeros((8, Y_GROUPS, SUB, LANES), jnp.float32)
        for z in range(2):
            cross[z] = clear
            along[z] = clear

        def update(pair, carry):
            z = 2 * pair + 2
            for ys in range(Y_GROUPS):
                factors = [[factor[pz, px, ys] for px in range(2)] for pz in range(2)]
                for t in range(8):
                    w = [along[z + i, t, ys] for i in range(-1, 3)]
                    c = [cross[z + i, t, ys] for i in range(-2, 3)]
                    cells[z, t, ys] += factors[0][t % 2] * even_step(w, c)
                    cells[z + 1, t, ys] += factors[1][t % 2] * odd_step(w[1:], c[2:])
            return carry

        def one_sweep(sweep, carry):
            front = 2 * sweep + 2
            lax.fori_loop(2, front + 1, lateral, 0)
            lax.fori_loop(0, sweep, update, 0)
            for ys in range(Y_GROUPS):
                factors = [[factor[pz, px, ys] for px in range(2)] for pz in range(2)]
                for t in range(8):
                    w0, w1 = along[front - 1, t, ys], along[front, t, ys]
                    c0, c1, c2 = [cross[front + i, t, ys] for i in range(-2, 1)]
                    step = (22.0 / 3.0 * w1 - w0) + ((c1 + 8.0 * c2) - c0)
                    cells[front, t, ys] += factors[0][t % 2] * step
                    cells[front + 1, t, ys] = factors[1][t % 2] * (c2 - w1)
                    cells[front + 2, t, ys] = -factors[0][t % 2] * c2
            set_top()
            return carry

        lax.fori_loop(0, SWEEPS, one_sweep, 0)
        send(1, layers - 1)

    @pl.when(col == 1)
    def _():
        fill_factors(where_ref, factor)
        set_top()

        def one_sweep(sweep, carry):
            lateral(2, 0)
            for t in range(8):
                for ys in range(Y_GROUPS):
                    cells[2, t, ys] = -factor[0, t % 2, ys] * cross[2, t, ys]
            return carry

        lax.fori_loop(0, SWEEPS, one_sweep, 0)
        send(0, 1)


def surface_change(where, speed, layers, rows):
    work = pltpu.VMEM((layers + 2, 8, Y_GROUPS, SUB, LANES), jnp.float32)
    line = pltpu.VMEM((8, Y_GROUPS, SUB, LANES), jnp.float32)
    return pl.pallas_call(
        change_kernel,
        out_shape=f32(layers, 8, rows, LANES),
        in_specs=[SMEM, VMEM],
        out_specs=HBM,
        scratch_shapes=[
            pltpu.VMEM((layers + 3, 8, Y_GROUPS, SUB, LANES), jnp.float32),
            work, work, line, line,
            pltpu.VMEM((2, 2, Y_GROUPS, SUB, LANES), jnp.float32),
            pltpu.VMEM((layers, 8, Y_ROWS, LANES), jnp.float32),
            pltpu.SemaphoreType.DMA((layers,)),
        ],
        compiler_params=params(32),
        cost_estimate=cost(8),
        name="surface_change",
    )(where, speed)


def base_kernel(
    where_ref, wide_ref, zlow_ref, zhigh_ref, change_ref, speed_ref, select_hbm_ref,
    velocity_ref, out_ref, field, along, cross, line_a, line_b, factor, change, select, parts, sems,
):
    col, cols = where_ref[0, 1], where_ref[0, 2]
    layers, _, rows, _ = change_ref.shape
    total = layers + 2 * DEEP
    arrivals = []
    for i in range(total):
        z = (i + DEEP) % total
        source = wide_ref if i < layers else zhigh_ref if i < layers + DEEP else zlow_ref
        arrivals.append(pltpu.make_async_copy(source.at[i % DEEP], field.at[z], sems.at[z]))
    for arrival in arrivals:
        arrival.start()
    choose = pltpu.make_async_copy(select_hbm_ref, select, sems.at[total + 2])
    choose.start()
    all_change = pltpu.make_async_copy(
        change_ref.at[pl.ds(1, layers - 1)], change.at[pl.ds(1, layers - 1)], sems.at[total]
    )
    one_change = pltpu.make_async_copy(
        change_ref.at[pl.ds(0, 1)], change.at[pl.ds(0, 1)], sems.at[total + 1]
    )
    pl.when(col == 0)(all_change.start)
    pl.when(col == 1)(one_change.start)
    fill_factors(where_ref, factor)
    count = (layers + 1) * rows

    def cut(value, at, t):
        first, second = split(value)
        lanes = slice(LANES * t, LANES * (t + 1))
        parts[at : at + rows, lanes] = first
        parts[count + at : count + at + rows, lanes] = second

    for t in range(8):
        cut(speed_ref[t, DEEP : DEEP + rows, :], 0, t)

    def lateral(z, carry):
        def put(t, ys, w, c):
            along[z, t, ys] = w
            cross[z, t, ys] = c

        lateral_lines(lambda t, ys: field[z, t, strided(ys), :], line_a, line_b, put)
        return carry

    def update(pair, carry):
        z = 2 * pair
        for ys in range(Y_GROUPS):
            factors = [[factor[pz, px, ys] for px in range(2)] for pz in range(2)]
            for t in range(8):
                w = [along[z + i, t, ys] for i in range(-1, 3)]
                c = [cross[z + i, t, ys] for i in range(-2, 3)]
                even, odd = even_step(w, c), odd_step(w[1:], c[2:])
                scale = jnp.where((col == 0) & (z == DEEP), 0.0, factors[0][t % 2])
                even = field[z, t, strided(ys), :] + scale * even
                odd = field[z + 1, t, strided(ys), :] + factors[1][t % 2] * odd
                field[z, t, strided(ys), :] = even
                field[z + 1, t, strided(ys), :] = odd
        return carry

    def update_all(sweep):
        low_pair = jnp.where(col == 0, DEEP // 2, sweep + 1)
        high_pair = jnp.where(col == cols - 1, (DEEP + layers) // 2, total // 2 - sweep - 1)
        lax.fori_loop(low_pair, high_pair, update, 0)

    begin = jnp.where(col == 0, DEEP, 0)
    end = jnp.where(col == cols - 1, DEEP + layers + 1, total - 1)

    def first_lateral(i, carry):
        z = lax.rem(i + DEEP, total)
        pltpu.make_async_copy(wide_ref.at[0], field.at[z], sems.at[z]).wait()

        @pl.when((z >= begin) & (z < end))
        def _():
            lateral(z, 0)

        return carry

    def later_sweep(sweep, carry):
        lax.fori_loop(
            jnp.maximum(begin, 2 * sweep), jnp.minimum(end, total - 2 * sweep - 1), lateral, 0
        )
        update_all(sweep)
        return carry

    @pl.when(col == 0)
    def _():
        clear = jnp.zeros((8, Y_GROUPS, SUB, LANES), jnp.float32)
        for z in (DEEP - 2, DEEP - 1):
            along[z] = clear
            cross[z] = clear

    lax.fori_loop(0, total, first_lateral, 0)
    update_all(0)
    lax.fori_loop(1, SWEEPS, later_sweep, 0)

    row = lax.broadcasted_iota(jnp.int32, (rows, LANES), 0)
    by_row = jnp.where(row % 2 == 0, stored(0), stored(1)).astype(jnp.float32)
    back_row = jnp.where(row % 2 == 0, 1 / stored(0), 1 / stored(1)).astype(jnp.float32)

    @pl.when(col == 0)
    def _():
        all_change.wait()
        for t in range(8):
            top = speed_ref[t, DEEP : DEEP + rows, :] * (by_row * (0.5 * stored(0) * stored(t % 2)))
            field[DEEP, t, DEEP : DEEP + rows, :] += top
            for z in range(1, layers):
                field[DEEP + z, t, DEEP : DEEP + rows, :] += change[z, t]

    @pl.when(col == 1)
    def _():
        one_change.wait()
        for t in range(8):
            field[DEEP, t, DEEP : DEEP + rows, :] += change[0, t]

    for z in range(layers):
        for t in range(8):
            value = field[DEEP + z, t, DEEP : DEEP + rows, :]
            cut(value * (back_row * (1 / (stored(z % 2) * stored(t % 2)))), rows * (z + 1), t)

    def write(at, value):
        velocity_ref[:, at] = value[:rows]
        out_ref[:, :, at] = value[rows:].reshape(layers, rows, 256)

    choose.wait()
    plain_columns(select, parts[...], count, write)


def base_sweeps(where, wide, zlow, zhigh, change, speed, select):
    layers, _, rows, _ = change.shape
    total = layers + 2 * DEEP
    work = pltpu.VMEM((total, 8, Y_GROUPS, SUB, LANES), jnp.float32)
    line = pltpu.VMEM((8, Y_GROUPS, SUB, LANES), jnp.float32)
    return pl.pallas_call(
        base_kernel,
        out_shape=(f32(rows, 8 * LANES), f32(layers, rows, 8 * LANES)),
        in_specs=[SMEM] + [HBM] * 4 + [VMEM, HBM],
        out_specs=(VMEM, VMEM),
        scratch_shapes=[
            pltpu.VMEM((total, 8, Y_ROWS, LANES), jnp.float32),
            work, work, line, line,
            pltpu.VMEM((2, 2, Y_GROUPS, SUB, LANES), jnp.float32),
            pltpu.VMEM((layers, 8, rows, LANES), jnp.float32),
            pltpu.VMEM(select.shape, jnp.bfloat16),
            pltpu.VMEM((2 * (layers + 1) * rows, 8 * LANES), jnp.bfloat16),
            pltpu.SemaphoreType.DMA((total + 3,)),
        ],
        compiler_params=params(50),
        cost_estimate=cost(25),
        name="base_sweeps",
    )(where, wide, zlow, zhigh, change, speed, select)


mass_even = (-1.0 / 15.0, 2.0 / 15.0, 8.0 / 15.0, 2.0 / 15.0, -1.0 / 15.0)
mass_odd = (0.0, 2.0 / 15.0, 16.0 / 15.0, 2.0 / 15.0, 0.0)


def mass_along(padded, axis):
    count = padded.shape[axis] - 4
    pieces = [lax.slice_in_dim(padded, i, i + count, axis=axis) for i in range(5)]
    even = sum(mass_even[i] * pieces[i] for i in range(5))
    odd = sum(mass_odd[i] * pieces[i] for i in range(1, 4))
    at_even = lax.broadcasted_iota(jnp.int32, even.shape, axis) % 2 == 0
    return jnp.where(at_even, even, odd)


def with_rows(x, width):
    size = lax.axis_size("vol")
    up = [(i, i + 1) for i in range(size - 1)]
    down = [(j, i) for i, j in up]
    before = lax.ppermute(x[-width:], "vol", up)
    after = lax.ppermute(x[:width], "vol", down)
    return jnp.concatenate([before, x, after], axis=0)


def stepwise(flux, metric):
    root = jnp.sqrt(metric)

    def dot(a, b):
        return lax.psum(jnp.sum(a * b), "vol")

    def step(_, state):
        solved, residual, direction, norm = state
        padded = jnp.pad(with_rows(root * direction, 2), ((0, 0), (2, 2)))
        image = root * mass_along(mass_along(padded, 1), 0)
        alpha = norm / dot(direction, image)
        solved = solved + alpha * direction
        residual = residual - alpha * image
        after = dot(residual, residual)
        direction = residual + after / norm * direction
        return solved, residual, direction, after

    state = (jnp.zeros_like(flux), flux, flux, dot(flux, flux))
    return with_rows(lax.fori_loop(0, ITERS, step, state)[0], DEEP)


def after(x, *others):
    return lax.optimization_barrier((x,) + others)[0]


def on_device(face_area, face_speed, face_node, face_count, surface_metric, displacement):
    vols, cols = lax.axis_size("vol"), lax.axis_size("col")
    vol, col = lax.axis_index("vol"), lax.axis_index("col")
    core = col % 2
    where = [core, col, jnp.int32(cols), vol, jnp.int32(vols), jnp.int32(displacement.shape[1])]
    where = jnp.stack(where).astype(jnp.int32).reshape(1, 6)
    up = [(i, i + 1) for i in range(vols - 1)]
    down = [(j, i) for i, j in up]
    col_up = [(i, i + 1) for i in range(cols - 1)]
    col_down = [(j, i) for i, j in col_up]
    packed = displacement.shape[0] * DEEP

    select = plain_selection()

    def moved(x, steps):
        dv, dc = steps
        pairs = [
            (i * cols + j, (i + dv) * cols + j + dc)
            for i in range(vols)
            for j in range(cols)
            if 0 <= i + dv < vols and 0 <= j + dc < cols
        ]
        return lax.ppermute(x, ("vol", "col"), pairs)

    rows_up, rows_down = outgoing_rows(displacement, surface_metric)
    keep, send = face_sums(where, face_count, after(face_area, rows_up), face_speed, face_node)
    with jax.named_scope("flux_sum"):
        keep = keep + lax.ppermute(send, "col", [(j, j ^ 1) for j in range(cols)])
        turned = [
            lax.ppermute(keep, "col", [(j, (j + 2 * k) % cols) for j in range(cols)]) for k in (1, 2, 3)
        ]
    with jax.named_scope("row_halo"):
        rows_before, rows_after = moved(rows_up, (1, 0)), moved(rows_down, (-1, 0))
    wide, root = regroup(displacement, surface_metric, rows_before, rows_after)
    with jax.named_scope("flux_sum"):
        turned = lax.optimization_barrier((*turned, wide))
        own = (keep + turned[1]) + (turned[0] + turned[2])
    with jax.named_scope("flux_halo"):
        other = lax.ppermute(own, "col", [(j, j ^ 1) for j in range(cols)])
        pairs = []
        for i in range(vols):
            for j in range(cols):
                to = i - 1 if j % 2 == 0 else i + 1
                if 0 <= to < vols:
                    pairs.append((i * cols + j, to * cols + j))
        same = lax.ppermute(own, ("vol", "col"), pairs)
        cross = lax.ppermute(same, "col", [(j, j ^ 1) for j in range(cols)])

    with jax.named_scope("depth_halo"):
        sent = after(wide, own)
        zlow, zhigh = moved(sent, (0, 1)), moved(sent, (0, -1))
    basis, spread = surface_basis(where, vols, own, other, same, cross, root)
    with jax.named_scope("gather_sums"):
        gathered = lax.all_to_all(spread, "vol", 0, 0)
    speed, flag = surface_solve(basis, gathered)

    def finish(speed):
        change = surface_change(where, speed, displacement.shape[0], displacement.shape[1])
        return base_sweeps(where, wide, zlow, zhigh, change, speed, select)

    def step_by_step():
        low = jnp.where(core == 0, own, other)
        high = jnp.where(core == 0, other, own)
        flux = jnp.concatenate([low, high], axis=1)
        flux = flux.transpose(1, 2, 0).reshape(surface_metric.shape)
        solved = stepwise(flux, surface_metric)
        return finish(solved.reshape(Y_ROWS, LANES, 8).transpose(2, 0, 1))

    return lax.cond(flag[0, 0] > 0, lambda: finish(speed), step_by_step)


def solution(mesh):
    in_specs = (
        P("vol", "col"),
        P("vol", "col"),
        P("vol", "col"),
        P("vol", "col"),
        P("vol", None),
        P("col", "vol", None),
    )
    out_specs = (P("vol", None), P("col", "vol", None))
    return jax.shard_map(
        on_device, mesh=mesh, in_specs=in_specs, out_specs=out_specs, check_vma=False
    )
```

```python
import jax
import jax.numpy as jnp
import numpy as np
from jax import lax
from jax.experimental import pallas as pl
from jax.experimental.pallas import tpu as pltpu
from jax.sharding import PartitionSpec as P

ITERS = 10
SWEEPS = 4
LANES = 128
SUB = 8
MIB = 1024 * 1024
DEEP = 2 * SWEEPS
HALO = 32
ROWS = 128
GROUPS = 16
Y_GROUPS = 10
Y_ROWS = 80

BASIS_LOW = 0.1
BASIS_HIGH = 12.0
CONDITION_MAX = 2000.0


def rolled(x, shift, axis):
    return pltpu.roll(x, shift % x.shape[axis], axis)


def column_ring(tiles):
    n = len(tiles)
    lane = lax.broadcasted_iota(jnp.int32, tiles[0].shape, 1)
    first, last = lane == 0, lane == LANES - 1
    return (
        [jnp.where(first, 0.0, rolled(tiles[j], 1, 1)) for j in (n - 2, n - 1)]
        + list(tiles)
        + [jnp.where(last, 0.0, rolled(tiles[j], -1, 1)) for j in (0, 1)]
    )


def row_ring(rows):
    n = len(rows)
    return (
        [rolled(rows[j], 1, 0) for j in (n - 2, n - 1)]
        + list(rows)
        + [rolled(rows[j], -1, 0) for j in (0, 1)]
    )


def mass_line(padded, index):
    i = index + 2
    near = padded[i - 1] + padded[i + 1]
    if index % 2:
        return near + 4.0 * padded[i]
    return (near + 8.0 * padded[i]) - (padded[i - 2] + padded[i + 2])


def both_line(padded, index):
    i = index + 2
    near = padded[i - 1] + padded[i + 1]
    return (8.0 / 3.0 if index % 2 else 22.0 / 3.0) * padded[i] - near


def stored(parity):
    return 1.0 if parity else 0.5


def given(parity):
    return 0.5 if parity else 1.0


SMEM = pl.BlockSpec(memory_space=pltpu.SMEM)
VMEM = pl.BlockSpec(memory_space=pltpu.VMEM)
HBM = pl.BlockSpec(memory_space=pltpu.HBM)


def f32(*shape):
    return jax.ShapeDtypeStruct(shape, jnp.float32)


def params(mib):
    return pltpu.CompilerParams(vmem_limit_bytes=mib * MIB)


def cost(us):
    return pl.CostEstimate(flops=0, bytes_accessed=int(us * 100_000), transcendentals=0)


def split(x):
    first = x.astype(jnp.bfloat16)
    return first, (x - first.astype(jnp.float32)).astype(jnp.bfloat16)


def to_blocked(j):
    x = lax.broadcasted_iota(jnp.int32, (1024, 256), 0)
    n = lax.broadcasted_iota(jnp.int32, (1024, 256), 1)
    hit = x == 8 * (n & 127) + j + (n >> 7)
    return jnp.where(hit, 1.0, 0.0).astype(jnp.bfloat16)


def plain_selection():
    k = np.arange(1024)
    out = np.zeros((1024, 1024), np.float32)
    out[k, 8 * (k % LANES) + k // LANES] = 1.0
    return jnp.asarray(out, jnp.bfloat16)


def regroup_kernel(block_ref, metric_ref, before_ref, after_ref, wide_ref, root_ref, parts_ref):
    layers, rows, _ = block_ref.shape
    packed = DEEP * layers
    total = layers * Y_ROWS + ROWS

    def put(at, value):
        first, second = split(value)
        parts_ref[at : at + value.shape[0], :] = first
        parts_ref[total + at : total + at + value.shape[0], :] = second

    for z in range(layers):
        put(Y_ROWS * z, before_ref[DEEP * z : DEEP * (z + 1), :])
        put(Y_ROWS * z + DEEP, block_ref[z])
        put(Y_ROWS * z + DEEP + rows, after_ref[DEEP * z : DEEP * (z + 1), :])
    row = lax.broadcasted_iota(jnp.int32, (Y_ROWS, LANES), 0)
    by_row = jnp.where(row % 2 == 0, stored(0), stored(1)).astype(jnp.float32)
    at = layers * Y_ROWS
    put(at, jnp.sqrt(before_ref[packed:, :]))
    put(at + HALO, jnp.sqrt(metric_ref[...]))
    put(at + HALO + rows, jnp.sqrt(after_ref[packed:, :]))
    for j in range(0, 8, 2):
        pair = jnp.dot(parts_ref[...], to_blocked(j), preferred_element_type=jnp.float32)
        pair = pair[:total] + pair[total:]
        for i in range(2):
            tile = pair[:, LANES * i : LANES * (i + 1)]
            for z in range(layers):
                wide_ref[z, j + i] = tile[Y_ROWS * z : Y_ROWS * (z + 1)] * (by_row * (stored(z % 2) * stored(i)))
            root_ref[j + i] = tile[layers * Y_ROWS :]


def regroup(block, metric, before, after):
    layers, rows, cols = block.shape
    return pl.pallas_call(
        regroup_kernel,
        out_shape=(f32(layers, 8, Y_ROWS, LANES), f32(8, ROWS, LANES)),
        in_specs=[VMEM] * 4,
        out_specs=(VMEM, VMEM),
        scratch_shapes=[pltpu.VMEM((2 * (Y_ROWS * layers + ROWS), cols), jnp.bfloat16)],
        compiler_params=params(32),
        cost_estimate=cost(150),
        name="regroup",
    )(block, metric, before, after)


def plain_columns(select_ref, parts, rows, write):
    for q in range(4):
        at = slice(256 * q, 256 * (q + 1))
        value = jnp.dot(parts, select_ref[:, at], preferred_element_type=jnp.float32)
        write(at, value[:rows] + value[rows:])


def face_kernel(
    where_ref, count_ref, area_ref, speed_ref, node_ref,
    keep_ref, send_ref, area, speed, nodes, acc_ref, sems,
):
    slots = area_ref.shape[1]
    fetches = [
        pltpu.make_async_copy(source, target, sems.at[i])
        for i, (source, target) in enumerate(((area_ref, area), (speed_ref, speed), (node_ref, nodes)))
    ]
    for fetch in fetches:
        fetch.start()
    chunk = min(4096, slots)
    core = where_ref[0, 0]
    ids = lax.broadcasted_iota(jnp.int32, (256, chunk), 0)
    ids = ids.astype(jnp.float32).astype(jnp.bfloat16)
    zero = jnp.zeros((), jnp.bfloat16)
    one = jnp.ones((), jnp.bfloat16)
    contract = (((1,), (1,)), ((), ()))
    acc_ref[...] = jnp.zeros_like(acc_ref)
    for fetch in fetches:
        fetch.wait()

    def wide(x):
        return jnp.broadcast_to(x.astype(jnp.bfloat16), (256, chunk))

    def body(step, carry):
        at = pl.ds(pl.multiple_of(step * chunk, chunk), chunk)
        slot = lax.broadcasted_iota(jnp.int32, (1, chunk), 1) + step * chunk
        value = jnp.where(slot < count_ref[0, 0], area[:, at] * speed[:, at], 0.0)
        node = nodes[:, at]
        low = (((node & 1) << 7) + ((node >> 3) & 127)).astype(jnp.float32)
        high = (((node >> 1) & 3) * 64 + (node >> 10)).astype(jnp.float32)
        first = value.astype(jnp.bfloat16)
        second = value - first.astype(jnp.float32)
        here = wide(high) == ids
        upper = jnp.where(here, wide(first), zero)
        lower = jnp.where(here, wide(second), zero)
        columns = jnp.where(wide(low) == ids, one, zero)
        both = jnp.concatenate([upper, lower], axis=0)
        acc_ref[...] += lax.dot_general(both, columns, contract, preferred_element_type=jnp.float32)
        return carry

    lax.fori_loop(0, slots // chunk, body, 0)
    for j in range(8):
        at, lanes = 64 * (j // 2), slice(LANES * (j % 2), LANES * (j % 2 + 1))
        near, far = at + 32 * core, at + 32 - 32 * core
        keep_ref[j] = acc_ref[pl.ds(near, 32), lanes] + acc_ref[pl.ds(256 + near, 32), lanes]
        send_ref[j] = acc_ref[pl.ds(far, 32), lanes] + acc_ref[pl.ds(256 + far, 32), lanes]


def face_sums(where, count, area, speed, node):
    half = f32(8, 32, LANES)
    return pl.pallas_call(
        face_kernel,
        out_shape=(half, half),
        in_specs=[SMEM, SMEM] + [HBM] * 3,
        out_specs=(VMEM, VMEM),
        scratch_shapes=[
            pltpu.VMEM(area.shape, jnp.float32),
            pltpu.VMEM(area.shape, jnp.float32),
            pltpu.VMEM(area.shape, jnp.int32),
            pltpu.VMEM((512, 256), jnp.float32),
            pltpu.SemaphoreType.DMA((3,)),
        ],
        compiler_params=params(50),
        cost_estimate=cost(7),
        name="face_sums",
    )(where, count, area, speed, node)


def cut_kernel(block_ref, metric_ref, up_ref, down_ref, sems):
    layers, rows, _ = block_ref.shape
    copies = []
    for out_ref, row, root_row in ((up_ref, rows - DEEP, rows - HALO), (down_ref, 0, 0)):
        for z in range(layers):
            part = block_ref.at[z, pl.ds(row, DEEP), :]
            copies.append((part, out_ref.at[pl.ds(DEEP * z, DEEP), :]))
        part = metric_ref.at[pl.ds(root_row, HALO), :]
        copies.append((part, out_ref.at[pl.ds(DEEP * layers, HALO), :]))
    copies = [pltpu.make_async_copy(*pair, sems.at[i]) for i, pair in enumerate(copies)]
    for copy in copies:
        copy.start()
    for copy in copies:
        copy.wait()


def outgoing_rows(block, metric):
    layers, _, cols = block.shape
    rows = f32(DEEP * layers + HALO, cols)
    return pl.pallas_call(
        cut_kernel,
        out_shape=(rows, rows),
        in_specs=[HBM, HBM],
        out_specs=(VMEM, VMEM),
        scratch_shapes=[pltpu.SemaphoreType.DMA((2 * layers + 2,))],
        compiler_params=params(56),
        cost_estimate=cost(1),
        name="outgoing_rows",
    )(block, metric)


def basis_kernel(
    where_ref, own_ref, other_ref, same_ref, cross_ref, root_ref,
    field, sums_ref, rows, root, outer, line, partial,
):
    core = where_ref[0, 0]
    centre = (BASIS_LOW + BASIS_HIGH) / 2
    scale = 2 / (BASIS_HIGH - BASIS_LOW)
    for t in range(8):
        rows[t, pl.ds(32 + 32 * core, 32), :] = own_ref[t]
        rows[t, pl.ds(64 - 32 * core, 32), :] = other_ref[t]
        rows[t, pl.ds(96 * core, 32), :] = cross_ref[t]
        rows[t, pl.ds(96 - 96 * core, 32), :] = same_ref[t]
    for t in range(8):
        for ys in range(GROUPS):
            field[0, t, ys] = rows[t, pl.ds(ys, SUB, stride=GROUPS), :]
            value = root_ref[t, pl.ds(ys, SUB, stride=GROUPS), :]
            root[t, ys] = value * (stored(t % 2) * stored(ys % 2))
            outer[t, ys] = value * (2 * scale * 4.0 / 225.0 / (given(t % 2) * given(ys % 2)))

    group = lax.broadcasted_iota(jnp.int32, (SUB, LANES), 0)
    own_rows = jnp.where((group >= 2) & (group < 6), 1.0, 0.0).astype(jnp.float32)

    def step(k, begin, end):
        def put(k, t, ys, value):
            if not end:
                field[k, t, ys] = value

        for ys in range(GROUPS):
            padded = column_ring([field[k, t, ys] * root[t, ys] for t in range(8)])
            for t in range(8):
                line[ys, t] = mass_line(padded, t)
        squares, shifts = [], []
        for t in range(8):
            square = jnp.zeros((SUB, LANES), jnp.float32)
            shifted = jnp.zeros((SUB, LANES), jnp.float32)
            padded = row_ring([line[ys, t] for ys in range(GROUPS)])
            for ys in range(GROUPS):
                now = field[k, t, ys]
                later = outer[t, ys] * mass_line(padded, ys) - (2 * centre * scale) * now
                later = 0.5 * later if begin else later - field[k - 1, t, ys]
                put(k + 1, t, ys, later)
                square = square + now * now
                shifted = shifted + later * now
            squares.append(square)
            shifts.append(shifted)

        def add(parts):
            while len(parts) > 1:
                parts = [parts[i] + parts[i + 1] for i in range(0, len(parts), 2)]
            return jnp.sum(parts[0] * own_rows, axis=0, keepdims=True)

        partial[pl.ds(2 * k, 1), :] = add(squares)
        partial[pl.ds(2 * k + 1, 1), :] = add(shifts)

    def later_step(k, carry):
        step(k, False, False)
        return carry

    partial[...] = jnp.zeros_like(partial)
    step(0, True, False)
    lax.fori_loop(1, ITERS - 1, later_step, 0)
    step(ITERS - 1, False, True)
    whole = jnp.sum(partial[...], axis=1, keepdims=True)
    row = lax.broadcasted_iota(jnp.int32, partial.shape, 0)
    lane = lax.broadcasted_iota(jnp.int32, partial.shape, 1)
    line_of = jnp.sum(jnp.where(row == lane, whole, 0.0), axis=0, keepdims=True)
    sums_ref[...] = jnp.broadcast_to(line_of[None], sums_ref.shape)


def surface_basis(where, vols, own, other, same, cross, root):
    return pl.pallas_call(
        basis_kernel,
        out_shape=(f32(ITERS, 8, GROUPS, SUB, LANES), f32(vols, SUB, LANES)),
        in_specs=[SMEM] + [VMEM] * 5,
        out_specs=(VMEM, VMEM),
        scratch_shapes=[
            pltpu.VMEM((8, ROWS, LANES), jnp.float32),
            pltpu.VMEM((8, GROUPS, SUB, LANES), jnp.float32),
            pltpu.VMEM((8, GROUPS, SUB, LANES), jnp.float32),
            pltpu.VMEM((GROUPS, 8, SUB, LANES), jnp.float32),
            pltpu.VMEM((24, LANES), jnp.float32),
        ],
        compiler_params=params(24),
        cost_estimate=cost(7),
        name="surface_basis",
    )(where, own, other, same, cross, root)


def solve_weights():
    n = ITERS
    moment = np.zeros((2 * n, 2 * n))
    for m in range(2 * n):
        if m < 2:
            moment[m, m] = 1.0
        else:
            moment[m, m] = 2.0
            moment[m, m % 2] = -1.0
    centre, half = (BASIS_LOW + BASIS_HIGH) / 2, (BASIS_HIGH - BASIS_LOW) / 2
    weights = np.zeros((2 * n, 16, LANES))
    for i in range(n):
        for j in range(n):
            lower = abs(j - 1)
            for factor, index in (
                (centre / 2, i + j),
                (centre / 2, abs(i - j)),
                (half / 4, i + j + 1),
                (half / 4, abs(i - j - 1)),
                (half / 4, i + lower),
                (half / 4, abs(i - lower)),
            ):
                weights[:, i, j] += factor * moment[index]
        weights[:, i, n] += moment[i]
    return weights.astype(np.float32)


def solve_kernel(part_ref, sums_ref, weights_ref, out_ref, flag_ref, rows):
    n = ITERS
    total = sums_ref[0]
    for i in range(1, sums_ref.shape[0]):
        total = total + sums_ref[i]
    row = lax.broadcasted_iota(jnp.int32, (16, LANES), 0)
    lane = lax.broadcasted_iota(jnp.int32, (16, LANES), 1)
    system = jnp.where((lane == row + 16) & (row < n), 1.0, 0.0).astype(jnp.float32)
    for m in range(2 * n):
        system = system + weights_ref[m] * total[0:1, m : m + 1]
    centre = jnp.sum(jnp.where(lane == row, system, 0.0), axis=1, keepdims=True)
    for k in range(n):
        pivot_row = system[k : k + 1, :] / system[k : k + 1, k : k + 1]
        column = system[:, k : k + 1]
        system = jnp.where(row == k, pivot_row, system - column * pivot_row)
    inverse = jnp.sum(jnp.where(lane == row + 16, system, 0.0), axis=1, keepdims=True)
    figure = jnp.broadcast_to(centre * inverse, (16, LANES))
    inside = (row < n) & (lane == 0)
    least = jnp.min(jnp.where(inside, figure, 1.0))
    whole = jnp.sum(jnp.where(inside, figure, 0.0))
    flag_ref[0, 0] = jnp.where((least > 0.5) & (whole < CONDITION_MAX), 1, 0).astype(jnp.int32)
    weights = [jnp.broadcast_to(system[k : k + 1, n : n + 1], (SUB, LANES)) for k in range(n)]
    for t in range(8):
        for ys in range(GROUPS):
            value = weights[0] * part_ref[0, t, ys]
            for k in range(1, n):
                value = value + weights[k] * part_ref[k, t, ys]
            rows[t, pl.ds(ys, SUB, stride=GROUPS), :] = value
        out_ref[t] = rows[t, HALO - DEEP : HALO - DEEP + Y_ROWS, :]


def surface_solve(basis, sums):
    return pl.pallas_call(
        solve_kernel,
        out_shape=(f32(8, Y_ROWS, LANES), jax.ShapeDtypeStruct((1, 1), jnp.int32)),
        in_specs=[VMEM, VMEM, VMEM],
        out_specs=(VMEM, SMEM),
        scratch_shapes=[pltpu.VMEM((8, ROWS, LANES), jnp.float32)],
        compiler_params=params(24),
        cost_estimate=cost(3),
        name="surface_solve",
    )(basis, sums, jnp.asarray(solve_weights()))


def fill_factors(where_ref, factor):
    vol, vols, rows = where_ref[0, 3], where_ref[0, 4], where_ref[0, 5]
    group = lax.broadcasted_iota(jnp.int32, (SUB, LANES), 0)
    mass, stiff = (8.0, 16.0), (14.0, 16.0)
    for ys in range(Y_GROUPS):
        row = group * Y_GROUPS + ys
        outside = ((vol == 0) & (row < DEEP)) | ((vol == vols - 1) & (row >= DEEP + rows))
        py = ys % 2
        for pz in range(2):
            for px in range(2):
                value = -12.0 / (
                    stiff[pz] * mass[py] * mass[px]
                    + mass[pz] * (stiff[py] * mass[px] + mass[py] * stiff[px])
                )
                for p in (pz, py, px):
                    value = value * stored(p) / given(p)
                factor[pz, px, ys] = jnp.where(outside, 0.0, jnp.float32(value))


def lateral_lines(get, line_a, line_b, put):
    for t in range(8):
        u = row_ring([get(t, ys) for ys in range(Y_GROUPS)])
        for ys in range(Y_GROUPS):
            m = mass_line(u, ys)
            line_a[t, ys] = m
            line_b[t, ys] = both_line(u, ys) - m
    for ys in range(Y_GROUPS):
        a = column_ring([line_a[t, ys] for t in range(8)])
        b = column_ring([line_b[t, ys] for t in range(8)])
        for t in range(8):
            put(t, ys, mass_line(a, t), both_line(a, t) + mass_line(b, t))


def even_step(w, c):
    near = c[1] + c[3]
    return (22.0 / 3.0 * w[1] - (w[0] + w[2])) + ((near + 8.0 * c[2]) - (c[0] + c[4]))


def odd_step(w, c):
    return (8.0 / 3.0 * w[1] - (w[0] + w[2])) + ((c[0] + c[2]) + 4.0 * c[1])


def strided(ys):
    return pl.ds(ys, SUB, stride=Y_GROUPS)


def change_kernel(
    where_ref, speed_ref, out_ref, cells, along, cross, line_a, line_b, factor, plain, sems,
):
    col = where_ref[0, 1]
    layers, _, rows, _ = out_ref.shape

    def lateral(z, carry):
        def put(t, ys, w, c):
            along[z, t, ys] = w
            cross[z, t, ys] = c

        lateral_lines(lambda t, ys: cells[z, t, ys], line_a, line_b, put)
        return carry

    def set_top():
        for t in range(8):
            for ys in range(Y_GROUPS):
                scale = 0.5 * stored(0) * stored(t % 2) * stored(ys % 2)
                cells[2, t, ys] = scale * speed_ref[t, strided(ys), :]

    def send(first, count):
        copies = []
        for z in range(first, first + count):
            for t in range(8):
                for ys in range(Y_GROUPS):
                    plain[z, t, strided(ys), :] = cells[z + 2, t, ys]
            copy = pltpu.make_async_copy(
                plain.at[z, :, pl.ds(DEEP, rows), :], out_ref.at[z], sems.at[z]
            )
            copy.start()
            copies.append(copy)
        for copy in copies:
            copy.wait()

    @pl.when(col == 0)
    def _():
        fill_factors(where_ref, factor)
        set_top()
        clear = jnp.zeros((8, Y_GROUPS, SUB, LANES), jnp.float32)
        for z in range(2):
            cross[z] = clear
            along[z] = clear

        def update(pair, carry):
            z = 2 * pair + 2
            for ys in range(Y_GROUPS):
                factors = [[factor[pz, px, ys] for px in range(2)] for pz in range(2)]
                for t in range(8):
                    w = [along[z + i, t, ys] for i in range(-1, 3)]
                    c = [cross[z + i, t, ys] for i in range(-2, 3)]
                    cells[z, t, ys] += factors[0][t % 2] * even_step(w, c)
                    cells[z + 1, t, ys] += factors[1][t % 2] * odd_step(w[1:], c[2:])
            return carry

        def one_sweep(sweep, carry):
            front = 2 * sweep + 2
            lax.fori_loop(2, front + 1, lateral, 0)
            lax.fori_loop(0, sweep, update, 0)
            for ys in range(Y_GROUPS):
                factors = [[factor[pz, px, ys] for px in range(2)] for pz in range(2)]
                for t in range(8):
                    w0, w1 = along[front - 1, t, ys], along[front, t, ys]
                    c0, c1, c2 = [cross[front + i, t, ys] for i in range(-2, 1)]
                    step = (22.0 / 3.0 * w1 - w0) + ((c1 + 8.0 * c2) - c0)
                    cells[front, t, ys] += factors[0][t % 2] * step
                    cells[front + 1, t, ys] = factors[1][t % 2] * (c2 - w1)
                    cells[front + 2, t, ys] = -factors[0][t % 2] * c2
            set_top()
            return carry

        lax.fori_loop(0, SWEEPS, one_sweep, 0)
        send(1, layers - 1)

    @pl.when(col == 1)
    def _():
        fill_factors(where_ref, factor)
        set_top()

        def one_sweep(sweep, carry):
            lateral(2, 0)
            for t in range(8):
                for ys in range(Y_GROUPS):
                    cells[2, t, ys] = -factor[0, t % 2, ys] * cross[2, t, ys]
            return carry

        lax.fori_loop(0, SWEEPS, one_sweep, 0)
        send(0, 1)


def surface_change(where, speed, layers, rows):
    work = pltpu.VMEM((layers + 2, 8, Y_GROUPS, SUB, LANES), jnp.float32)
    line = pltpu.VMEM((8, Y_GROUPS, SUB, LANES), jnp.float32)
    return pl.pallas_call(
        change_kernel,
        out_shape=f32(layers, 8, rows, LANES),
        in_specs=[SMEM, VMEM],
        out_specs=HBM,
        scratch_shapes=[
            pltpu.VMEM((layers + 3, 8, Y_GROUPS, SUB, LANES), jnp.float32),
            work, work, line, line,
            pltpu.VMEM((2, 2, Y_GROUPS, SUB, LANES), jnp.float32),
            pltpu.VMEM((layers, 8, Y_ROWS, LANES), jnp.float32),
            pltpu.SemaphoreType.DMA((layers,)),
        ],
        compiler_params=params(32),
        cost_estimate=cost(8),
        name="surface_change",
    )(where, speed)


def base_kernel(
    where_ref, wide_ref, zlow_ref, zhigh_ref, change_ref, speed_ref, select_hbm_ref,
    velocity_ref, out_ref, field, along, cross, line_a, line_b, factor, change, select, parts, sems,
):
    col, cols = where_ref[0, 1], where_ref[0, 2]
    layers, _, rows, _ = change_ref.shape
    total = layers + 2 * DEEP
    arrivals = []
    for i in range(total):
        z = (i + DEEP) % total
        source = wide_ref if i < layers else zhigh_ref if i < layers + DEEP else zlow_ref
        arrivals.append(pltpu.make_async_copy(source.at[i % DEEP], field.at[z], sems.at[z]))
    for arrival in arrivals:
        arrival.start()
    choose = pltpu.make_async_copy(select_hbm_ref, select, sems.at[total + 2])
    choose.start()
    all_change = pltpu.make_async_copy(
        change_ref.at[pl.ds(1, layers - 1)], change.at[pl.ds(1, layers - 1)], sems.at[total]
    )
    one_change = pltpu.make_async_copy(
        change_ref.at[pl.ds(0, 1)], change.at[pl.ds(0, 1)], sems.at[total + 1]
    )
    pl.when(col == 0)(all_change.start)
    pl.when(col == 1)(one_change.start)
    fill_factors(where_ref, factor)
    count = (layers + 1) * rows

    def cut(value, at, t):
        first, second = split(value)
        lanes = slice(LANES * t, LANES * (t + 1))
        parts[at : at + rows, lanes] = first
        parts[count + at : count + at + rows, lanes] = second

    for t in range(8):
        cut(speed_ref[t, DEEP : DEEP + rows, :], 0, t)

    def lateral(z, carry):
        def put(t, ys, w, c):
            along[z, t, ys] = w
            cross[z, t, ys] = c

        lateral_lines(lambda t, ys: field[z, t, strided(ys), :], line_a, line_b, put)
        return carry

    def update(pair, carry):
        z = 2 * pair
        for ys in range(Y_GROUPS):
            factors = [[factor[pz, px, ys] for px in range(2)] for pz in range(2)]
            for t in range(8):
                w = [along[z + i, t, ys] for i in range(-1, 3)]
                c = [cross[z + i, t, ys] for i in range(-2, 3)]
                even, odd = even_step(w, c), odd_step(w[1:], c[2:])
                scale = jnp.where((col == 0) & (z == DEEP), 0.0, factors[0][t % 2])
                even = field[z, t, strided(ys), :] + scale * even
                odd = field[z + 1, t, strided(ys), :] + factors[1][t % 2] * odd
                field[z, t, strided(ys), :] = even
                field[z + 1, t, strided(ys), :] = odd
        return carry

    def update_all(sweep):
        low_pair = jnp.where(col == 0, DEEP // 2, sweep + 1)
        high_pair = jnp.where(col == cols - 1, (DEEP + layers) // 2, total // 2 - sweep - 1)
        lax.fori_loop(low_pair, high_pair, update, 0)

    begin = jnp.where(col == 0, DEEP, 0)
    end = jnp.where(col == cols - 1, DEEP + layers + 1, total - 1)

    def first_lateral(i, carry):
        z = lax.rem(i + DEEP, total)
        pltpu.make_async_copy(wide_ref.at[0], field.at[z], sems.at[z]).wait()

        @pl.when((z >= begin) & (z < end))
        def _():
            lateral(z, 0)

        return carry

    def later_sweep(sweep, carry):
        lax.fori_loop(
            jnp.maximum(begin, 2 * sweep), jnp.minimum(end, total - 2 * sweep - 1), lateral, 0
        )
        update_all(sweep)
        return carry

    @pl.when(col == 0)
    def _():
        clear = jnp.zeros((8, Y_GROUPS, SUB, LANES), jnp.float32)
        for z in (DEEP - 2, DEEP - 1):
            along[z] = clear
            cross[z] = clear

    lax.fori_loop(0, total, first_lateral, 0)
    update_all(0)
    lax.fori_loop(1, SWEEPS, later_sweep, 0)

    row = lax.broadcasted_iota(jnp.int32, (rows, LANES), 0)
    by_row = jnp.where(row % 2 == 0, stored(0), stored(1)).astype(jnp.float32)
    back_row = jnp.where(row % 2 == 0, 1 / stored(0), 1 / stored(1)).astype(jnp.float32)

    @pl.when(col == 0)
    def _():
        all_change.wait()
        for t in range(8):
            top = speed_ref[t, DEEP : DEEP + rows, :] * (by_row * (0.5 * stored(0) * stored(t % 2)))
            field[DEEP, t, DEEP : DEEP + rows, :] += top
            for z in range(1, layers):
                field[DEEP + z, t, DEEP : DEEP + rows, :] += change[z, t]

    @pl.when(col == 1)
    def _():
        one_change.wait()
        for t in range(8):
            field[DEEP, t, DEEP : DEEP + rows, :] += change[0, t]

    for z in range(layers):
        for t in range(8):
            value = field[DEEP + z, t, DEEP : DEEP + rows, :]
            cut(value * (back_row * (1 / (stored(z % 2) * stored(t % 2)))), rows * (z + 1), t)

    def write(at, value):
        velocity_ref[:, at] = value[:rows]
        out_ref[:, :, at] = value[rows:].reshape(layers, rows, 256)

    choose.wait()
    plain_columns(select, parts[...], count, write)


def base_sweeps(where, wide, zlow, zhigh, change, speed, select):
    layers, _, rows, _ = change.shape
    total = layers + 2 * DEEP
    work = pltpu.VMEM((total, 8, Y_GROUPS, SUB, LANES), jnp.float32)
    line = pltpu.VMEM((8, Y_GROUPS, SUB, LANES), jnp.float32)
    return pl.pallas_call(
        base_kernel,
        out_shape=(f32(rows, 8 * LANES), f32(layers, rows, 8 * LANES)),
        in_specs=[SMEM] + [HBM] * 4 + [VMEM, HBM],
        out_specs=(VMEM, VMEM),
        scratch_shapes=[
            pltpu.VMEM((total, 8, Y_ROWS, LANES), jnp.float32),
            work, work, line, line,
            pltpu.VMEM((2, 2, Y_GROUPS, SUB, LANES), jnp.float32),
            pltpu.VMEM((layers, 8, rows, LANES), jnp.float32),
            pltpu.VMEM(select.shape, jnp.bfloat16),
            pltpu.VMEM((2 * (layers + 1) * rows, 8 * LANES), jnp.bfloat16),
            pltpu.SemaphoreType.DMA((total + 3,)),
        ],
        compiler_params=params(50),
        cost_estimate=cost(25),
        name="base_sweeps",
    )(where, wide, zlow, zhigh, change, speed, select)


mass_even = (-1.0 / 15.0, 2.0 / 15.0, 8.0 / 15.0, 2.0 / 15.0, -1.0 / 15.0)
mass_odd = (0.0, 2.0 / 15.0, 16.0 / 15.0, 2.0 / 15.0, 0.0)


def mass_along(padded, axis):
    count = padded.shape[axis] - 4
    pieces = [lax.slice_in_dim(padded, i, i + count, axis=axis) for i in range(5)]
    even = sum(mass_even[i] * pieces[i] for i in range(5))
    odd = sum(mass_odd[i] * pieces[i] for i in range(1, 4))
    at_even = lax.broadcasted_iota(jnp.int32, even.shape, axis) % 2 == 0
    return jnp.where(at_even, even, odd)


def with_rows(x, width):
    size = lax.axis_size("vol")
    up = [(i, i + 1) for i in range(size - 1)]
    down = [(j, i) for i, j in up]
    before = lax.ppermute(x[-width:], "vol", up)
    after = lax.ppermute(x[:width], "vol", down)
    return jnp.concatenate([before, x, after], axis=0)


def stepwise(flux, metric):
    root = jnp.sqrt(metric)

    def dot(a, b):
        return lax.psum(jnp.sum(a * b), "vol")

    def step(_, state):
        solved, residual, direction, norm = state
        padded = jnp.pad(with_rows(root * direction, 2), ((0, 0), (2, 2)))
        image = root * mass_along(mass_along(padded, 1), 0)
        alpha = norm / dot(direction, image)
        solved = solved + alpha * direction
        residual = residual - alpha * image
        after = dot(residual, residual)
        direction = residual + after / norm * direction
        return solved, residual, direction, after

    state = (jnp.zeros_like(flux), flux, flux, dot(flux, flux))
    return with_rows(lax.fori_loop(0, ITERS, step, state)[0], DEEP)


def after(x, *others):
    return lax.optimization_barrier((x,) + others)[0]


def on_device(face_area, face_speed, face_node, face_count, surface_metric, displacement):
    vols, cols = lax.axis_size("vol"), lax.axis_size("col")
    vol, col = lax.axis_index("vol"), lax.axis_index("col")
    core = col % 2
    where = [core, col, jnp.int32(cols), vol, jnp.int32(vols), jnp.int32(displacement.shape[1])]
    where = jnp.stack(where).astype(jnp.int32).reshape(1, 6)
    up = [(i, i + 1) for i in range(vols - 1)]
    down = [(j, i) for i, j in up]
    col_up = [(i, i + 1) for i in range(cols - 1)]
    col_down = [(j, i) for i, j in col_up]
    packed = displacement.shape[0] * DEEP

    select = plain_selection()

    def moved(x, steps):
        dv, dc = steps
        pairs = [
            (i * cols + j, (i + dv) * cols + j + dc)
            for i in range(vols)
            for j in range(cols)
            if 0 <= i + dv < vols and 0 <= j + dc < cols
        ]
        return lax.ppermute(x, ("vol", "col"), pairs)

    rows_up, rows_down = outgoing_rows(displacement, surface_metric)
    keep, send = face_sums(where, face_count, after(face_area, rows_up), face_speed, face_node)
    with jax.named_scope("flux_sum"):
        keep = keep + lax.ppermute(send, "col", [(j, j ^ 1) for j in range(cols)])
        turned = [
            lax.ppermute(keep, "col", [(j, (j + 2 * k) % cols) for j in range(cols)]) for k in (1, 2, 3)
        ]
    with jax.named_scope("row_halo"):
        rows_before, rows_after = moved(rows_up, (1, 0)), moved(rows_down, (-1, 0))
    wide, root = regroup(displacement, surface_metric, rows_before, rows_after)
    with jax.named_scope("flux_sum"):
        turned = lax.optimization_barrier((*turned, wide))
        own = (keep + turned[1]) + (turned[0] + turned[2])
    with jax.named_scope("flux_halo"):
        other = lax.ppermute(own, "col", [(j, j ^ 1) for j in range(cols)])
        pairs = []
        for i in range(vols):
            for j in range(cols):
                to = i - 1 if j % 2 == 0 else i + 1
                if 0 <= to < vols:
                    pairs.append((i * cols + j, to * cols + j))
        same = lax.ppermute(own, ("vol", "col"), pairs)
        cross = lax.ppermute(same, "col", [(j, j ^ 1) for j in range(cols)])

    with jax.named_scope("depth_halo"):
        sent = after(wide, own)
        zlow, zhigh = moved(sent, (0, 1)), moved(sent, (0, -1))
    basis, spread = surface_basis(where, vols, own, other, same, cross, root)
    with jax.named_scope("gather_sums"):
        gathered = lax.all_to_all(spread, "vol", 0, 0)
    speed, flag = surface_solve(basis, gathered)

    def finish(speed):
        change = surface_change(where, speed, displacement.shape[0], displacement.shape[1])
        return base_sweeps(where, wide, zlow, zhigh, change, speed, select)

    def step_by_step():
        low = jnp.where(core == 0, own, other)
        high = jnp.where(core == 0, other, own)
        flux = jnp.concatenate([low, high], axis=1)
        flux = flux.transpose(1, 2, 0).reshape(surface_metric.shape)
        solved = stepwise(flux, surface_metric)
        return finish(solved.reshape(Y_ROWS, LANES, 8).transpose(2, 0, 1))

    return lax.cond(flag[0, 0] > 0, lambda: finish(speed), step_by_step)


def solution(mesh):
    in_specs = (
        P("vol", "col"),
        P("vol", "col"),
        P("vol", "col"),
        P("vol", "col"),
        P("vol", None),
        P("col", "vol", None),
    )
    out_specs = (P("vol", None), P("col", "vol", None))
    return jax.shard_map(
        on_device, mesh=mesh, in_specs=in_specs, out_specs=out_specs, check_vma=False
    )
```

```python
import jax
import jax.numpy as jnp
import numpy as np
from jax import lax
from jax.experimental import pallas as pl
from jax.experimental.pallas import tpu as pltpu
from jax.sharding import PartitionSpec as P

ITERS = 10
SWEEPS = 4
LANES = 128
SUB = 8
MIB = 1024 * 1024
DEEP = 2 * SWEEPS
HALO = 32
ROWS = 128
GROUPS = 16
Y_GROUPS = 10
Y_ROWS = 80

BASIS_LOW = 0.1
BASIS_HIGH = 12.0
CONDITION_MAX = 2000.0


def rolled(x, shift, axis):
    return pltpu.roll(x, shift % x.shape[axis], axis)


def column_ring(tiles):
    n = len(tiles)
    lane = lax.broadcasted_iota(jnp.int32, tiles[0].shape, 1)
    first, last = lane == 0, lane == LANES - 1
    return (
        [jnp.where(first, 0.0, rolled(tiles[j], 1, 1)) for j in (n - 2, n - 1)]
        + list(tiles)
        + [jnp.where(last, 0.0, rolled(tiles[j], -1, 1)) for j in (0, 1)]
    )


def row_ring(rows):
    n = len(rows)
    return (
        [rolled(rows[j], 1, 0) for j in (n - 2, n - 1)]
        + list(rows)
        + [rolled(rows[j], -1, 0) for j in (0, 1)]
    )


def mass_line(padded, index):
    i = index + 2
    near = padded[i - 1] + padded[i + 1]
    if index % 2:
        return near + 4.0 * padded[i]
    return (near + 8.0 * padded[i]) - (padded[i - 2] + padded[i + 2])


def both_line(padded, index):
    i = index + 2
    near = padded[i - 1] + padded[i + 1]
    return (8.0 / 3.0 if index % 2 else 22.0 / 3.0) * padded[i] - near


def stored(parity):
    return 1.0 if parity else 0.5


def given(parity):
    return 0.5 if parity else 1.0


SMEM = pl.BlockSpec(memory_space=pltpu.SMEM)
VMEM = pl.BlockSpec(memory_space=pltpu.VMEM)
HBM = pl.BlockSpec(memory_space=pltpu.HBM)


def f32(*shape):
    return jax.ShapeDtypeStruct(shape, jnp.float32)


def params(mib):
    return pltpu.CompilerParams(vmem_limit_bytes=mib * MIB)


def cost(us):
    return pl.CostEstimate(flops=0, bytes_accessed=int(us * 100_000), transcendentals=0)


def split(x):
    first = x.astype(jnp.bfloat16)
    return first, (x - first.astype(jnp.float32)).astype(jnp.bfloat16)


def to_blocked(j):
    x = lax.broadcasted_iota(jnp.int32, (1024, 256), 0)
    n = lax.broadcasted_iota(jnp.int32, (1024, 256), 1)
    hit = x == 8 * (n & 127) + j + (n >> 7)
    return jnp.where(hit, 1.0, 0.0).astype(jnp.bfloat16)


def plain_selection():
    k = np.arange(1024)
    out = np.zeros((1024, 1024), np.float32)
    out[k, 8 * (k % LANES) + k // LANES] = 1.0
    return jnp.asarray(out, jnp.bfloat16)


def regroup_kernel(block_ref, metric_ref, before_ref, after_ref, wide_ref, root_ref, parts_ref):
    layers, rows, _ = block_ref.shape
    packed = DEEP * layers
    total = layers * Y_ROWS + ROWS

    def put(at, value):
        first, second = split(value)
        parts_ref[at : at + value.shape[0], :] = first
        parts_ref[total + at : total + at + value.shape[0], :] = second

    for z in range(layers):
        put(Y_ROWS * z, before_ref[DEEP * z : DEEP * (z + 1), :])
        put(Y_ROWS * z + DEEP, block_ref[z])
        put(Y_ROWS * z + DEEP + rows, after_ref[DEEP * z : DEEP * (z + 1), :])
    row = lax.broadcasted_iota(jnp.int32, (Y_ROWS, LANES), 0)
    by_row = jnp.where(row % 2 == 0, stored(0), stored(1)).astype(jnp.float32)
    at = layers * Y_ROWS
    put(at, jnp.sqrt(before_ref[packed:, :]))
    put(at + HALO, jnp.sqrt(metric_ref[...]))
    put(at + HALO + rows, jnp.sqrt(after_ref[packed:, :]))
    for j in range(0, 8, 2):
        pair = jnp.dot(parts_ref[...], to_blocked(j), preferred_element_type=jnp.float32)
        pair = pair[:total] + pair[total:]
        for i in range(2):
            tile = pair[:, LANES * i : LANES * (i + 1)]
            for z in range(layers):
                wide_ref[z, j + i] = tile[Y_ROWS * z : Y_ROWS * (z + 1)] * (by_row * (stored(z % 2) * stored(i)))
            root_ref[j + i] = tile[layers * Y_ROWS :]


def regroup(block, metric, before, after):
    layers, rows, cols = block.shape
    return pl.pallas_call(
        regroup_kernel,
        out_shape=(f32(layers, 8, Y_ROWS, LANES), f32(8, ROWS, LANES)),
        in_specs=[VMEM] * 4,
        out_specs=(VMEM, VMEM),
        scratch_shapes=[pltpu.VMEM((2 * (Y_ROWS * layers + ROWS), cols), jnp.bfloat16)],
        compiler_params=params(32),
        cost_estimate=cost(150),
        name="regroup",
    )(block, metric, before, after)


def plain_columns(select_ref, parts, rows, write):
    for q in range(4):
        at = slice(256 * q, 256 * (q + 1))
        value = jnp.dot(parts, select_ref[:, at], preferred_element_type=jnp.float32)
        write(at, value[:rows] + value[rows:])


def face_kernel(
    where_ref, count_ref, area_ref, speed_ref, node_ref,
    keep_ref, send_ref, area, speed, nodes, acc_ref, sems,
):
    slots = area_ref.shape[1]
    fetches = [
        pltpu.make_async_copy(source, target, sems.at[i])
        for i, (source, target) in enumerate(((area_ref, area), (speed_ref, speed), (node_ref, nodes)))
    ]
    for fetch in fetches:
        fetch.start()
    chunk = min(4096, slots)
    core = where_ref[0, 0]
    ids = lax.broadcasted_iota(jnp.int32, (256, chunk), 0)
    ids = ids.astype(jnp.float32).astype(jnp.bfloat16)
    zero = jnp.zeros((), jnp.bfloat16)
    one = jnp.ones((), jnp.bfloat16)
    contract = (((1,), (1,)), ((), ()))
    acc_ref[...] = jnp.zeros_like(acc_ref)
    for fetch in fetches:
        fetch.wait()

    def wide(x):
        return jnp.broadcast_to(x.astype(jnp.bfloat16), (256, chunk))

    def body(step, carry):
        at = pl.ds(pl.multiple_of(step * chunk, chunk), chunk)
        slot = lax.broadcasted_iota(jnp.int32, (1, chunk), 1) + step * chunk
        value = jnp.where(slot < count_ref[0, 0], area[:, at] * speed[:, at], 0.0)
        node = nodes[:, at]
        low = (((node & 1) << 7) + ((node >> 3) & 127)).astype(jnp.float32)
        high = (((node >> 1) & 3) * 64 + (node >> 10)).astype(jnp.float32)
        first = value.astype(jnp.bfloat16)
        second = value - first.astype(jnp.float32)
        here = wide(high) == ids
        upper = jnp.where(here, wide(first), zero)
        lower = jnp.where(here, wide(second), zero)
        columns = jnp.where(wide(low) == ids, one, zero)
        both = jnp.concatenate([upper, lower], axis=0)
        acc_ref[...] += lax.dot_general(both, columns, contract, preferred_element_type=jnp.float32)
        return carry

    lax.fori_loop(0, slots // chunk, body, 0)
    for j in range(8):
        at, lanes = 64 * (j // 2), slice(LANES * (j % 2), LANES * (j % 2 + 1))
        near, far = at + 32 * core, at + 32 - 32 * core
        keep_ref[j] = acc_ref[pl.ds(near, 32), lanes] + acc_ref[pl.ds(256 + near, 32), lanes]
        send_ref[j] = acc_ref[pl.ds(far, 32), lanes] + acc_ref[pl.ds(256 + far, 32), lanes]


def face_sums(where, count, area, speed, node):
    half = f32(8, 32, LANES)
    return pl.pallas_call(
        face_kernel,
        out_shape=(half, half),
        in_specs=[SMEM, SMEM] + [HBM] * 3,
        out_specs=(VMEM, VMEM),
        scratch_shapes=[
            pltpu.VMEM(area.shape, jnp.float32),
            pltpu.VMEM(area.shape, jnp.float32),
            pltpu.VMEM(area.shape, jnp.int32),
            pltpu.VMEM((512, 256), jnp.float32),
            pltpu.SemaphoreType.DMA((3,)),
        ],
        compiler_params=params(32),
        cost_estimate=cost(7),
        name="face_sums",
    )(where, count, area, speed, node)


def cut_kernel(block_ref, metric_ref, up_ref, down_ref, sems):
    layers, rows, _ = block_ref.shape
    copies = []
    for out_ref, row, root_row in ((up_ref, rows - DEEP, rows - HALO), (down_ref, 0, 0)):
        for z in range(layers):
            part = block_ref.at[z, pl.ds(row, DEEP), :]
            copies.append((part, out_ref.at[pl.ds(DEEP * z, DEEP), :]))
        part = metric_ref.at[pl.ds(root_row, HALO), :]
        copies.append((part, out_ref.at[pl.ds(DEEP * layers, HALO), :]))
    copies = [pltpu.make_async_copy(*pair, sems.at[i]) for i, pair in enumerate(copies)]
    for copy in copies:
        copy.start()
    for copy in copies:
        copy.wait()


def outgoing_rows(block, metric):
    layers, _, cols = block.shape
    rows = f32(DEEP * layers + HALO, cols)
    return pl.pallas_call(
        cut_kernel,
        out_shape=(rows, rows),
        in_specs=[HBM, HBM],
        out_specs=(VMEM, VMEM),
        scratch_shapes=[pltpu.SemaphoreType.DMA((2 * layers + 2,))],
        compiler_params=params(56),
        cost_estimate=cost(1),
        name="outgoing_rows",
    )(block, metric)


def basis_kernel(
    where_ref, own_ref, other_ref, same_ref, cross_ref, root_ref,
    field, sums_ref, rows, root, outer, line, partial,
):
    core = where_ref[0, 0]
    centre = (BASIS_LOW + BASIS_HIGH) / 2
    scale = 2 / (BASIS_HIGH - BASIS_LOW)
    for t in range(8):
        rows[t, pl.ds(32 + 32 * core, 32), :] = own_ref[t]
        rows[t, pl.ds(64 - 32 * core, 32), :] = other_ref[t]
        rows[t, pl.ds(96 * core, 32), :] = cross_ref[t]
        rows[t, pl.ds(96 - 96 * core, 32), :] = same_ref[t]
    for t in range(8):
        for ys in range(GROUPS):
            field[0, t, ys] = rows[t, pl.ds(ys, SUB, stride=GROUPS), :]
            value = root_ref[t, pl.ds(ys, SUB, stride=GROUPS), :]
            root[t, ys] = value * (stored(t % 2) * stored(ys % 2))
            outer[t, ys] = value * (2 * scale * 4.0 / 225.0 / (given(t % 2) * given(ys % 2)))

    group = lax.broadcasted_iota(jnp.int32, (SUB, LANES), 0)
    own_rows = jnp.where((group >= 2) & (group < 6), 1.0, 0.0).astype(jnp.float32)

    def step(k, begin, end):
        def put(k, t, ys, value):
            if not end:
                field[k, t, ys] = value

        for ys in range(GROUPS):
            padded = column_ring([field[k, t, ys] * root[t, ys] for t in range(8)])
            for t in range(8):
                line[ys, t] = mass_line(padded, t)
        squares, shifts = [], []
        for t in range(8):
            square = jnp.zeros((SUB, LANES), jnp.float32)
            shifted = jnp.zeros((SUB, LANES), jnp.float32)
            padded = row_ring([line[ys, t] for ys in range(GROUPS)])
            for ys in range(GROUPS):
                now = field[k, t, ys]
                later = outer[t, ys] * mass_line(padded, ys) - (2 * centre * scale) * now
                later = 0.5 * later if begin else later - field[k - 1, t, ys]
                put(k + 1, t, ys, later)
                square = square + now * now
                shifted = shifted + later * now
            squares.append(square)
            shifts.append(shifted)

        def add(parts):
            while len(parts) > 1:
                parts = [parts[i] + parts[i + 1] for i in range(0, len(parts), 2)]
            return jnp.sum(parts[0] * own_rows, axis=0, keepdims=True)

        partial[pl.ds(2 * k, 1), :] = add(squares)
        partial[pl.ds(2 * k + 1, 1), :] = add(shifts)

    def later_step(k, carry):
        step(k, False, False)
        return carry

    partial[...] = jnp.zeros_like(partial)
    step(0, True, False)
    lax.fori_loop(1, ITERS - 1, later_step, 0)
    step(ITERS - 1, False, True)
    whole = jnp.sum(partial[...], axis=1, keepdims=True)
    row = lax.broadcasted_iota(jnp.int32, partial.shape, 0)
    lane = lax.broadcasted_iota(jnp.int32, partial.shape, 1)
    line_of = jnp.sum(jnp.where(row == lane, whole, 0.0), axis=0, keepdims=True)
    sums_ref[...] = jnp.broadcast_to(line_of[None], sums_ref.shape)


def surface_basis(where, vols, own, other, same, cross, root):
    return pl.pallas_call(
        basis_kernel,
        out_shape=(f32(ITERS, 8, GROUPS, SUB, LANES), f32(vols, SUB, LANES)),
        in_specs=[SMEM] + [VMEM] * 5,
        out_specs=(VMEM, VMEM),
        scratch_shapes=[
            pltpu.VMEM((8, ROWS, LANES), jnp.float32),
            pltpu.VMEM((8, GROUPS, SUB, LANES), jnp.float32),
            pltpu.VMEM((8, GROUPS, SUB, LANES), jnp.float32),
            pltpu.VMEM((GROUPS, 8, SUB, LANES), jnp.float32),
            pltpu.VMEM((24, LANES), jnp.float32),
        ],
        compiler_params=params(24),
        cost_estimate=cost(7),
        name="surface_basis",
    )(where, own, other, same, cross, root)


def solve_weights():
    n = ITERS
    moment = np.zeros((2 * n, 2 * n))
    for m in range(2 * n):
        if m < 2:
            moment[m, m] = 1.0
        else:
            moment[m, m] = 2.0
            moment[m, m % 2] = -1.0
    centre, half = (BASIS_LOW + BASIS_HIGH) / 2, (BASIS_HIGH - BASIS_LOW) / 2
    weights = np.zeros((2 * n, 16, LANES))
    for i in range(n):
        for j in range(n):
            lower = abs(j - 1)
            for factor, index in (
                (centre / 2, i + j),
                (centre / 2, abs(i - j)),
                (half / 4, i + j + 1),
                (half / 4, abs(i - j - 1)),
                (half / 4, i + lower),
                (half / 4, abs(i - lower)),
            ):
                weights[:, i, j] += factor * moment[index]
        weights[:, i, n] += moment[i]
    return weights.astype(np.float32)


def solve_kernel(part_ref, sums_ref, weights_ref, out_ref, flag_ref, rows):
    n = ITERS
    total = sums_ref[0]
    for i in range(1, sums_ref.shape[0]):
        total = total + sums_ref[i]
    row = lax.broadcasted_iota(jnp.int32, (16, LANES), 0)
    lane = lax.broadcasted_iota(jnp.int32, (16, LANES), 1)
    system = jnp.where((lane == row + 16) & (row < n), 1.0, 0.0).astype(jnp.float32)
    for m in range(2 * n):
        system = system + weights_ref[m] * total[0:1, m : m + 1]
    centre = jnp.sum(jnp.where(lane == row, system, 0.0), axis=1, keepdims=True)
    for k in range(n):
        pivot_row = system[k : k + 1, :] / system[k : k + 1, k : k + 1]
        column = system[:, k : k + 1]
        system = jnp.where(row == k, pivot_row, system - column * pivot_row)
    inverse = jnp.sum(jnp.where(lane == row + 16, system, 0.0), axis=1, keepdims=True)
    figure = jnp.broadcast_to(centre * inverse, (16, LANES))
    inside = (row < n) & (lane == 0)
    least = jnp.min(jnp.where(inside, figure, 1.0))
    whole = jnp.sum(jnp.where(inside, figure, 0.0))
    flag_ref[0, 0] = jnp.where((least > 0.5) & (whole < CONDITION_MAX), 1, 0).astype(jnp.int32)
    weights = [jnp.broadcast_to(system[k : k + 1, n : n + 1], (SUB, LANES)) for k in range(n)]
    for t in range(8):
        for ys in range(GROUPS):
            value = weights[0] * part_ref[0, t, ys]
            for k in range(1, n):
                value = value + weights[k] * part_ref[k, t, ys]
            rows[t, pl.ds(ys, SUB, stride=GROUPS), :] = value
        out_ref[t] = rows[t, HALO - DEEP : HALO - DEEP + Y_ROWS, :]


def surface_solve(basis, sums):
    return pl.pallas_call(
        solve_kernel,
        out_shape=(f32(8, Y_ROWS, LANES), jax.ShapeDtypeStruct((1, 1), jnp.int32)),
        in_specs=[VMEM, VMEM, VMEM],
        out_specs=(VMEM, SMEM),
        scratch_shapes=[pltpu.VMEM((8, ROWS, LANES), jnp.float32)],
        compiler_params=params(24),
        cost_estimate=cost(3),
        name="surface_solve",
    )(basis, sums, jnp.asarray(solve_weights()))


def fill_factors(where_ref, factor):
    vol, vols, rows = where_ref[0, 3], where_ref[0, 4], where_ref[0, 5]
    group = lax.broadcasted_iota(jnp.int32, (SUB, LANES), 0)
    mass, stiff = (8.0, 16.0), (14.0, 16.0)
    for ys in range(Y_GROUPS):
        row = group * Y_GROUPS + ys
        outside = ((vol == 0) & (row < DEEP)) | ((vol == vols - 1) & (row >= DEEP + rows))
        py = ys % 2
        for pz in range(2):
            for px in range(2):
                value = -12.0 / (
                    stiff[pz] * mass[py] * mass[px]
                    + mass[pz] * (stiff[py] * mass[px] + mass[py] * stiff[px])
                )
                for p in (pz, py, px):
                    value = value * stored(p) / given(p)
                factor[pz, px, ys] = jnp.where(outside, 0.0, jnp.float32(value))


def lateral_lines(get, line_a, line_b, put):
    for t in range(8):
        u = row_ring([get(t, ys) for ys in range(Y_GROUPS)])
        for ys in range(Y_GROUPS):
            m = mass_line(u, ys)
            line_a[t, ys] = m
            line_b[t, ys] = both_line(u, ys) - m
    for ys in range(Y_GROUPS):
        a = column_ring([line_a[t, ys] for t in range(8)])
        b = column_ring([line_b[t, ys] for t in range(8)])
        for t in range(8):
            put(t, ys, mass_line(a, t), both_line(a, t) + mass_line(b, t))


def even_step(w, c):
    near = c[1] + c[3]
    return (22.0 / 3.0 * w[1] - (w[0] + w[2])) + ((near + 8.0 * c[2]) - (c[0] + c[4]))


def odd_step(w, c):
    return (8.0 / 3.0 * w[1] - (w[0] + w[2])) + ((c[0] + c[2]) + 4.0 * c[1])


def strided(ys):
    return pl.ds(ys, SUB, stride=Y_GROUPS)


def change_kernel(
    where_ref, speed_ref, out_ref, cells, along, cross, line_a, line_b, factor, plain, sems,
):
    col = where_ref[0, 1]
    layers, _, rows, _ = out_ref.shape

    def lateral(z, carry):
        def put(t, ys, w, c):
            along[z, t, ys] = w
            cross[z, t, ys] = c

        lateral_lines(lambda t, ys: cells[z, t, ys], line_a, line_b, put)
        return carry

    def set_top():
        for t in range(8):
            for ys in range(Y_GROUPS):
                scale = 0.5 * stored(0) * stored(t % 2) * stored(ys % 2)
                cells[2, t, ys] = scale * speed_ref[t, strided(ys), :]

    def send(first, count):
        copies = []
        for z in range(first, first + count):
            for t in range(8):
                for ys in range(Y_GROUPS):
                    plain[z, t, strided(ys), :] = cells[z + 2, t, ys]
            copy = pltpu.make_async_copy(
                plain.at[z, :, pl.ds(DEEP, rows), :], out_ref.at[z], sems.at[z]
            )
            copy.start()
            copies.append(copy)
        for copy in copies:
            copy.wait()

    @pl.when(col == 0)
    def _():
        fill_factors(where_ref, factor)
        set_top()
        clear = jnp.zeros((8, Y_GROUPS, SUB, LANES), jnp.float32)
        for z in range(2):
            cross[z] = clear
            along[z] = clear

        def update(pair, carry):
            z = 2 * pair + 2
            for ys in range(Y_GROUPS):
                factors = [[factor[pz, px, ys] for px in range(2)] for pz in range(2)]
                for t in range(8):
                    w = [along[z + i, t, ys] for i in range(-1, 3)]
                    c = [cross[z + i, t, ys] for i in range(-2, 3)]
                    cells[z, t, ys] += factors[0][t % 2] * even_step(w, c)
                    cells[z + 1, t, ys] += factors[1][t % 2] * odd_step(w[1:], c[2:])
            return carry

        def one_sweep(sweep, carry):
            front = 2 * sweep + 2
            lax.fori_loop(2, front + 1, lateral, 0)
            lax.fori_loop(0, sweep, update, 0)
            for ys in range(Y_GROUPS):
                factors = [[factor[pz, px, ys] for px in range(2)] for pz in range(2)]
                for t in range(8):
                    w0, w1 = along[front - 1, t, ys], along[front, t, ys]
                    c0, c1, c2 = [cross[front + i, t, ys] for i in range(-2, 1)]
                    step = (22.0 / 3.0 * w1 - w0) + ((c1 + 8.0 * c2) - c0)
                    cells[front, t, ys] += factors[0][t % 2] * step
                    cells[front + 1, t, ys] = factors[1][t % 2] * (c2 - w1)
                    cells[front + 2, t, ys] = -factors[0][t % 2] * c2
            set_top()
            return carry

        lax.fori_loop(0, SWEEPS, one_sweep, 0)
        send(1, layers - 1)

    @pl.when(col == 1)
    def _():
        fill_factors(where_ref, factor)
        set_top()

        def one_sweep(sweep, carry):
            lateral(2, 0)
            for t in range(8):
                for ys in range(Y_GROUPS):
                    cells[2, t, ys] = -factor[0, t % 2, ys] * cross[2, t, ys]
            return carry

        lax.fori_loop(0, SWEEPS, one_sweep, 0)
        send(0, 1)


def surface_change(where, speed, layers, rows):
    work = pltpu.VMEM((layers + 2, 8, Y_GROUPS, SUB, LANES), jnp.float32)
    line = pltpu.VMEM((8, Y_GROUPS, SUB, LANES), jnp.float32)
    return pl.pallas_call(
        change_kernel,
        out_shape=f32(layers, 8, rows, LANES),
        in_specs=[SMEM, VMEM],
        out_specs=HBM,
        scratch_shapes=[
            pltpu.VMEM((layers + 3, 8, Y_GROUPS, SUB, LANES), jnp.float32),
            work, work, line, line,
            pltpu.VMEM((2, 2, Y_GROUPS, SUB, LANES), jnp.float32),
            pltpu.VMEM((layers, 8, Y_ROWS, LANES), jnp.float32),
            pltpu.SemaphoreType.DMA((layers,)),
        ],
        compiler_params=params(32),
        cost_estimate=cost(8),
        name="surface_change",
    )(where, speed)


def base_kernel(
    where_ref, wide_ref, zlow_ref, zhigh_ref, change_ref, speed_ref, select_hbm_ref,
    velocity_ref, out_ref, field, along, cross, line_a, line_b, factor, change, select, parts, sems,
):
    col, cols = where_ref[0, 1], where_ref[0, 2]
    layers, _, rows, _ = change_ref.shape
    total = layers + 2 * DEEP
    arrivals = []
    for i in range(total):
        z = (i + DEEP) % total
        source = wide_ref if i < layers else zhigh_ref if i < layers + DEEP else zlow_ref
        arrivals.append(pltpu.make_async_copy(source.at[i % DEEP], field.at[z], sems.at[z]))
    for arrival in arrivals:
        arrival.start()
    choose = pltpu.make_async_copy(select_hbm_ref, select, sems.at[total + 2])
    choose.start()
    all_change = pltpu.make_async_copy(
        change_ref.at[pl.ds(1, layers - 1)], change.at[pl.ds(1, layers - 1)], sems.at[total]
    )
    one_change = pltpu.make_async_copy(
        change_ref.at[pl.ds(0, 1)], change.at[pl.ds(0, 1)], sems.at[total + 1]
    )
    pl.when(col == 0)(all_change.start)
    pl.when(col == 1)(one_change.start)
    fill_factors(where_ref, factor)
    count = (layers + 1) * rows

    def cut(value, at, t):
        first, second = split(value)
        lanes = slice(LANES * t, LANES * (t + 1))
        parts[at : at + rows, lanes] = first
        parts[count + at : count + at + rows, lanes] = second

    for t in range(8):
        cut(speed_ref[t, DEEP : DEEP + rows, :], 0, t)

    def lateral(z, carry):
        def put(t, ys, w, c):
            along[z, t, ys] = w
            cross[z, t, ys] = c

        lateral_lines(lambda t, ys: field[z, t, strided(ys), :], line_a, line_b, put)
        return carry

    def update(pair, carry):
        z = 2 * pair
        for ys in range(Y_GROUPS):
            factors = [[factor[pz, px, ys] for px in range(2)] for pz in range(2)]
            for t in range(8):
                w = [along[z + i, t, ys] for i in range(-1, 3)]
                c = [cross[z + i, t, ys] for i in range(-2, 3)]
                even, odd = even_step(w, c), odd_step(w[1:], c[2:])
                scale = jnp.where((col == 0) & (z == DEEP), 0.0, factors[0][t % 2])
                even = field[z, t, strided(ys), :] + scale * even
                odd = field[z + 1, t, strided(ys), :] + factors[1][t % 2] * odd
                field[z, t, strided(ys), :] = even
                field[z + 1, t, strided(ys), :] = odd
        return carry

    def update_all(sweep):
        low_pair = jnp.where(col == 0, DEEP // 2, sweep + 1)
        high_pair = jnp.where(col == cols - 1, (DEEP + layers) // 2, total // 2 - sweep - 1)
        lax.fori_loop(low_pair, high_pair, update, 0)

    begin = jnp.where(col == 0, DEEP, 0)
    end = jnp.where(col == cols - 1, DEEP + layers + 1, total - 1)

    def first_lateral(i, carry):
        z = lax.rem(i + DEEP, total)
        pltpu.make_async_copy(wide_ref.at[0], field.at[z], sems.at[z]).wait()

        @pl.when((z >= begin) & (z < end))
        def _():
            lateral(z, 0)

        return carry

    def later_sweep(sweep, carry):
        lax.fori_loop(
            jnp.maximum(begin, 2 * sweep), jnp.minimum(end, total - 2 * sweep - 1), lateral, 0
        )
        update_all(sweep)
        return carry

    @pl.when(col == 0)
    def _():
        clear = jnp.zeros((8, Y_GROUPS, SUB, LANES), jnp.float32)
        for z in (DEEP - 2, DEEP - 1):
            along[z] = clear
            cross[z] = clear

    lax.fori_loop(0, total, first_lateral, 0)
    update_all(0)
    lax.fori_loop(1, SWEEPS, later_sweep, 0)

    row = lax.broadcasted_iota(jnp.int32, (rows, LANES), 0)
    by_row = jnp.where(row % 2 == 0, stored(0), stored(1)).astype(jnp.float32)
    back_row = jnp.where(row % 2 == 0, 1 / stored(0), 1 / stored(1)).astype(jnp.float32)

    @pl.when(col == 0)
    def _():
        all_change.wait()
        for t in range(8):
            top = speed_ref[t, DEEP : DEEP + rows, :] * (by_row * (0.5 * stored(0) * stored(t % 2)))
            field[DEEP, t, DEEP : DEEP + rows, :] += top
            for z in range(1, layers):
                field[DEEP + z, t, DEEP : DEEP + rows, :] += change[z, t]

    @pl.when(col == 1)
    def _():
        one_change.wait()
        for t in range(8):
            field[DEEP, t, DEEP : DEEP + rows, :] += change[0, t]

    for z in range(layers):
        for t in range(8):
            value = field[DEEP + z, t, DEEP : DEEP + rows, :]
            cut(value * (back_row * (1 / (stored(z % 2) * stored(t % 2)))), rows * (z + 1), t)

    def write(at, value):
        velocity_ref[:, at] = value[:rows]
        out_ref[:, :, at] = value[rows:].reshape(layers, rows, 256)

    choose.wait()
    plain_columns(select, parts[...], count, write)


def base_sweeps(where, wide, zlow, zhigh, change, speed, select):
    layers, _, rows, _ = change.shape
    total = layers + 2 * DEEP
    work = pltpu.VMEM((total, 8, Y_GROUPS, SUB, LANES), jnp.float32)
    line = pltpu.VMEM((8, Y_GROUPS, SUB, LANES), jnp.float32)
    return pl.pallas_call(
        base_kernel,
        out_shape=(f32(rows, 8 * LANES), f32(layers, rows, 8 * LANES)),
        in_specs=[SMEM] + [HBM] * 4 + [VMEM, HBM],
        out_specs=(VMEM, VMEM),
        scratch_shapes=[
            pltpu.VMEM((total, 8, Y_ROWS, LANES), jnp.float32),
            work, work, line, line,
            pltpu.VMEM((2, 2, Y_GROUPS, SUB, LANES), jnp.float32),
            pltpu.VMEM((layers, 8, rows, LANES), jnp.float32),
            pltpu.VMEM(select.shape, jnp.bfloat16),
            pltpu.VMEM((2 * (layers + 1) * rows, 8 * LANES), jnp.bfloat16),
            pltpu.SemaphoreType.DMA((total + 3,)),
        ],
        compiler_params=params(50),
        cost_estimate=cost(25),
        name="base_sweeps",
    )(where, wide, zlow, zhigh, change, speed, select)


mass_even = (-1.0 / 15.0, 2.0 / 15.0, 8.0 / 15.0, 2.0 / 15.0, -1.0 / 15.0)
mass_odd = (0.0, 2.0 / 15.0, 16.0 / 15.0, 2.0 / 15.0, 0.0)


def mass_along(padded, axis):
    count = padded.shape[axis] - 4
    pieces = [lax.slice_in_dim(padded, i, i + count, axis=axis) for i in range(5)]
    even = sum(mass_even[i] * pieces[i] for i in range(5))
    odd = sum(mass_odd[i] * pieces[i] for i in range(1, 4))
    at_even = lax.broadcasted_iota(jnp.int32, even.shape, axis) % 2 == 0
    return jnp.where(at_even, even, odd)


def with_rows(x, width):
    size = lax.axis_size("vol")
    up = [(i, i + 1) for i in range(size - 1)]
    down = [(j, i) for i, j in up]
    before = lax.ppermute(x[-width:], "vol", up)
    after = lax.ppermute(x[:width], "vol", down)
    return jnp.concatenate([before, x, after], axis=0)


def stepwise(flux, metric):
    root = jnp.sqrt(metric)

    def dot(a, b):
        return lax.psum(jnp.sum(a * b), "vol")

    def step(_, state):
        solved, residual, direction, norm = state
        padded = jnp.pad(with_rows(root * direction, 2), ((0, 0), (2, 2)))
        image = root * mass_along(mass_along(padded, 1), 0)
        alpha = norm / dot(direction, image)
        solved = solved + alpha * direction
        residual = residual - alpha * image
        after = dot(residual, residual)
        direction = residual + after / norm * direction
        return solved, residual, direction, after

    state = (jnp.zeros_like(flux), flux, flux, dot(flux, flux))
    return with_rows(lax.fori_loop(0, ITERS, step, state)[0], DEEP)


def after(x, *others):
    return lax.optimization_barrier((x,) + others)[0]


def on_device(face_area, face_speed, face_node, face_count, surface_metric, displacement):
    vols, cols = lax.axis_size("vol"), lax.axis_size("col")
    vol, col = lax.axis_index("vol"), lax.axis_index("col")
    core = col % 2
    where = [core, col, jnp.int32(cols), vol, jnp.int32(vols), jnp.int32(displacement.shape[1])]
    where = jnp.stack(where).astype(jnp.int32).reshape(1, 6)
    up = [(i, i + 1) for i in range(vols - 1)]
    down = [(j, i) for i, j in up]
    col_up = [(i, i + 1) for i in range(cols - 1)]
    col_down = [(j, i) for i, j in col_up]
    packed = displacement.shape[0] * DEEP

    select = plain_selection()

    def moved(x, steps):
        dv, dc = steps
        pairs = [
            (i * cols + j, (i + dv) * cols + j + dc)
            for i in range(vols)
            for j in range(cols)
            if 0 <= i + dv < vols and 0 <= j + dc < cols
        ]
        return lax.ppermute(x, ("vol", "col"), pairs)

    rows_up, rows_down = outgoing_rows(displacement, surface_metric)
    keep, send = face_sums(where, face_count, after(face_area, rows_up), face_speed, face_node)
    with jax.named_scope("flux_sum"):
        keep = keep + lax.ppermute(send, "col", [(j, j ^ 1) for j in range(cols)])
        turned = [
            lax.ppermute(keep, "col", [(j, (j + 2 * k) % cols) for j in range(cols)]) for k in (1, 2, 3)
        ]
    with jax.named_scope("row_halo"):
        rows_before, rows_after = moved(rows_up, (1, 0)), moved(rows_down, (-1, 0))
    wide, root = regroup(displacement, surface_metric, rows_before, rows_after)
    with jax.named_scope("flux_sum"):
        turned = lax.optimization_barrier((*turned, wide))
        own = (keep + turned[1]) + (turned[0] + turned[2])
    with jax.named_scope("flux_halo"):
        other = lax.ppermute(own, "col", [(j, j ^ 1) for j in range(cols)])
        pairs = []
        for i in range(vols):
            for j in range(cols):
                to = i - 1 if j % 2 == 0 else i + 1
                if 0 <= to < vols:
                    pairs.append((i * cols + j, to * cols + j))
        same = lax.ppermute(own, ("vol", "col"), pairs)
        cross = lax.ppermute(same, "col", [(j, j ^ 1) for j in range(cols)])

    with jax.named_scope("depth_halo"):
        sent = after(wide, own)
        zlow, zhigh = moved(sent, (0, 1)), moved(sent, (0, -1))
    basis, spread = surface_basis(where, vols, own, other, same, cross, root)
    with jax.named_scope("gather_sums"):
        gathered = lax.all_to_all(spread, "vol", 0, 0)
    speed, flag = surface_solve(basis, gathered)

    def finish(speed):
        change = surface_change(where, speed, displacement.shape[0], displacement.shape[1])
        return base_sweeps(where, wide, zlow, zhigh, change, speed, select)

    def step_by_step():
        low = jnp.where(core == 0, own, other)
        high = jnp.where(core == 0, other, own)
        flux = jnp.concatenate([low, high], axis=1)
        flux = flux.transpose(1, 2, 0).reshape(surface_metric.shape)
        solved = stepwise(flux, surface_metric)
        return finish(solved.reshape(Y_ROWS, LANES, 8).transpose(2, 0, 1))

    return lax.cond(flag[0, 0] > 0, lambda: finish(speed), step_by_step)


def solution(mesh):
    in_specs = (
        P("vol", "col"),
        P("vol", "col"),
        P("vol", "col"),
        P("vol", "col"),
        P("vol", None),
        P("col", "vol", None),
    )
    out_specs = (P("vol", None), P("col", "vol", None))
    return jax.shard_map(
        on_device, mesh=mesh, in_specs=in_specs, out_specs=out_specs, check_vma=False
    )
```
